32 devices in a mesh: dp: 8 (over z, y), tensor: 4 (over x, core).
Axes of the slice: x: 2, y: 2, z: 4, core: 2. Of those that a mesh axis runs over, the one named last changes fastest.
Arguments:
- block_input: bfloat16 [4096, 1024], P('dp'), may hold values from -6 to 6
- lengths: int32 [8], P('dp'), may hold values from 16 to 512, as said below
- norm_params: float32 [8, 1024], replicated
- qkv_weight: float32 [1024, 3, 1024], P(None, None, 'tensor')
- out_weight: float32 [1024, 1024], P('tensor')
- up_weight: float32 [1024, 4096], P(None, 'tensor')
- down_weight: float32 [4096, 1024], P('tensor')
- qkv_first: float32 [1024, 3, 1024], P('dp', None, 'tensor'), may hold values from -40 to 40
- qkv_second: float32 [1024, 3, 1024], P('dp', None, 'tensor')
- out_first: float32 [1024, 1024], P('tensor', 'dp'), may hold values from -40 to 40
- out_second: float32 [1024, 1024], P('tensor', 'dp')
- up_first: float32 [1024, 4096], P('dp', 'tensor'), may hold values from -20 to 20
- up_second: float32 [1024, 4096], P('dp', 'tensor')
- down_first: float32 [4096, 1024], P('tensor', 'dp'), may hold values from -40 to 40
- down_second: float32 [4096, 1024], P('tensor', 'dp')
- norm_first: float32 [8, 1024], P(None, 'dp'), may hold values from -40 to 40
- norm_second: float32 [8, 1024], P(None, 'dp')
- out_grad: bfloat16 [4096, 1024], P('dp'), may hold values from -6 to 6
Outputs:
- block_output: bfloat16 [4096, 1024], P('dp')
- input_grad: bfloat16 [4096, 1024], P('dp')
- qkv_new: float32 [1024, 3, 1024], P('dp', None, 'tensor')
- qkv_first_new: float32 [1024, 3, 1024], P('dp', None, 'tensor')
- qkv_second_new: float32 [1024, 3, 1024], P('dp', None, 'tensor')
- out_new: float32 [1024, 1024], P('tensor', 'dp')
- out_first_new: float32 [1024, 1024], P('tensor', 'dp')
- out_second_new: float32 [1024, 1024], P('tensor', 'dp')
- up_new: float32 [1024, 4096], P('dp', 'tensor')
- up_first_new: float32 [1024, 4096], P('dp', 'tensor')
- up_second_new: float32 [1024, 4096], P('dp', 'tensor')
- down_new: float32 [4096, 1024], P('tensor', 'dp')
- down_first_new: float32 [4096, 1024], P('tensor', 'dp')
- down_second_new: float32 [4096, 1024], P('tensor', 'dp')
- norm_new: float32 [8, 1024], P(None, 'dp')
- norm_first_new: float32 [8, 1024], P(None, 'dp')
- norm_second_new: float32 [8, 1024], P(None, 'dp')
- matrix_norms: float32 [2, 4], replicated
The draws below stay inside these ranges and needn't reach their ends.
Inputs may be any that keep to these rules, and one draw needn't show every extreme that they name: `lengths`: each slot holds one sequence of that many live tokens at its head, the rest padding; some sequence fills its slot.
All inputs are finite; a program needn't handle non-finite values.
Results may differ from the reference program's by a relative error of at most 0.014.
The reference program's roundings to bfloat16 on the way count: a program that leaves them out, or rounds other values in their place, can miss the bound.
Values sent between devices are 32-bit elements; how exact they have to be, the bound alone decides.
No kernel may reach another device: no remote copies, remote signals or barrier semaphores. Data moves between devices by JAX's collectives and lax.ppermute only.
A program may use at most 128 MiB of HBM per device.

```python
import jax
import jax.numpy as jnp
from jax import lax

D = 1024
HEADS = 16
HEAD_DIM = 64
FF = 4096
SEQ_LEN = 512
STEP = 10
HEAD_WIDTH = 1024
SEQS = 8
TOKENS = 4096
MIN_LEN = 16


def ramp_factors(key, row_count, col_count):
    row_key, col_key = jax.random.split(key)
    row_part = (0.6 + 0.8 * jnp.arange(row_count, dtype=jnp.float32) / row_count) * jnp.exp(jax.random.uniform(row_key, (row_count,), jnp.float32, -0.3, 0.3))
    col_part = (0.6 + 0.8 * jnp.arange(col_count, dtype=jnp.float32) / col_count) * jnp.exp(jax.random.uniform(col_key, (col_count,), jnp.float32, -0.3, 0.3))
    return (row_part, col_part)


def shaped_weight(base, key, fan_in):
    row_part, col_part = ramp_factors(key, base.shape[0], base.shape[-1])
    extra = (1,) * (base.ndim - 2)
    return base * fan_in ** (-0.5) * row_part.reshape((base.shape[0],) + extra + (1,)) * col_part


def second_moment(key, shape, scale):
    row_count = shape[0]
    col_count = shape[-1]
    extra = (1,) * (len(shape) - 2)
    row_ramp = (jnp.arange(row_count, dtype=jnp.float32) / row_count).reshape((row_count,) + extra + (1,))
    col_ramp = jnp.arange(col_count, dtype=jnp.float32) / col_count
    spread = jnp.exp(jax.random.uniform(key, shape, jnp.float32, 0.0, 0.69))
    return 0.001 * scale * (1.0 + 0.5 * row_ramp + 0.5 * col_ramp) * spread


def draw_lengths(key, part):
    key = jax.random.fold_in(key, 21)
    length_key, pick_key = jax.random.split(key)
    drawn = jax.random.randint(length_key, (SEQS,), MIN_LEN, SEQ_LEN + 1)
    picked = jax.random.randint(pick_key, (), 0, SEQS)
    return jnp.where(jnp.arange(SEQS) == picked, SEQ_LEN, drawn).astype(jnp.int32)


def draw_norm_params(key, part):
    key = jax.random.fold_in(key, 11)
    gain_key, offset_key = jax.random.split(key)
    gains = jax.random.uniform(gain_key, (4, D), jnp.float32, 0.6, 1.4)
    offsets = 0.3 * jax.random.normal(offset_key, (4, D), jnp.float32)
    return jnp.stack([gains, offsets], axis=1).reshape(8, D)


def draw_qkv_weight(key, part):
    key = jax.random.fold_in(key, 1)
    base_key, side_key = jax.random.split(key)
    shape = (D, 3, HEADS * HEAD_DIM)
    base = jax.random.normal(base_key, shape, jnp.float32)
    return shaped_weight(base, side_key, D)


def draw_out_weight(key, part):
    key = jax.random.fold_in(key, 2)
    base_key, side_key = jax.random.split(key)
    shape = (HEADS * HEAD_DIM, D)
    base = jax.random.normal(base_key, shape, jnp.float32)
    return shaped_weight(base, side_key, HEADS * HEAD_DIM)


def draw_up_weight(key, part):
    key = jax.random.fold_in(key, 3)
    base_key, side_key = jax.random.split(key)
    shape = (D, FF)
    base = jax.random.normal(base_key, shape, jnp.float32)
    return shaped_weight(base, side_key, D)


def draw_down_weight(key, part):
    key = jax.random.fold_in(key, 4)
    base_key, side_key = jax.random.split(key)
    shape = (FF, D)
    base = jax.random.normal(base_key, shape, jnp.float32)
    return shaped_weight(base, side_key, FF)


def draw_qkv_second(key, part):
    key = jax.random.fold_in(key, 31)
    return second_moment(key, (D, 3, HEADS * HEAD_DIM), 1.0 * TOKENS)


def draw_out_second(key, part):
    key = jax.random.fold_in(key, 32)
    return second_moment(key, (HEADS * HEAD_DIM, D), 1.0 * TOKENS)


def draw_up_second(key, part):
    key = jax.random.fold_in(key, 33)
    return second_moment(key, (D, FF), 0.25 * TOKENS)


def draw_down_second(key, part):
    key = jax.random.fold_in(key, 34)
    return second_moment(key, (FF, D), 1.0 * TOKENS)


def draw_norm_second(key, part):
    key = jax.random.fold_in(key, 35)
    return second_moment(key, (8, D), 1.0 * TOKENS)


def level_of(rng, dims, shards, low, largest):
    level, own = 1.0, jax.random.fold_in(rng, 6)
    for dim, shards_of in shards:
        draws = jnp.exp(jax.random.uniform(jax.random.fold_in(own, dim), (shards_of,), jnp.float32, low / len(shards), largest / len(shards)))
        level = level * jnp.repeat(draws, dims[dim] // shards_of).reshape([-1 if axis == dim else 1 for axis in range(len(dims))])
    return level


def bell_draw(rng, shape, scale, most, cuts=(), kind=jnp.bfloat16):
    factor_of = level_of(rng, shape, cuts, -0.22, 0.18) if cuts else 1.0
    array = jax.random.normal(rng, shape, jnp.float32) * scale * factor_of
    return jnp.minimum(jnp.maximum(array, -most), most).astype(kind)


def setup_inputs(seed: int = 0) -> dict:
    streams_of = jax.random.split(jax.random.key(seed), 19)
    block_input = bell_draw(streams_of[0], (TOKENS, D), 1.0, 6.0, ((0, 8),))
    lengths = draw_lengths(jax.random.fold_in(streams_of[18], 71), 0)
    norm_params = draw_norm_params(jax.random.fold_in(streams_of[18], 71), 0)
    qkv_weight = draw_qkv_weight(jax.random.fold_in(streams_of[18], 71), 0)
    out_weight = draw_out_weight(jax.random.fold_in(streams_of[18], 71), 0)
    up_weight = draw_up_weight(jax.random.fold_in(streams_of[18], 71), 0)
    down_weight = draw_down_weight(jax.random.fold_in(streams_of[18], 71), 0)
    qkv_first = bell_draw(streams_of[7], (D, 3, HEAD_WIDTH), (0.111 * TOKENS ** 0.5), 40.0, ((0, 8), (2, 4)), jnp.float32)
    qkv_second = draw_qkv_second(jax.random.fold_in(streams_of[18], 71), 0)
    out_first = bell_draw(streams_of[9], (HEAD_WIDTH, D), (0.111 * TOKENS ** 0.5), 40.0, ((0, 4), (1, 8)), jnp.float32)
    out_second = draw_out_second(jax.random.fold_in(streams_of[18], 71), 0)
    up_first = bell_draw(streams_of[11], (D, FF), (0.056 * TOKENS ** 0.5), 20.0, ((0, 8), (1, 4)), jnp.float32)
    up_second = draw_up_second(jax.random.fold_in(streams_of[18], 71), 0)
    down_first = bell_draw(streams_of[13], (FF, D), (0.111 * TOKENS ** 0.5), 40.0, ((0, 4), (1, 8)), jnp.float32)
    down_second = draw_down_second(jax.random.fold_in(streams_of[18], 71), 0)
    norm_first = bell_draw(streams_of[15], (8, D), (0.111 * TOKENS ** 0.5), 40.0, ((1, 8),), jnp.float32)
    norm_second = draw_norm_second(jax.random.fold_in(streams_of[18], 71), 0)
    out_grad = bell_draw(streams_of[17], (TOKENS, D), 1.0, 6.0, ((0, 8),))
    return {"block_input": block_input, "lengths": lengths, "norm_params": norm_params, "qkv_weight": qkv_weight, "out_weight": out_weight, "up_weight": up_weight, "down_weight": down_weight, "qkv_first": qkv_first, "qkv_second": qkv_second, "out_first": out_first, "out_second": out_second, "up_first": up_first, "up_second": up_second, "down_first": down_first, "down_second": down_second, "norm_first": norm_first, "norm_second": norm_second, "out_grad": out_grad}


norm_epsilon = 1e-05
rotary_base = 10000.0
mask_fill = -1000000000.0
first_decay = 0.9
second_decay = 0.999
adam_epsilon = 1e-06
trust_epsilon = 1e-06
decay_rate = 0.01
learn_rate = 0.25

@jax.custom_vjp
def low(v):
    return lax.optimization_barrier(v.astype(jnp.bfloat16)).astype(jnp.float32)

@jax.custom_vjp
def low_back(v):
    return v

def low_keep(v):
    return (low(v), None)

def low_pass(kept, grad):
    return (grad,)

def back_keep(v):
    return (v, None)

def back_low(kept, grad):
    return (low(grad),)
low.defvjp(low_keep, low_pass)
low_back.defvjp(back_keep, back_low)

def layer_norm(values, gain, offset):
    center = values - lax.optimization_barrier(jnp.mean(values, axis=-1, keepdims=True))
    inverse = lax.rsqrt(lax.optimization_barrier(jnp.mean(center * center, axis=-1, keepdims=True)) + norm_epsilon)
    return center * inverse * gain + offset

def rotary_tables(length, head_size):
    half_size = head_size // 2
    frequency = rotary_base ** (-(jnp.arange(half_size, dtype=jnp.float32) * 2.0 / head_size))
    angles = jnp.arange(length, dtype=jnp.float32)[:, None] * frequency[None, :]
    return (jnp.cos(angles), jnp.sin(angles))

def rotate(values, cosine_table, sine_table):
    half_size = values.shape[-1] // 2
    leading = values[..., :half_size]
    trailing = values[..., half_size:]
    cosine_part = cosine_table[:, None, :]
    sine_part = sine_table[:, None, :]
    return jnp.concatenate([leading * cosine_part - trailing * sine_part, trailing * cosine_part + leading * sine_part], axis=-1)

def matmul(left, right):
    return jnp.dot(left, right, precision=lax.Precision.HIGHEST)

def moment_step(gradient, first_state, second_state):
    first_new = first_decay * first_state + (1.0 - first_decay) * gradient
    second_new = second_decay * second_state + (1.0 - second_decay) * gradient * gradient
    direction = first_new / (1.0 - first_decay ** STEP) / (jnp.sqrt(second_new / (1.0 - second_decay ** STEP)) + adam_epsilon)
    return (first_new, second_new, direction)

def sequence_layer(inputs, live_len, qkv_flat, out_matrix, up_matrix, down_matrix, norms):
    row_count = inputs.shape[0]
    width_heads = HEADS * HEAD_DIM
    positions = jnp.arange(row_count)
    query_live = (positions < live_len).astype(jnp.float32)[:, None, None]
    visible = (positions[None, :] <= positions[:, None]) & (positions[None, :] < live_len)
    cosine_table, sine_table = rotary_tables(row_count, HEAD_DIM)
    normed_in = low(layer_norm(inputs, norms[0], norms[1]))
    projected = low_back(matmul(normed_in, qkv_flat)).reshape(row_count, 3, HEADS, HEAD_DIM)
    query = low(rotate(projected[:, 0], cosine_table, sine_table))
    keys = low(rotate(projected[:, 1], cosine_table, sine_table))
    values = low(projected[:, 2])
    scores = jnp.einsum('qhd,khd->hqk', query, keys, precision=lax.Precision.HIGHEST) * HEAD_DIM ** (-0.5)
    scores = jnp.where(visible[None], low_back(scores), mask_fill)
    top_score = lax.optimization_barrier(jnp.max(scores, axis=-1, keepdims=True))
    expo = jnp.exp(scores - top_score)
    probs = expo / lax.optimization_barrier(jnp.sum(expo, axis=-1, keepdims=True))
    mixed = jnp.einsum('hqk,khd->qhd', low(probs), values, precision=lax.Precision.HIGHEST) * query_live
    attn = low(low_back(mixed.reshape(row_count, width_heads)))
    branch = low_back(matmul(attn, out_matrix))
    hidden_state = inputs + layer_norm(branch, norms[2], norms[3])
    normed_mid = low(layer_norm(hidden_state, norms[4], norms[5]))
    up_part = low_back(matmul(normed_mid, up_matrix))
    active = low(jax.nn.gelu(up_part, approximate=False))
    mlp_out = low_back(matmul(active, down_matrix))
    return hidden_state + layer_norm(mlp_out, norms[6], norms[7])

def reference(block_input, lengths, norm_params, qkv_weight, out_weight, up_weight, down_weight, qkv_first, qkv_second, out_first, out_second, up_first, up_second, down_first, down_second, norm_first, norm_second, out_grad):
    width_heads = HEADS * HEAD_DIM
    inputs = block_input.astype(jnp.float32).reshape(SEQS, SEQ_LEN, D)
    cotangent = out_grad.astype(jnp.float32).reshape(SEQS, SEQ_LEN, D)

    def forward(stream, qkv_matrix, out_matrix, up_matrix, down_matrix, norms):
        qkv_flat = low(qkv_matrix).reshape(D, 3 * width_heads)
        out_low = low(out_matrix)
        up_low = low(up_matrix)
        down_low = low(down_matrix)

        def one_sequence(pair):
            return sequence_layer(pair[0], pair[1], qkv_flat, out_low, up_low, down_low, norms)
        return lax.map(jax.checkpoint(one_sequence), (stream, lengths))
    outputs, pullback = jax.vjp(forward, inputs, qkv_weight, out_weight, up_weight, down_weight, norm_params)
    grad_input, grad_qkv, grad_out, grad_up, grad_down, grad_norms = pullback(cotangent)
    masters = (qkv_weight, out_weight, up_weight, down_weight)
    gradients = (grad_qkv, grad_out, grad_up, grad_down)
    firsts = (qkv_first, out_first, up_first, down_first)
    seconds = (qkv_second, out_second, up_second, down_second)
    results = []
    weight_list = []
    update_list = []
    for master, gradient, first_state, second_state in zip(masters, gradients, firsts, seconds):
        first_new, second_new, direction = moment_step(gradient, first_state, second_state)
        update = direction + decay_rate * master
        weight_norm = jnp.sqrt(jnp.sum(master * master))
        update_norm = jnp.sqrt(jnp.sum(update * update) + trust_epsilon)
        results.append(master - learn_rate * (weight_norm / update_norm) * update)
        results.append(first_new)
        results.append(second_new)
        weight_list.append(weight_norm)
        update_list.append(update_norm)
    norm_first_new, norm_second_new, norm_direction = moment_step(grad_norms, norm_first, norm_second)
    norm_new = norm_params - learn_rate * norm_direction
    matrix_norms = jnp.stack([jnp.stack(weight_list), jnp.stack(update_list)])
    return (outputs.reshape(TOKENS, D).astype(jnp.bfloat16), grad_input.reshape(TOKENS, D).astype(jnp.bfloat16), results[0], results[1], results[2], results[3], results[4], results[5], results[6], results[7], results[8], results[9], results[10], results[11], norm_new, norm_first_new, norm_second_new, matrix_norms)
```

```python
import jax
import jax.numpy as jnp
from jax import lax
from jax.experimental import pallas as pl
from jax.experimental.pallas import tpu as pltpu
from jax.sharding import PartitionSpec as P

HEAD_DIM = 64
STEP = 10
CHUNKS = 2

norm_epsilon = 1e-05
rotary_base = 10000.0
mask_fill = -1000000000.0
first_decay = 0.9
second_decay = 0.999
adam_epsilon = 1e-06
trust_epsilon = 1e-06
decay_rate = 0.01
learn_rate = 0.25


def log2_of(count):
    bits = 0
    while (1 << bits) < count:
        bits += 1
    return bits


def swap(values, axis, bit):
    count = lax.axis_size(axis)
    return lax.ppermute(values, axis, [(i, i ^ (1 << bit)) for i in range(count)])


def sum_rows(send, keep):
    total = keep + swap(send, "tensor", 0)
    for bit in range(1, log2_of(lax.axis_size("tensor"))):
        total = total + swap(total, "tensor", bit)
    return total


def scatter_chunks(pieces):
    total = pieces
    for bit in range(log2_of(lax.axis_size("dp"))):
        middle = total.shape[0] // 2
        total = total[:middle] + swap(total[middle:], "dp", bit)
    return total[0]


def chunk_order(count):
    bits = log2_of(count)
    order = []
    for place in range(count):
        distance = 0
        for bit in range(bits):
            if place & (1 << (bits - 1 - bit)):
                distance |= 1 << bit
        order.append(distance)
    return order


def relative_columns(values, rank, count):
    own = values.shape[1] // count
    return jnp.concatenate(
        [
            lax.dynamic_slice_in_dim(values, (rank ^ distance) * own, own, 1)
            for distance in chunk_order(count)
        ],
        axis=1,
    )


def normalize(values):
    center = values - jnp.mean(values, axis=-1, keepdims=True)
    inverse = lax.rsqrt(jnp.mean(center * center, axis=-1, keepdims=True) + norm_epsilon)
    return center * inverse, inverse


def norm_back(incoming, normed, inverse, gain):
    scaled = incoming * gain
    inner = (
        scaled
        - jnp.mean(scaled, axis=-1, keepdims=True)
        - normed * jnp.mean(scaled * normed, axis=-1, keepdims=True)
    )
    return (inner * inverse, jnp.sum(incoming * normed, axis=0), jnp.sum(incoming, axis=0))


def rotary_tables(length, head_size):
    half_size = head_size // 2
    frequency = rotary_base ** (-(jnp.arange(half_size, dtype=jnp.float32) * 2.0 / head_size))
    angles = jnp.arange(length, dtype=jnp.float32)[:, None] * frequency[None, :]
    return (jnp.cos(angles), jnp.sin(angles))


def rotate(values, cosine_table, sine_table):
    half_size = values.shape[-1] // 2
    leading = values[..., :half_size]
    trailing = values[..., half_size:]
    cosine_part = cosine_table[:, None, :]
    sine_part = sine_table[:, None, :]
    return jnp.concatenate(
        [
            leading * cosine_part - trailing * sine_part,
            trailing * cosine_part + leading * sine_part,
        ],
        axis=-1,
    )


def moment_step(gradient, first_state, second_state):
    first_new = first_decay * first_state + (1.0 - first_decay) * gradient
    second_new = second_decay * second_state + (1.0 - second_decay) * gradient * gradient
    direction = (
        first_new
        / (1.0 - first_decay**STEP)
        / (jnp.sqrt(second_new / (1.0 - second_decay**STEP)) + adam_epsilon)
    )
    return (first_new, second_new, direction)


def gelu_parts(up):
    mass = 0.5 * (1.0 + lax.erf(up * (0.5**0.5)))
    slope = mass + up * jnp.exp(-0.5 * up * up) * ((2.0 * jnp.pi) ** -0.5)
    return up * mass, slope


def dot(left, right):
    return jnp.dot(left, right, preferred_element_type=jnp.float32)


def dot_rows(left, right):
    return lax.dot_general(left, right, (((0,), (0,)), ((), ())), preferred_element_type=jnp.float32)


def dot_wide(left, right):
    return lax.dot_general(left, right, (((1,), (1,)), ((), ())), preferred_element_type=jnp.float32)


def place_kernel(core_ref, mine_ref, theirs_ref, out_ref):
    core = core_ref[0]
    out_ref[:, core] = mine_ref[...].astype(out_ref.dtype)
    out_ref[:, 1 - core] = theirs_ref[...].astype(out_ref.dtype)


def place_rows(core, mine, theirs):
    count, rows, width = mine.shape
    return pl.pallas_call(
        place_kernel,
        out_shape=jax.ShapeDtypeStruct((count, 2, rows, width), jnp.bfloat16),
        in_specs=[
            pl.BlockSpec(memory_space=pltpu.SMEM),
            pl.BlockSpec(memory_space=pltpu.VMEM),
            pl.BlockSpec(memory_space=pltpu.VMEM),
        ],
        out_specs=pl.BlockSpec(memory_space=pltpu.VMEM),
        compiler_params=pltpu.CompilerParams(vmem_limit_bytes=32 * 1024 * 1024),
    )(core.reshape(1), mine, theirs)


def shards(
    block_input,
    lengths,
    norm_params,
    qkv_weight,
    out_weight,
    up_weight,
    down_weight,
    qkv_first,
    qkv_second,
    out_first,
    out_second,
    up_first,
    up_second,
    down_first,
    down_second,
    norm_first,
    norm_second,
    out_grad,
):
    low = jnp.bfloat16
    row_count, width = block_input.shape
    head_size = HEAD_DIM
    local_width = qkv_weight.shape[2]
    local_heads = local_width // head_size
    score_scale = head_size ** (-0.5)
    group_count = lax.axis_size("dp")
    group_rank = lax.axis_index("dp")
    core = lax.rem(lax.axis_index("tensor"), 2)
    own_rows = width // group_count
    own_start = group_rank * own_rows
    part = row_count // CHUNKS
    half = part // 2
    own_at = [c * part + core * half for c in range(CHUNKS)]
    other_at = [c * part + (1 - core) * half for c in range(CHUNKS)]

    def rows_at(values, start):
        return lax.dynamic_slice_in_dim(values, start, half, 0)

    def both_cores(mine):
        theirs = swap(mine, "tensor", 0)
        return place_rows(jnp.int32(0), mine[None], theirs[None]).reshape(part, mine.shape[1])

    def in_place(mine):
        stacked = jnp.stack(mine)
        theirs = swap(stacked, "tensor", 0)
        return place_rows(core, stacked, theirs).reshape(row_count, mine[0].shape[1])

    qkv_own = lax.dynamic_slice_in_dim(qkv_weight, own_start, own_rows, 0)
    out_own = lax.dynamic_slice_in_dim(out_weight, own_start, own_rows, 1)
    up_own = lax.dynamic_slice_in_dim(up_weight, own_start, own_rows, 0)
    down_own = lax.dynamic_slice_in_dim(down_weight, own_start, own_rows, 1)
    norm_own = lax.dynamic_slice_in_dim(norm_params, own_start, own_rows, 1)
    masters = (qkv_own, out_own, up_own, down_own)
    qkv_low = qkv_weight.reshape(width, 3 * local_width).astype(low)
    out_low = out_weight.astype(low)
    up_low = up_weight.astype(low)
    down_low = down_weight.astype(low)
    residual = block_input.astype(jnp.float32)
    live_len = lengths[0]
    positions = jnp.arange(row_count)
    query_live = (positions < live_len).astype(jnp.float32)[:, None, None]
    cosine_table, sine_table = rotary_tables(row_count, head_size)

    stat_in_all, inverse_in_all = normalize(residual)
    normed_in_low = (stat_in_all * norm_params[0] + norm_params[1]).astype(low)
    projected = dot(normed_in_low, qkv_low).reshape(row_count, 3, local_heads, head_size)
    query = rotate(projected[:, 0], cosine_table, sine_table).astype(low)
    keys = rotate(projected[:, 1], cosine_table, sine_table).astype(low)
    values = projected[:, 2].astype(low)

    def scores_of(rows, reach):
        visible = (positions[None, :reach] <= positions[rows, None]) & (
            positions[None, :reach] < live_len
        )
        raw_scores = (
            jnp.einsum(
                "qhd,khd->hqk", query[rows], keys[:reach], preferred_element_type=jnp.float32
            )
            * score_scale
        )
        return jnp.where(visible[None], raw_scores, mask_fill)

    attn_parts = []
    branch_parts = []
    log_totals = []
    for c in range(CHUNKS):
        rows = slice(c * part, (c + 1) * part)
        reach = (c + 1) * part
        scores = scores_of(rows, reach)
        top_score = jnp.max(scores, axis=-1, keepdims=True)
        expo = jnp.exp(scores - top_score)
        total_mass = jnp.sum(expo, axis=-1, keepdims=True)
        probs = expo / total_mass
        log_totals.append(top_score + jnp.log(total_mass))
        mixed = (
            jnp.einsum(
                "hqk,khd->qhd",
                probs.astype(low),
                values[:reach],
                preferred_element_type=jnp.float32,
            )
            * query_live[rows]
        )
        attn_c = mixed.reshape(part, local_width).astype(low)
        attn_parts.append(attn_c)
        send = dot(rows_at(attn_c, (1 - core) * half), out_low)
        keep = dot(rows_at(attn_c, core * half), out_low)
        branch_parts.append(sum_rows(send, keep))

    hidden = []
    stat_branch = []
    stat_mid = []
    normed_mid = []
    up_parts = []
    active = []
    mlp_parts = []
    for c in range(CHUNKS):
        stat, inverse = normalize(branch_parts[c])
        stat_branch.append((stat, inverse))
        inputs = rows_at(residual, own_at[c])
        hidden.append(inputs + stat * norm_params[2] + norm_params[3])
        stat, inverse = normalize(hidden[c])
        stat_mid.append((stat, inverse))
        normed_mid.append(both_cores(stat * norm_params[4] + norm_params[5]))
        up = dot(normed_mid[c], up_low)
        value, slope = gelu_parts(up)
        up_parts.append(slope)
        active.append(value.astype(low))
        send = dot(active[c][half:], down_low)
        keep = dot(active[c][:half], down_low)
        mlp_parts.append(sum_rows(send, keep))

    block_rows = []
    grad_final = []
    grad_mlp = []
    gain_three = offset_three = 0.0
    for c in range(CHUNKS):
        stat, inverse = normalize(mlp_parts[c])
        block_rows.append(hidden[c] + stat * norm_params[6] + norm_params[7])
        grad_final.append(rows_at(out_grad, own_at[c]).astype(jnp.float32))
        back, gain, offset = norm_back(grad_final[c], stat, inverse, norm_params[6])
        gain_three, offset_three = gain_three + gain, offset_three + offset
        grad_mlp.append(both_cores(back))
    block_output = in_place(block_rows)

    grad_up_low = []
    grad_mid = []
    for c in range(CHUNKS):
        grad_active = dot_wide(grad_mlp[c], down_low)
        grad_up_low.append((grad_active * up_parts[c]).astype(low))
        send = dot_wide(grad_up_low[c][half:], up_low)
        keep = dot_wide(grad_up_low[c][:half], up_low)
        grad_mid.append(sum_rows(send, keep))

    def stacked_columns(left, right, split):
        product = dot_rows(left, relative_columns(right, group_rank, group_count))
        return product.reshape(left.shape[1], group_count, split).transpose(1, 0, 2)

    def stacked_rows(left, right):
        product = dot_rows(relative_columns(left, group_rank, group_count), right)
        return product.reshape(group_count, own_rows, right.shape[1])

    grad_down = scatter_chunks(
        stacked_columns(jnp.concatenate(active), jnp.concatenate(grad_mlp), own_rows)
    )
    grad_up = scatter_chunks(
        stacked_rows(jnp.concatenate(normed_mid), jnp.concatenate(grad_up_low))
    )

    grad_hidden = []
    grad_branch = []
    gain_two = offset_two = gain_one = offset_one = 0.0
    for c in range(CHUNKS):
        back, gain, offset = norm_back(grad_mid[c], *stat_mid[c], norm_params[4])
        gain_two, offset_two = gain_two + gain, offset_two + offset
        grad_hidden.append(grad_final[c] + back)
        back, gain, offset = norm_back(grad_hidden[c], *stat_branch[c], norm_params[2])
        gain_one, offset_one = gain_one + gain, offset_one + offset
        grad_branch.append(back)
    grad_branch_low = in_place(grad_branch)
    attn_low = jnp.concatenate(attn_parts)
    grad_attn = dot_wide(grad_branch_low, out_low)
    grad_mixed = grad_attn.astype(low).reshape(
        row_count, local_heads, head_size
    ) * query_live.astype(low)
    scores_again = scores_of(slice(0, row_count), row_count)
    probs_again = jnp.exp(scores_again - jnp.concatenate(log_totals, axis=1))
    grad_values = jnp.einsum(
        "hqk,qhd->khd", probs_again.astype(low), grad_mixed, preferred_element_type=jnp.float32
    )
    grad_probs = jnp.einsum("qhd,khd->hqk", grad_mixed, values, preferred_element_type=jnp.float32)
    row_inner = jnp.sum(grad_probs * probs_again, axis=-1, keepdims=True)
    grad_scores = (probs_again * (grad_probs - row_inner)).astype(low)
    grad_query = (
        jnp.einsum("hqk,khd->qhd", grad_scores, keys, preferred_element_type=jnp.float32)
        * score_scale
    )
    grad_keys = (
        jnp.einsum("hqk,qhd->khd", grad_scores, query, preferred_element_type=jnp.float32)
        * score_scale
    )
    grad_rows = jnp.stack(
        [
            rotate(grad_query, cosine_table, -sine_table),
            rotate(grad_keys, cosine_table, -sine_table),
            grad_values,
        ],
        axis=1,
    )
    grad_rows_low = grad_rows.reshape(row_count, 3 * local_width).astype(low)
    grad_qkv = scatter_chunks(stacked_rows(normed_in_low, grad_rows_low)).reshape(
        own_rows, 3, local_width
    )
    grad_out = scatter_chunks(stacked_columns(attn_low, grad_branch_low, own_rows))

    gain_zero = offset_zero = 0.0
    input_rows = []
    for c in range(CHUNKS):
        send = dot_wide(rows_at(grad_rows_low, other_at[c]), qkv_low)
        keep = dot_wide(rows_at(grad_rows_low, own_at[c]), qkv_low)
        total = sum_rows(send, keep)
        back, gain, offset = norm_back(
            total, rows_at(stat_in_all, own_at[c]), rows_at(inverse_in_all, own_at[c]), norm_params[0]
        )
        gain_zero, offset_zero = gain_zero + gain, offset_zero + offset
        input_rows.append(grad_hidden[c] + back)
    input_grad = in_place(input_rows)

    grad_norms = jnp.stack(
        [
            gain_zero,
            offset_zero,
            gain_one,
            offset_one,
            gain_two,
            offset_two,
            gain_three,
            offset_three,
        ]
    )
    grad_norms = grad_norms + swap(grad_norms, "tensor", 0)
    norm_chunks = relative_columns(grad_norms, group_rank, group_count)
    norm_chunks = norm_chunks.reshape(8, group_count, own_rows).transpose(1, 0, 2)
    norm_gradient = scatter_chunks(norm_chunks)

    own_grads = (grad_qkv, grad_out, grad_up, grad_down)
    firsts = (qkv_first, out_first, up_first, down_first)
    seconds = (qkv_second, out_second, up_second, down_second)
    stepped = [
        moment_step(gradient, first_state, second_state)
        for gradient, first_state, second_state in zip(own_grads, firsts, seconds)
    ]
    updates = [entry[2] + decay_rate * master for entry, master in zip(stepped, masters)]
    squares = jnp.stack(
        [jnp.stack([jnp.sum(v * v) for v in group]) for group in (masters, updates)]
    )
    for axis in ("tensor", "dp"):
        for bit in range(log2_of(lax.axis_size(axis))):
            squares = squares + swap(squares, axis, bit)
    weight_magnitude = jnp.sqrt(squares[0])
    update_magnitude = jnp.sqrt(squares[1] + trust_epsilon)
    new_masters = [
        master - learn_rate * (weight_magnitude[index] / update_magnitude[index]) * update
        for index, (master, update) in enumerate(zip(masters, updates))
    ]
    norm_first_new, norm_second_new, norm_direction = moment_step(
        norm_gradient, norm_first, norm_second
    )
    norm_new = norm_own - learn_rate * norm_direction
    matrix_norms = jnp.stack([weight_magnitude, update_magnitude])
    return (
        block_output,
        input_grad,
        new_masters[0],
        stepped[0][0],
        stepped[0][1],
        new_masters[1],
        stepped[1][0],
        stepped[1][1],
        new_masters[2],
        stepped[2][0],
        stepped[2][1],
        new_masters[3],
        stepped[3][0],
        stepped[3][1],
        norm_new,
        norm_first_new,
        norm_second_new,
        matrix_norms,
    )

def solution(mesh):
    in_specs = (
        P("dp", None),
        P("dp"),
        P(),
        P(None, None, "tensor"),
        P("tensor", None),
        P(None, "tensor"),
        P("tensor", None),
        P("dp", None, "tensor"),
        P("dp", None, "tensor"),
        P("tensor", "dp"),
        P("tensor", "dp"),
        P("dp", "tensor"),
        P("dp", "tensor"),
        P("tensor", "dp"),
        P("tensor", "dp"),
        P(None, "dp"),
        P(None, "dp"),
        P("dp", None),
    )
    out_specs = (
        P("dp", None),
        P("dp", None),
        P("dp", None, "tensor"),
        P("dp", None, "tensor"),
        P("dp", None, "tensor"),
        P("tensor", "dp"),
        P("tensor", "dp"),
        P("tensor", "dp"),
        P("dp", "tensor"),
        P("dp", "tensor"),
        P("dp", "tensor"),
        P("tensor", "dp"),
        P("tensor", "dp"),
        P("tensor", "dp"),
        P(None, "dp"),
        P(None, "dp"),
        P(None, "dp"),
        P(),
    )
    return jax.shard_map(shards, mesh=mesh, in_specs=in_specs, out_specs=out_specs, check_vma=False)
```

```python
import functools

import jax
import jax.numpy as jnp
import numpy as np
from jax import lax
from jax.experimental import pallas as pl
from jax.experimental.pallas import tpu as pltpu
from jax.sharding import PartitionSpec as P

HEAD_DIM = 64
STEP = 10
CHUNKS = 2
LANES = 128

norm_epsilon = 1e-05
rotary_base = 10000.0
mask_fill = -1000000000.0
first_decay = 0.9
second_decay = 0.999
adam_epsilon = 1e-06
trust_epsilon = 1e-06
decay_rate = 0.01
learn_rate = 0.25

LOW = jnp.bfloat16
WIDE = jnp.float32
VMEM = pl.BlockSpec(memory_space=pltpu.VMEM)
SMEM = pl.BlockSpec(memory_space=pltpu.SMEM)
ANY = pl.BlockSpec(memory_space=pl.ANY)


def log2_of(count):
    bits = 0
    while (1 << bits) < count:
        bits += 1
    return bits


def after(values, *earlier):
    return lax.optimization_barrier((values,) + earlier)[0]


def swap(values, axis, distance):
    count = lax.axis_size(axis)
    return lax.ppermute(values, axis, [(i, i ^ distance) for i in range(count)])


def sum_rows(send, keep):
    mine, theirs = keep, swap(send, "tensor", 1)
    for bit in range(1, log2_of(lax.axis_size("tensor"))):
        mine = mine + theirs
        theirs = swap(mine, "tensor", 1 << bit)
    return mine, theirs


def sum_all(values, axis, most=2):
    bits = log2_of(lax.axis_size(axis))
    start = 0
    while start < bits:
        taken = min(most, bits - start)
        terms = [values] + [
            swap(values, axis, distance << start) for distance in range(1, 1 << taken)
        ]
        while len(terms) > 1:
            terms = [terms[i] + terms[i + 1] for i in range(0, len(terms), 2)]
        values = terms[0]
        start += taken
    return values


def chunk_order(count, bits):
    order = [0]
    for bit in reversed(bits):
        order = order + [distance ^ (1 << bit) for distance in order]
    return order


def scatter_terms(send, keep, bits):
    terms = [keep, swap(send, "dp", 1 << bits[0])]
    size = keep.shape[0]
    for bit in bits[1:]:
        size //= 2
        outgoing = terms[0][size : 2 * size]
        for term in terms[1:]:
            outgoing = outgoing + term[size : 2 * size]
        terms.append(swap(outgoing, "dp", 1 << bit))
    return terms


def normalize(values):
    center = values - jnp.mean(values, axis=-1, keepdims=True)
    inverse = lax.rsqrt(jnp.mean(center * center, axis=-1, keepdims=True) + norm_epsilon)
    return center * inverse, inverse


def norm_back(incoming, normed, inverse, gain):
    scaled = incoming * gain
    inner = (
        scaled
        - jnp.mean(scaled, axis=-1, keepdims=True)
        - normed * jnp.mean(scaled * normed, axis=-1, keepdims=True)
    )
    gain_grad = jnp.sum(incoming * normed, axis=0, keepdims=True)
    return inner * inverse, gain_grad, jnp.sum(incoming, axis=0, keepdims=True)


def rotary_tables(length):
    half = HEAD_DIM // 2
    lane = np.arange(LANES)
    frequency = (rotary_base ** (-((lane % half).astype(np.float32) * 2.0 / HEAD_DIM))).astype(np.float32)
    angles = np.arange(length, dtype=np.float32)[:, None] * frequency[None, :]
    sign = np.where(lane % HEAD_DIM < half, -1.0, 1.0)
    cosine = np.cos(angles.astype(np.float64)).astype(np.float32)
    sine = (np.sin(angles.astype(np.float64)) * sign[None, :]).astype(np.float32)
    return jnp.asarray(cosine), jnp.asarray(sine)


def turn(values, cosine, sine):
    half = HEAD_DIM // 2
    lane = lax.broadcasted_iota(jnp.int32, (1, LANES), 1)
    first = lax.rem(lane, HEAD_DIM) < half
    tiles = []
    for start in range(0, values.shape[1], LANES):
        tile = values[:, start : start + LANES]
        other = jnp.where(
            first, pltpu.roll(tile, LANES - half, 1), pltpu.roll(tile, half, 1)
        )
        tiles.append(tile * cosine + other * sine)
    return tiles[0] if len(tiles) == 1 else jnp.concatenate(tiles, axis=1)


def gelu_mass(up):
    return 0.5 * (1.0 + lax.erf(up * (0.5**0.5)))


def dot(left, right):
    return jnp.dot(left, right, preferred_element_type=WIDE)


def dot_rows(left, right):
    return lax.dot_general(left, right, (((0,), (0,)), ((), ())), preferred_element_type=WIDE)


def dot_wide(left, right):
    return lax.dot_general(left, right, (((1,), (1,)), ((), ())), preferred_element_type=WIDE)


def of_head(values, head):
    lane = lax.broadcasted_iota(jnp.int32, (1, values.shape[1]), 1)
    mine = (lane >= head * HEAD_DIM) & (lane < (head + 1) * HEAD_DIM)
    return jnp.where(mine, values, jnp.zeros_like(values))


def core_index():
    return lax.rem(lax.axis_index("tensor"), 2)


def shaped(*shape, kind=WIDE):
    return jax.ShapeDtypeStruct(shape, kind)


def call(kernel, outs, args, specs=None, flops=0, scratch=(), megabytes=40, name=None):
    moved = sum(a.size * a.dtype.itemsize for a in args) + sum(
        int(np.prod(o.shape)) * jnp.dtype(o.dtype).itemsize for o in outs
    )
    blocks = any(spec.block_shape is not None for spec in specs or [])
    return pl.pallas_call(
        kernel,
        grid=(1,) if blocks else (),
        out_shape=tuple(outs),
        in_specs=specs or [VMEM] * len(args),
        out_specs=tuple([VMEM] * len(outs)),
        scratch_shapes=list(scratch),
        compiler_params=pltpu.CompilerParams(vmem_limit_bytes=megabytes * 1024 * 1024),
        cost_estimate=pl.CostEstimate(flops=int(flops), bytes_accessed=int(moved), transcendentals=0),
        name=name,
    )(*args)


def project(normed, weights, cosine, sine):
    query = turn(dot(normed, weights[0]), cosine, sine).astype(LOW)
    keys = turn(dot(normed, weights[1]), cosine, sine).astype(LOW)
    return query, keys, dot(normed, weights[2]).astype(LOW)


def attend(query, keys, values, first_row, live_len):
    rows, reach = query.shape[0], keys.shape[0]
    row = first_row + lax.broadcasted_iota(jnp.int32, (rows, reach), 0)
    column = lax.broadcasted_iota(jnp.int32, (rows, reach), 1)
    visible = (column <= row) & (column < live_len)
    lane = lax.broadcasted_iota(jnp.int32, (1, LANES), 1)
    mixed = jnp.zeros((rows, query.shape[1]), WIDE)
    masses = jnp.zeros((rows, LANES), WIDE)
    for head in range(query.shape[1] // HEAD_DIM):
        scores = dot_wide(of_head(query, head), keys) * HEAD_DIM ** (-0.5)
        scores = jnp.where(visible, scores, mask_fill)
        top = jnp.max(scores, axis=-1, keepdims=True)
        expo = jnp.exp(scores - top)
        total = jnp.sum(expo, axis=-1, keepdims=True)
        probs = (expo * (1.0 / total)).astype(LOW)
        mixed = mixed + dot(probs, of_head(values, head))
        masses = jnp.where(lane == head, top + jnp.log(total), masses)
    live = first_row + lax.broadcasted_iota(jnp.int32, (rows, 1), 0) < live_len
    return jnp.where(live, mixed, 0.0).astype(LOW), masses


def split_rows(left_ref, right, send_ref, keep_ref, how):
    half = send_ref.shape[0]
    core = core_index()
    send_ref[...] = how(left_ref[pl.ds((1 - core) * half, half), :], right)
    keep_ref[...] = how(left_ref[pl.ds(core * half, half), :], right)


def first_kernel(
    live_ref, x_ref, norm_ref, cos_ref, sin_ref, qkv_ref, out_ref,
    qkv_low_ref, out_low_ref, normed_ref, q_ref, k_ref, v_ref, attn_ref, mass_ref, send_ref, keep_ref,
    qkv_in, out_in, arrived,
):
    copies = [
        pltpu.make_async_copy(qkv_ref.at[j], qkv_in.at[j], arrived.at[j]) for j in range(3)
    ]
    copies.append(pltpu.make_async_copy(out_ref, out_in, arrived.at[3]))
    for copy in copies:
        copy.start()
    stat, _ = normalize(x_ref[...].astype(WIDE))
    normed = (stat * norm_ref[0:1, :] + norm_ref[1:2, :]).astype(LOW)
    normed_ref[...] = normed
    weights = []
    for j in range(3):
        copies[j].wait()
        weights.append(qkv_in[j].astype(LOW))
        qkv_low_ref[j] = weights[j]
    query, keys, values = project(normed, weights, cos_ref[...], sin_ref[...])
    q_ref[...], k_ref[...], v_ref[...] = query, keys, values
    attn_ref[...], mass_ref[...] = attend(query, keys, values, 0, live_ref[0])
    copies[3].wait()
    out_low = out_in[...].astype(LOW)
    out_low_ref[...] = out_low
    split_rows(attn_ref, out_low, send_ref, keep_ref, dot)


def next_kernel(
    live_ref, x_ref, norm_ref, cos_ref, sin_ref, qkv_low_ref, out_low_ref, *refs, first_row
):
    earlier = first_row // x_ref.shape[0]
    k_before, v_before = refs[:earlier], refs[earlier : 2 * earlier]
    normed_ref, q_ref, k_ref, v_ref, attn_ref, mass_ref, send_ref, keep_ref = refs[2 * earlier :]
    stat, _ = normalize(x_ref[...].astype(WIDE))
    normed = (stat * norm_ref[0:1, :] + norm_ref[1:2, :]).astype(LOW)
    normed_ref[...] = normed
    weights = [qkv_low_ref[j] for j in range(3)]
    query, keys, values = project(normed, weights, cos_ref[...], sin_ref[...])
    q_ref[...], k_ref[...], v_ref[...] = query, keys, values
    keys = jnp.concatenate([ref[...] for ref in k_before] + [keys], axis=0)
    values = jnp.concatenate([ref[...] for ref in v_before] + [values], axis=0)
    attn_ref[...], mass_ref[...] = attend(query, keys, values, first_row, live_ref[0])
    split_rows(attn_ref, out_low_ref[...], send_ref, keep_ref, dot)


def middle_kernel(first_row, x_ref, norm_ref, mine_ref, theirs_ref, branch_ref, hidden_ref, normed_ref):
    half = mine_ref.shape[0]
    branch = mine_ref[...] + theirs_ref[...]
    branch_ref[...] = branch
    stat, _ = normalize(branch)
    inputs = x_ref[pl.ds(first_row + core_index() * half, half), :].astype(WIDE)
    hidden = inputs + stat * norm_ref[2:3, :] + norm_ref[3:4, :]
    hidden_ref[...] = hidden
    stat, _ = normalize(hidden)
    normed_ref[...] = stat * norm_ref[4:5, :] + norm_ref[5:6, :]


def mlp_kernel(own_ref, other_ref, up_w_ref, down_w_ref, normed_ref, up_ref, active_ref, send_ref, keep_ref):
    half = own_ref.shape[0]
    normed = jnp.concatenate([own_ref[...].astype(LOW), other_ref[...].astype(LOW)], axis=0)
    normed_ref[...] = normed
    step = min(256, up_w_ref.shape[1])
    total = None
    for start in range(0, up_w_ref.shape[1], step):
        block = slice(start, start + step)
        up = dot(normed, up_w_ref[:, block])
        up_ref[:, block] = up
        active = (up * gelu_mass(up)).astype(LOW)
        active_ref[:, block] = active
        product = dot(active, down_w_ref[block, :])
        total = product if total is None else total + product
    keep_ref[...] = total[:half]
    send_ref[...] = total[half:]


def loss_kernel(
    first_row, grad_ref, norm_ref, hidden_ref, mine_ref, theirs_ref, block_ref, back_ref, sums_ref
):
    half = mine_ref.shape[0]
    stat, inverse = normalize(mine_ref[...] + theirs_ref[...])
    block_ref[...] = hidden_ref[...] + stat * norm_ref[6:7, :] + norm_ref[7:8, :]
    incoming = grad_ref[pl.ds(first_row + core_index() * half, half), :].astype(WIDE)
    back, gain, offset = norm_back(incoming, stat, inverse, norm_ref[6:7, :])
    back_ref[...] = back
    sums_ref[0:1, :] = gain
    sums_ref[1:2, :] = offset


def mlp_back_kernel(
    own_ref, other_ref, up_ref, up_w_ref, down_w_ref, grad_mlp_ref, grad_up_ref, send_ref, keep_ref
):
    half = own_ref.shape[0]
    grad_mlp = jnp.concatenate([own_ref[...].astype(LOW), other_ref[...].astype(LOW)], axis=0)
    grad_mlp_ref[...] = grad_mlp
    step = min(256, up_w_ref.shape[1])
    total = None
    for start in range(0, up_w_ref.shape[1], step):
        block = slice(start, start + step)
        up = up_ref[:, block]
        slope = gelu_mass(up) + up * jnp.exp(-0.5 * up * up) * float((2.0 * np.pi) ** -0.5)
        grad_up = (dot_wide(grad_mlp, down_w_ref[block, :]) * slope).astype(LOW)
        grad_up_ref[:, block] = grad_up
        product = dot_wide(grad_up, up_w_ref[:, block])
        total = product if total is None else total + product
    keep_ref[...] = total[:half]
    send_ref[...] = total[half:]


def norms_back_kernel(
    first_row, grad_ref, norm_ref, hidden_ref, branch_ref, mine_ref, theirs_ref,
    grad_hidden_ref, back_ref, sums_ref,
):
    half = mine_ref.shape[0]
    stat, inverse = normalize(hidden_ref[...])
    back, gain, offset = norm_back(
        mine_ref[...] + theirs_ref[...], stat, inverse, norm_ref[4:5, :]
    )
    incoming = grad_ref[pl.ds(first_row + core_index() * half, half), :].astype(WIDE)
    grad_hidden = incoming + back
    grad_hidden_ref[...] = grad_hidden
    sums_ref[2:3, :] = gain
    sums_ref[3:4, :] = offset
    stat, inverse = normalize(branch_ref[...])
    back, gain, offset = norm_back(grad_hidden, stat, inverse, norm_ref[2:3, :])
    back_ref[...] = back
    sums_ref[0:1, :] = gain
    sums_ref[1:2, :] = offset


def attention_back_kernel(live_ref, out_low_ref, cos_ref, sin_ref, *refs, chunks):
    groups = [refs[i * chunks : (i + 1) * chunks] for i in range(6)]
    own, other, query_refs, key_refs, value_refs, mass_refs = groups
    grad_branch_ref, rows_ref = refs[6 * chunks : 6 * chunks + 2]
    keys_sum, values_sum = refs[6 * chunks + 2 :]
    half = own[0].shape[0]
    part = 2 * half
    core = core_index()
    live_len = live_ref[0]
    local = rows_ref.shape[1] // 3
    heads = local // HEAD_DIM
    for c in range(chunks):
        grad_branch_ref[pl.ds(c * part + core * half, half), :] = own[c][...].astype(LOW)
        grad_branch_ref[pl.ds(c * part + (1 - core) * half, half), :] = other[c][...].astype(LOW)
    keys_all = jnp.concatenate([ref[...] for ref in key_refs], axis=0)
    values_all = jnp.concatenate([ref[...] for ref in value_refs], axis=0)
    for c in range(chunks):
        reach = (c + 1) * part
        first_row = c * part
        row = first_row + lax.broadcasted_iota(jnp.int32, (part, reach), 0)
        column = lax.broadcasted_iota(jnp.int32, (part, reach), 1)
        visible = (column <= row) & (column < live_len)
        live = first_row + lax.broadcasted_iota(jnp.int32, (part, 1), 0) < live_len
        grad_attn = dot_wide(grad_branch_ref[first_row : first_row + part, :], out_low_ref[...])
        grad_mixed = jnp.where(live, grad_attn, 0.0).astype(LOW)
        query, masses = query_refs[c][...], mass_refs[c][...]
        keys, values = keys_all[:reach], values_all[:reach]
        grad_query = jnp.zeros((part, local), WIDE)
        grad_keys = jnp.zeros((reach, local), WIDE)
        grad_values = jnp.zeros((reach, local), WIDE)
        for head in range(heads):
            query_h, grad_h = of_head(query, head), of_head(grad_mixed, head)
            scores = dot_wide(query_h, keys) * HEAD_DIM ** (-0.5)
            scores = jnp.where(visible, scores, mask_fill)
            probs = jnp.exp(scores - masses[:, head : head + 1])
            grad_values = grad_values + dot_rows(probs.astype(LOW), grad_h)
            grad_probs = dot_wide(grad_h, values)
            inner = jnp.sum(grad_probs * probs, axis=-1, keepdims=True)
            grad_scores = (probs * (grad_probs - inner)).astype(LOW)
            grad_query = grad_query + dot(grad_scores, of_head(keys, head))
            grad_keys = grad_keys + dot_rows(grad_scores, query_h)
        cosine = cos_ref[first_row : first_row + part, :]
        sine = sin_ref[first_row : first_row + part, :]
        grad_query = turn(grad_query * HEAD_DIM ** (-0.5), cosine, -sine)
        rows_ref[first_row : first_row + part, 0:local] = grad_query.astype(LOW)
        if c == 0:
            keys_sum[0:reach, :] = grad_keys
            values_sum[0:reach, :] = grad_values
        else:
            keys_sum[0:first_row, :] += grad_keys[:first_row]
            keys_sum[first_row:reach, :] = grad_keys[first_row:]
            values_sum[0:first_row, :] += grad_values[:first_row]
            values_sum[first_row:reach, :] = grad_values[first_row:]
    grad_keys = turn(keys_sum[...] * HEAD_DIM ** (-0.5), cos_ref[...], -sin_ref[...])
    rows_ref[:, local : 2 * local] = grad_keys.astype(LOW)
    rows_ref[:, 2 * local : 3 * local] = values_sum[...].astype(LOW)


def picked_columns(refs, distances, own):
    rank = lax.axis_index("dp")
    blocks = []
    for distance in distances:
        start = pl.multiple_of(lax.bitwise_xor(rank, distance) * own, own)
        pieces = [ref[:, pl.ds(start, own)].astype(LOW) for ref in refs]
        blocks.append(pieces[0] if len(pieces) == 1 else jnp.concatenate(pieces, axis=0))
    return blocks[0] if len(blocks) == 1 else jnp.concatenate(blocks, axis=1)


def whole_rows(refs, window):
    pieces = [ref[:, window[0] : window[1]].astype(LOW) for ref in refs]
    return pieces[0] if len(pieces) == 1 else jnp.concatenate(pieces, axis=0)


def owned_columns_kernel(*refs, pairs, jobs, own):
    (lefts, rights), outs = pairs, refs[sum(pairs) :]
    left, right = refs[:lefts], refs[lefts : lefts + rights]
    for (distances, window), out_ref in zip(jobs, outs):
        rows = whole_rows(left, window)
        product = dot_rows(rows, picked_columns(right, distances, own))
        for place in range(len(distances)):
            out_ref[place] = product[:, place * own : (place + 1) * own]


def owned_rows_kernel(*refs, pairs, jobs, own):
    (lefts, rights), outs = pairs, refs[sum(pairs) :]
    left, right = refs[:lefts], refs[lefts : lefts + rights]
    for (distances, window), out_ref in zip(jobs, outs):
        product = dot_rows(picked_columns(left, distances, own), whole_rows(right, window))
        for place in range(len(distances)):
            out_ref[place] = product[place * own : (place + 1) * own, :]


def owned_parts_kernel(*refs, pairs, jobs, own):
    (lefts, rights), outs = pairs, refs[sum(pairs) :]
    left, right = refs[:lefts], refs[lefts : lefts + rights]
    for (distances, window), out_ref in zip(jobs, outs):
        local = out_ref.shape[3]
        columns = (window[0] * local, window[1] * local)
        product = dot_rows(picked_columns(left, distances, own), whole_rows(right, columns))
        for place in range(len(distances)):
            for j in range(window[1] - window[0]):
                out_ref[place, j] = product[
                    place * own : (place + 1) * own, j * local : (j + 1) * local
                ]


def rounded_kernel(*refs):
    refs[-1][...] = whole_rows(refs[:-1], (0, refs[0].shape[1]))


def narrow_products(kernel, left, right, jobs, outs, own):
    rank = lax.axis_index("dp")
    joined = []
    for arrays in (left, right):
        rows = sum(array.shape[0] for array in arrays)
        joined.append(call(rounded_kernel, [shaped(rows, arrays[0].shape[1], kind=LOW)], arrays)[0])
    results = []
    for (distances, window), out in zip(jobs, outs):
        pick = lambda array: jnp.concatenate(
            [lax.dynamic_slice_in_dim(array, (rank ^ d) * own, own, 1) for d in distances], axis=1
        )
        if kernel is owned_columns_kernel:
            product = dot_rows(joined[0][:, window[0] : window[1]], pick(joined[1]))
            product = product.reshape(-1, len(distances), own).transpose(1, 0, 2)
        elif kernel is owned_rows_kernel:
            product = dot_rows(pick(joined[0]), joined[1][:, window[0] : window[1]])
            product = product.reshape(out.shape)
        else:
            local = out.shape[3]
            columns = joined[1][:, window[0] * local : window[1] * local]
            product = dot_rows(pick(joined[0]), columns)
            product = product.reshape(len(distances), own, -1, local).transpose(0, 2, 1, 3)
        results.append(product)
    return results


def owner_products(kernel, left, right, pieces, own, send, name):
    count = lax.axis_size("dp")
    jobs, outs = [], []
    for window, bits in pieces:
        order = chunk_order(count, bits)
        order = order[count // 2 :] if send else order[: count // 2]
        jobs.append((order, window))
        size = window[1] - window[0]
        if kernel is owned_columns_kernel:
            outs.append(shaped(len(order), size, own))
        elif kernel is owned_rows_kernel:
            outs.append(shaped(len(order), own, size))
        else:
            outs.append(shaped(len(order), size, own, right[0].shape[1] // 3))
    if own % LANES:
        return narrow_products(kernel, left, right, jobs, outs, own)
    rows = sum(array.shape[0] for array in left)
    flops = 2 * rows * sum(int(np.prod(out.shape)) for out in outs)
    return call(
        functools.partial(kernel, pairs=(len(left), len(right)), jobs=jobs, own=own),
        outs,
        [*left, *right],
        flops=flops,
        name=name,
    )


def cut_windows(size):
    cut = size // 4 * 3
    return [(0, cut), (cut, size)]


def first_block(array):
    return pl.BlockSpec((1,) + array.shape[1:], lambda i: (0,) * array.ndim)


def input_back_kernel(rows_ref, qkv_low_ref, send_ref, keep_ref, *, chunks):
    half = send_ref.shape[0] // chunks
    local = qkv_low_ref.shape[2]
    core = core_index()
    for c in range(chunks):
        for target, which in ((send_ref, 1 - core), (keep_ref, core)):
            rows = rows_ref[pl.ds(c * 2 * half + which * half, half), :]
            total = None
            for j in range(3):
                product = dot_wide(rows[:, j * local : (j + 1) * local], qkv_low_ref[j])
                total = product if total is None else total + product
            target[c * half : (c + 1) * half, :] = total


def input_norm_kernel(x_ref, norm_ref, mine_ref, theirs_ref, *refs, chunks):
    grad_hidden = refs[:chunks]
    rows_ref, sums_ref = refs[chunks:]
    half = mine_ref.shape[0] // chunks
    core = core_index()
    gains = offsets = None
    for c in range(chunks):
        rows = slice(c * half, (c + 1) * half)
        inputs = x_ref[pl.ds(c * 2 * half + core * half, half), :].astype(WIDE)
        stat, inverse = normalize(inputs)
        back, gain, offset = norm_back(
            mine_ref[rows, :] + theirs_ref[rows, :], stat, inverse, norm_ref[0:1, :]
        )
        rows_ref[rows, :] = grad_hidden[c][...] + back
        gains = gain if gains is None else gains + gain
        offsets = offset if offsets is None else offsets + offset
    sums_ref[0:1, :] = gains
    sums_ref[1:2, :] = offsets


def place_kernel(mine_ref, theirs_ref, out_ref, *, chunks):
    half = theirs_ref.shape[0] // chunks
    core = core_index()
    for c in range(chunks):
        rows = slice(c * half, (c + 1) * half)
        out_ref[pl.ds((2 * c + core) * half, half), :] = mine_ref[rows, :].astype(LOW)
        out_ref[pl.ds((2 * c + 1 - core) * half, half), :] = theirs_ref[rows, :].astype(LOW)


def moment_step(gradient, first_state, second_state):
    first_new = first_decay * first_state + (1.0 - first_decay) * gradient
    second_new = second_decay * second_state + (1.0 - second_decay) * gradient * gradient
    direction = (
        first_new
        / (1.0 - first_decay**STEP)
        / (jnp.sqrt(second_new / (1.0 - second_decay**STEP)) + adam_epsilon)
    )
    return (first_new, second_new, direction)


def total_of(values):
    rows = values.reshape(-1, values.shape[-1])
    return jnp.sum(jnp.sum(rows, axis=0, keepdims=True), axis=1, keepdims=True)


def moments_kernel(master_ref, first_ref, second_ref, squares_ref, *refs, row, regions, counts):
    update_ref, first_new_ref, second_new_ref, table_ref = refs[-4:]
    at = 0
    sizes = []
    for region, count in zip(regions, counts):
        gradient = refs[at][0]
        for term in refs[at + 1 : at + count]:
            gradient = gradient + term[0]
        at += count
        first_new, second_new, direction = moment_step(
            gradient, first_ref[region], second_ref[region]
        )
        first_new_ref[region] = first_new
        second_new_ref[region] = second_new
        master = master_ref[region]
        update = direction + decay_rate * master
        update_ref[region] = update
        sizes.append((total_of(master * master), total_of(update * update)))
    table_ref[...] = squares_ref[...]
    for place, size in ((row, 0), (row + 4, 1)):
        amount = sizes[0][size]
        for other in sizes[1:]:
            amount = amount + other[size]
        table_ref[place : place + 1, :] = jnp.broadcast_to(amount, (1, LANES))


def masters_kernel(squares_ref, *refs):
    masters, updates = refs[:4], refs[4:8]
    outs, norms_ref = refs[8:12], refs[12]
    sizes = jnp.sqrt(squares_ref[0:4, :])
    steps = jnp.sqrt(squares_ref[4:8, :] + trust_epsilon)
    norms_ref[0:4, :] = sizes
    norms_ref[4:8, :] = steps
    ratio = learn_rate * (sizes / steps)
    for index in range(4):
        scale = ratio[index : index + 1, 0:1]
        if len(masters[index].shape) == 3:
            scale = scale.reshape(1, 1, 1)
        outs[index][...] = masters[index][...] - scale * updates[index][...]


def shards(
    block_input,
    lengths,
    norm_params,
    qkv_weight,
    out_weight,
    up_weight,
    down_weight,
    qkv_first,
    qkv_second,
    out_first,
    out_second,
    up_first,
    up_second,
    down_first,
    down_second,
    norm_first,
    norm_second,
    out_grad,
):
    row_count, width = block_input.shape
    local = qkv_weight.shape[2]
    hidden_units = up_weight.shape[1]
    group_count = lax.axis_size("dp")
    group_rank = lax.axis_index("dp")
    own = width // group_count
    own_start = group_rank * own
    part = row_count // CHUNKS
    half = part // 2
    chunks = range(CHUNKS)
    bits = list(range(log2_of(group_count)))
    bits_across = [1, 0] + bits[2:] if len(bits) > 1 else bits

    qkv_parts = jnp.transpose(qkv_weight, (1, 0, 2))
    cosine, sine = rotary_tables(row_count)

    weight_shapes = [shaped(3, width, local, kind=LOW), shaped(local, width, kind=LOW)]
    chunk_shapes = [
        shaped(part, width, kind=LOW),
        shaped(part, local, kind=LOW),
        shaped(part, local, kind=LOW),
        shaped(part, local, kind=LOW),
        shaped(part, local, kind=LOW),
        shaped(part, LANES),
        shaped(half, width),
        shaped(half, width),
    ]
    chunk_flops = 2 * part * width * 4 * local + 8 * part * part * local
    parts = []
    for c in chunks:
        rows = slice(c * part, (c + 1) * part)
        common = [lengths, block_input, norm_params, cosine, sine]
        row_block = lambda array, c=c: pl.BlockSpec((part, array.shape[1]), lambda i, c=c: (c, 0))
        specs = [SMEM, row_block(block_input), VMEM, row_block(cosine), row_block(sine)]
        if c == 0:
            outs = call(
                first_kernel,
                weight_shapes + chunk_shapes,
                common + [qkv_parts, out_weight],
                specs + [ANY, ANY],
                flops=chunk_flops,
                scratch=[
                    pltpu.VMEM((3, width, local), WIDE),
                    pltpu.VMEM((local, width), WIDE),
                    pltpu.SemaphoreType.DMA((4,)),
                ],
                name="attention_first",
            )
            qkv_low, out_low = outs[:2]
            parts.append(outs[2:])
        else:
            before = [p[2] for p in parts] + [p[3] for p in parts]
            parts.append(
                call(
                    functools.partial(next_kernel, first_row=c * part),
                    chunk_shapes,
                    common + [qkv_low, out_low] + before,
                    specs + [VMEM] * (2 + len(before)),
                    flops=chunk_flops,
                    name="attention_next",
                )
            )
    normed_in, query, keys, values, attn, masses, sends, keeps = zip(*parts)
    up_low = after(up_weight, sends[-1]).astype(LOW)
    down_low = after(down_weight, sends[-1]).astype(LOW)
    branch_terms = [sum_rows(sends[c], keeps[c]) for c in chunks]

    mlp_flops = 4 * part * width * hidden_units
    branch, hidden, normed_mid, up, active, mlp_terms = [], [], [], [], [], []
    for c in chunks:
        outs = call(
            functools.partial(middle_kernel, c * part),
            [shaped(half, width)] * 3,
            [block_input, norm_params, *branch_terms[c]],
            name="middle",
        )
        branch.append(outs[0])
        hidden.append(outs[1])
        other = swap(outs[2], "tensor", 1)
        outs = call(
            mlp_kernel,
            [
                shaped(part, width, kind=LOW),
                shaped(part, hidden_units),
                shaped(part, hidden_units, kind=LOW),
                shaped(half, width),
                shaped(half, width),
            ],
            [outs[2], other, up_low, down_low],
            flops=mlp_flops,
            name="mlp",
        )
        normed_mid.append(outs[0])
        up.append(outs[1])
        active.append(outs[2])
        mlp_terms.append(sum_rows(outs[3], outs[4]))

    block_rows, loss_sums, grad_final, grad_mlp, grad_up_rows, mid_terms = [], [], [], [], [], []
    down_sends = None

    down_windows = cut_windows(hidden_units)
    up_windows = down_windows
    pieces_of = lambda windows: list(zip(windows, [bits, bits_across]))

    for c in chunks:
        outs = call(
            functools.partial(loss_kernel, c * part),
            [shaped(half, width), shaped(half, width), shaped(2, width)],
            [out_grad, norm_params, hidden[c], *mlp_terms[c]],
            name="loss",
        )
        block_rows.append(outs[0])
        loss_sums.append(outs[2])
        grad_final += [outs[1], swap(outs[1], "tensor", 1)]
        mine, other = grad_final[-2:]
        if c == CHUNKS - 1:
            down_sends = owner_products(
                owned_columns_kernel, active, grad_final, pieces_of(down_windows), own, True, "down_send"
            )
            mine = after(mine, *down_sends)
        outs = call(
            mlp_back_kernel,
            [
                shaped(part, width, kind=LOW),
                shaped(part, hidden_units, kind=LOW),
                shaped(half, width),
                shaped(half, width),
            ],
            [mine, other, up[c], up_low, down_low],
            flops=mlp_flops,
            name="mlp_back",
        )
        grad_mlp.append(outs[0])
        grad_up_rows.append(outs[1])
        mid_terms.append(sum_rows(outs[2], outs[3]))
    down_keeps = owner_products(
        owned_columns_kernel, active, grad_final, pieces_of(down_windows), own, False, "down_keep"
    )
    up_sends = owner_products(
        owned_rows_kernel, normed_mid, grad_up_rows, pieces_of(up_windows), own, True, "up_send"
    )
    up_keeps = owner_products(
        owned_rows_kernel, normed_mid, grad_up_rows, pieces_of(up_windows), own, False, "up_keep"
    )
    down_terms = [
        scatter_terms(s, k, piece[1])
        for s, k, piece in zip(down_sends, down_keeps, pieces_of(down_windows))
    ]
    up_terms = [
        scatter_terms(s, k, piece[1])
        for s, k, piece in zip(up_sends, up_keeps, pieces_of(up_windows))
    ]

    grad_hidden, norms_sums, own_back, other_back = [], [], [], []
    for c in chunks:
        outs = call(
            functools.partial(norms_back_kernel, c * part),
            [shaped(half, width), shaped(half, width), shaped(4, width)],
            [out_grad, norm_params, hidden[c], branch[c], *mid_terms[c]],
            name="norms_back",
        )
        grad_hidden.append(outs[0])
        norms_sums.append(outs[2])
        own_back.append(outs[1])
        other_back.append(swap(outs[1], "tensor", 1))
    grad_branch, grad_rows = call(
        functools.partial(attention_back_kernel, chunks=CHUNKS),
        [shaped(row_count, width, kind=LOW), shaped(row_count, 3 * local, kind=LOW)],
        [lengths, out_low, cosine, sine, *own_back, *other_back, *query, *keys, *values, *masses],
        [SMEM] + [VMEM] * (3 + 6 * CHUNKS),
        flops=2 * row_count * width * local + 10 * row_count * row_count * local,
        scratch=[pltpu.VMEM((row_count, local), WIDE), pltpu.VMEM((row_count, local), WIDE)],
        name="attention_back",
    )
    qkv_pieces = [((1, 3), bits), ((0, 1), bits_across)]
    out_pieces = [((0, local), bits)]
    qkv_sends = owner_products(
        owned_parts_kernel, normed_in, [grad_rows], qkv_pieces, own, True, "qkv_send"
    )
    out_sends = owner_products(
        owned_columns_kernel, attn, [grad_branch], out_pieces, own, True, "out_send"
    )
    qkv_keeps = owner_products(
        owned_parts_kernel, normed_in, [grad_rows], qkv_pieces, own, False, "qkv_keep"
    )
    out_keeps = owner_products(
        owned_columns_kernel, attn, [grad_branch], out_pieces, own, False, "out_keep"
    )
    qkv_terms = [
        scatter_terms(s, k, piece[1]) for s, k, piece in zip(qkv_sends, qkv_keeps, qkv_pieces)
    ]
    out_terms = [
        scatter_terms(s, k, piece[1]) for s, k, piece in zip(out_sends, out_keeps, out_pieces)
    ]

    send, keep = call(
        functools.partial(input_back_kernel, chunks=CHUNKS),
        [shaped(row_count // 2, width)] * 2,
        [grad_rows, qkv_low],
        flops=2 * row_count * width * 3 * local,
        name="input_back",
    )
    in_terms = sum_rows(send, keep)
    input_rows, input_sums = call(
        functools.partial(input_norm_kernel, chunks=CHUNKS),
        [shaped(row_count // 2, width), shaped(2, width)],
        [block_input, norm_params, *in_terms, *grad_hidden],
        name="input_norm",
    )

    def place(mine, name):
        stacked = mine[0] if len(mine) == 1 else jnp.concatenate(mine, axis=0)
        theirs = swap(stacked, "tensor", 1)
        return call(
            functools.partial(place_kernel, chunks=CHUNKS),
            [shaped(row_count, width, kind=LOW)],
            [stacked, theirs],
            name=name,
        )[0]

    block_output = place(block_rows, "place_output")
    input_grad = place([input_rows], "place_input")

    def total(arrays):
        result = arrays[0]
        for array in arrays[1:]:
            result = result + array
        return result

    grad_norms = jnp.concatenate([input_sums, total(norms_sums), total(loss_sums)], axis=0)
    grad_norms = grad_norms + swap(grad_norms, "tensor", 1)
    norm_chunks = jnp.stack(
        [
            lax.dynamic_slice_in_dim(grad_norms, (group_rank ^ distance) * own, own, 1)
            for distance in chunk_order(group_count, bits)
        ]
    )
    middle = group_count // 2
    norm_gradient = total(
        [term[0] for term in scatter_terms(norm_chunks[middle:], norm_chunks[:middle], bits)]
    )
    norm_own = lax.dynamic_slice_in_dim(norm_params, own_start, own, 1)
    norm_first_new, norm_second_new, norm_direction = moment_step(
        norm_gradient, norm_first, norm_second
    )
    norm_new = norm_own - learn_rate * norm_direction

    masters = [
        jnp.transpose(lax.dynamic_slice_in_dim(qkv_weight, own_start, own, 0), (1, 0, 2)),
        lax.dynamic_slice_in_dim(out_weight, own_start, own, 1),
        lax.dynamic_slice_in_dim(up_weight, own_start, own, 0),
        lax.dynamic_slice_in_dim(down_weight, own_start, own, 1),
    ]
    states = [
        (jnp.transpose(qkv_first, (1, 0, 2)), jnp.transpose(qkv_second, (1, 0, 2))),
        (out_first, out_second),
        (up_first, up_second),
        (down_first, down_second),
    ]
    everything = slice(None)
    regions = [
        [(slice(*w), everything, everything) for w, _ in qkv_pieces],
        [(slice(*w), everything) for w, _ in out_pieces],
        [(everything, slice(*w)) for w in up_windows],
        [(slice(*w), everything) for w in down_windows],
    ]
    table = jnp.zeros((8, LANES), WIDE)
    stepped = [None] * 4
    for index, terms in ((3, down_terms), (2, up_terms), (1, out_terms), (0, qkv_terms)):
        flat = [term for piece in terms for term in piece]
        counts = [len(piece) for piece in terms]
        shape = masters[index].shape
        outs = call(
            functools.partial(moments_kernel, row=index, regions=regions[index], counts=counts),
            [shaped(*shape)] * 3 + [shaped(8, LANES)],
            [masters[index], *states[index], table, *flat],
            [VMEM] * 4 + [first_block(term) for term in flat],
            name="moments_" + ("qkv", "out", "up", "down")[index],
        )
        stepped[index] = outs[:3]
        table = outs[3]
    squares = sum_all(sum_all(table, "tensor"), "dp")
    outs = call(
        masters_kernel,
        [shaped(*master.shape) for master in masters] + [shaped(8, LANES)],
        [squares, *masters, *[entry[0] for entry in stepped]],
        name="masters",
    )
    back = lambda array: jnp.transpose(array, (1, 0, 2))
    matrix_norms = jnp.stack([outs[4][0:4, 0], outs[4][4:8, 0]])
    return (
        block_output,
        input_grad,
        back(outs[0]),
        back(stepped[0][1]),
        back(stepped[0][2]),
        outs[1],
        stepped[1][1],
        stepped[1][2],
        outs[2],
        stepped[2][1],
        stepped[2][2],
        outs[3],
        stepped[3][1],
        stepped[3][2],
        norm_new,
        norm_first_new,
        norm_second_new,
        matrix_norms,
    )


def solution(mesh):
    in_specs = (
        P("dp", None),
        P("dp"),
        P(),
        P(None, None, "tensor"),
        P("tensor", None),
        P(None, "tensor"),
        P("tensor", None),
        P("dp", None, "tensor"),
        P("dp", None, "tensor"),
        P("tensor", "dp"),
        P("tensor", "dp"),
        P("dp", "tensor"),
        P("dp", "tensor"),
        P("tensor", "dp"),
        P("tensor", "dp"),
        P(None, "dp"),
        P(None, "dp"),
        P("dp", None),
    )
    out_specs = (
        P("dp", None),
        P("dp", None),
        P("dp", None, "tensor"),
        P("dp", None, "tensor"),
        P("dp", None, "tensor"),
        P("tensor", "dp"),
        P("tensor", "dp"),
        P("tensor", "dp"),
        P("dp", "tensor"),
        P("dp", "tensor"),
        P("dp", "tensor"),
        P("tensor", "dp"),
        P("tensor", "dp"),
        P("tensor", "dp"),
        P(None, "dp"),
        P(None, "dp"),
        P(None, "dp"),
        P(),
    )
    return jax.shard_map(shards, mesh=mesh, in_specs=in_specs, out_specs=out_specs, check_vma=False)
```

```python
import functools

import jax
import jax.numpy as jnp
import numpy as np
from jax import lax
from jax.experimental import pallas as pl
from jax.experimental.pallas import tpu as pltpu
from jax.sharding import PartitionSpec as P

HEAD_DIM = 64
STEP = 10
CHUNKS = 2
LANES = 128

norm_epsilon = 1e-05
rotary_base = 10000.0
mask_fill = -1000000000.0
first_decay = 0.9
second_decay = 0.999
adam_epsilon = 1e-06
trust_epsilon = 1e-06
decay_rate = 0.01
learn_rate = 0.25

LOW = jnp.bfloat16
WIDE = jnp.float32
VMEM = pl.BlockSpec(memory_space=pltpu.VMEM)
SMEM = pl.BlockSpec(memory_space=pltpu.SMEM)
HBM = pl.BlockSpec(memory_space=pltpu.HBM)


def log2_of(count):
    bits = 0
    while (1 << bits) < count:
        bits += 1
    return bits


def swap(values, axis, distance):
    count = lax.axis_size(axis)
    return lax.ppermute(values, axis, [(i, i ^ distance) for i in range(count)])


def chunk_order(count, bits):
    order = [0]
    for bit in reversed(bits):
        order = order + [distance ^ (1 << bit) for distance in order]
    return order


def normalize(values):
    center = values - jnp.mean(values, axis=-1, keepdims=True)
    inverse = lax.rsqrt(jnp.mean(center * center, axis=-1, keepdims=True) + norm_epsilon)
    return center * inverse, inverse


def norm_back(incoming, normed, inverse, gain):
    scaled = incoming * gain
    inner = (
        scaled
        - jnp.mean(scaled, axis=-1, keepdims=True)
        - normed * jnp.mean(scaled * normed, axis=-1, keepdims=True)
    )
    gain_grad = jnp.sum(incoming * normed, axis=0, keepdims=True)
    return inner * inverse, gain_grad, jnp.sum(incoming, axis=0, keepdims=True)


def rotary_tables(length):
    half = HEAD_DIM // 2
    lane = np.arange(LANES)
    frequency = (rotary_base ** (-((lane % half).astype(np.float32) * 2.0 / HEAD_DIM))).astype(np.float32)
    angles = np.arange(length, dtype=np.float32)[:, None] * frequency[None, :]
    sign = np.where(lane % HEAD_DIM < half, -1.0, 1.0)
    cosine = np.cos(angles.astype(np.float64)).astype(np.float32)
    sine = (np.sin(angles.astype(np.float64)) * sign[None, :]).astype(np.float32)
    return jnp.asarray(cosine), jnp.asarray(sine)


def turn(values, cosine, sine):
    half = HEAD_DIM // 2
    lane = lax.broadcasted_iota(jnp.int32, (1, LANES), 1)
    first = lax.rem(lane, HEAD_DIM) < half
    tiles = []
    for start in range(0, values.shape[1], LANES):
        tile = values[:, start : start + LANES]
        other = jnp.where(
            first, pltpu.roll(tile, LANES - half, 1), pltpu.roll(tile, half, 1)
        )
        tiles.append(tile * cosine + other * sine)
    return tiles[0] if len(tiles) == 1 else jnp.concatenate(tiles, axis=1)


def gelu_mass(up):
    return 0.5 * (1.0 + lax.erf(up * (0.5**0.5)))


def dot(left, right):
    return jnp.dot(left, right, preferred_element_type=WIDE)


def dot_rows(left, right):
    return lax.dot_general(left, right, (((0,), (0,)), ((), ())), preferred_element_type=WIDE)


def dot_wide(left, right):
    return lax.dot_general(left, right, (((1,), (1,)), ((), ())), preferred_element_type=WIDE)


def of_head(values, head):
    lane = lax.broadcasted_iota(jnp.int32, (1, values.shape[1]), 1)
    mine = (lane >= head * HEAD_DIM) & (lane < (head + 1) * HEAD_DIM)
    return jnp.where(mine, values, jnp.zeros_like(values))


def core_index():
    return lax.rem(lax.axis_index("tensor"), 2)


def shaped(*shape, kind=WIDE):
    return jax.ShapeDtypeStruct(shape, kind)


def cut(rows, width, count=4):
    return [shaped(rows // count, width)] * count


def near(values):
    return [swap(piece, "tensor", 1) for piece in values]


class Take:
    def __init__(self, array, shape=None, index=None):
        self.array = array
        self.shape = array.shape if shape is None else shape
        self.index = index


class Raw:
    def __init__(self, array, spec):
        self.array = array
        self.spec = spec


class Rows:
    def __init__(self, refs):
        self.refs = refs
        self.step = refs[0].shape[0]
        self.shape = (self.step * len(refs), refs[0].shape[1])

    def spans(self, key):
        first, last = 0, self.shape[0]
        if key is not Ellipsis and key[0] != slice(None):
            first, last = key[0].start, key[0].stop
        for place, ref in enumerate(self.refs):
            start, stop = max(first, place * self.step), min(last, (place + 1) * self.step)
            if start < stop:
                inside = slice(start - place * self.step, stop - place * self.step)
                yield ref, inside, slice(start - first, stop - first)

    def __getitem__(self, key):
        pieces = [ref[inside, :] for ref, inside, _ in self.spans(key)]
        return pieces[0] if len(pieces) == 1 else jnp.concatenate(pieces, axis=0)

    def __setitem__(self, key, value):
        for ref, inside, outside in self.spans(key):
            ref[inside, :] = value[outside]


class Line:
    def __init__(self):
        self.token = jnp.zeros((8, LANES), WIDE)

    def call(self, kernel, outs, args, scratch=(), megabytes=12, name=None):
        arrays, specs, buffers, layout, takes = [], [], [], [], []
        for arg in args:
            if isinstance(arg, Take):
                layout.append(0)
                takes.append((len(arrays), arg))
                arrays.append(arg.array)
                specs.append(HBM)
                buffers.append(pltpu.VMEM(arg.shape, arg.array.dtype))
            elif isinstance(arg, Raw):
                layout.append(0)
                arrays.append(arg.array)
                specs.append(arg.spec)
            elif isinstance(arg, (list, tuple)):
                layout.append(len(arg))
                arrays += arg
                specs += [VMEM] * len(arg)
            else:
                layout.append(0)
                arrays.append(arg)
                specs.append(VMEM)
        if takes:
            buffers.append(pltpu.SemaphoreType.DMA((len(takes),)))
        out_layout = [len(out) if isinstance(out, list) else 0 for out in outs]
        out_shapes = [o for out in outs for o in (out if isinstance(out, list) else [out])]

        def joined(refs, layout):
            refs = list(refs)
            return [
                Rows([refs.pop(0) for _ in range(count)]) if count else refs.pop(0)
                for count in layout
            ]

        def body(*refs):
            inputs = list(refs[: len(arrays)])
            rest = refs[len(arrays) + 1 :]
            results, rest = rest[: len(out_shapes)], rest[len(out_shapes) + 1 :]
            own, rest = rest[: len(scratch)], rest[len(scratch) :]
            copies = []
            for place, (i, take) in enumerate(takes):
                source = inputs[i]
                if take.index is not None:
                    source = source.at[take.index()]
                copies.append(pltpu.make_async_copy(source, rest[place], rest[-1].at[place]))
                inputs[i] = rest[place]
            for copy in copies:
                copy.start()
            for copy in copies:
                copy.wait()
            kernel(*joined(inputs, layout), *joined(results, out_layout), *own)

        results = pl.pallas_call(
            body,
            out_shape=(*out_shapes, shaped(8, LANES)),
            in_specs=[*specs, HBM],
            out_specs=tuple([VMEM] * len(out_shapes) + [HBM]),
            scratch_shapes=[*scratch, *buffers],
            input_output_aliases={len(arrays): len(out_shapes)},
            compiler_params=pltpu.CompilerParams(vmem_limit_bytes=megabytes * 1024 * 1024),
            cost_estimate=pl.CostEstimate(flops=0, bytes_accessed=0, transcendentals=0),
            name=name,
        )(*arrays, self.token)
        self.token = results[-1]
        found = list(results[:-1])
        return [
            [found.pop(0) for _ in range(count)] if count else found.pop(0) for count in out_layout
        ]


def sum_kernel(*refs):
    total = refs[0][...]
    for ref in refs[1:-1]:
        total = total + ref[...]
    refs[-1][...] = total


def pairs_kernel(*refs):
    terms = [ref[...] for ref in refs[:-1]]
    while len(terms) > 1:
        terms = [terms[i] + terms[i + 1] for i in range(0, len(terms), 2)]
    refs[-1][...] = terms[0]


def add_rows(line, terms, name):
    return line.call(sum_kernel, [shaped(*terms[0].shape)], terms, name=name)[0]


def sum_rows(line, keep, arrived, name):
    mine, theirs = keep, arrived
    for bit in range(1, log2_of(lax.axis_size("tensor"))):
        mine = add_rows(line, [mine, theirs], name)
        theirs = swap(mine, "tensor", 1 << bit)
    return mine, theirs


def sum_all(line, values, axis, name, most=2):
    bits = log2_of(lax.axis_size(axis))
    for start in range(0, bits, most):
        taken = min(most, bits - start)
        terms = [values] + [
            swap(values, axis, distance << start) for distance in range(1, 1 << taken)
        ]
        values = line.call(pairs_kernel, [shaped(*values.shape)], terms, name=name)[0]
    return values


class Piece:
    def __init__(self, name, window, bits):
        self.name, self.window, self.bits = name, window, bits
        self.terms, self.stage = [], 0

    def start(self, send):
        self.terms = [swap(send, "dp", 1 << self.bits[0])]
        self.stage = 1

    def hold(self, keep):
        self.terms.insert(0, keep)
        self.size = keep.shape[0]

    def advance(self, line):
        self.size //= 2
        shape = (self.size,) + self.terms[0].shape[1:]
        index = lambda size=self.size: (pl.ds(size, size),)
        outgoing = line.call(
            sum_kernel,
            [shaped(*shape)],
            [Take(term, shape, index) for term in self.terms],
            name="sum_" + self.name,
        )[0]
        self.terms.append(swap(outgoing, "dp", 1 << self.bits[self.stage]))
        self.stage += 1


def project(normed, weights, cosine, sine):
    query = turn(dot(normed, weights[0]), cosine, sine).astype(LOW)
    keys = turn(dot(normed, weights[1]), cosine, sine).astype(LOW)
    return query, keys, dot(normed, weights[2]).astype(LOW)


def attend(query, keys, values, first_row, live_len):
    rows, reach = query.shape[0], keys.shape[0]
    row = first_row + lax.broadcasted_iota(jnp.int32, (rows, reach), 0)
    column = lax.broadcasted_iota(jnp.int32, (rows, reach), 1)
    visible = (column <= row) & (column < live_len)
    lane = lax.broadcasted_iota(jnp.int32, (1, LANES), 1)
    mixed = jnp.zeros((rows, query.shape[1]), WIDE)
    masses = jnp.zeros((rows, LANES), WIDE)
    for head in range(query.shape[1] // HEAD_DIM):
        scores = dot_wide(of_head(query, head), keys) * HEAD_DIM ** (-0.5)
        scores = jnp.where(visible, scores, mask_fill)
        top = jnp.max(scores, axis=-1, keepdims=True)
        expo = jnp.exp(scores - top)
        total = jnp.sum(expo, axis=-1, keepdims=True)
        probs = (expo * (1.0 / total)).astype(LOW)
        mixed = mixed + dot(probs, of_head(values, head))
        masses = jnp.where(lane == head, top + jnp.log(total), masses)
    live = first_row + lax.broadcasted_iota(jnp.int32, (rows, 1), 0) < live_len
    return jnp.where(live, mixed, 0.0).astype(LOW), masses


def split_rows(left_ref, right, send_ref, keep_ref, how):
    half = send_ref.shape[0]
    core = core_index()
    send_ref[...] = how(left_ref[pl.ds((1 - core) * half, half), :], right)
    keep_ref[...] = how(left_ref[pl.ds(core * half, half), :], right)


def first_kernel(
    live_ref, x_any, norm_any, cos_any, sin_any, qkv_any, out_any,
    qkv_low_ref, out_low_ref, normed_ref, q_ref, k_ref, v_ref, attn_ref, mass_ref, send_ref, keep_ref,
    x_ref, norm_ref, cos_ref, sin_ref, qkv_in, out_in, arrived,
):
    part = x_ref.shape[0]
    sources = [x_any.at[pl.ds(0, part)], norm_any, cos_any.at[pl.ds(0, part)], sin_any.at[pl.ds(0, part)]]
    targets = [x_ref, norm_ref, cos_ref, sin_ref]
    sources += [qkv_any.at[j] for j in range(3)] + [out_any]
    targets += [qkv_in.at[j] for j in range(3)] + [out_in]
    copies = [
        pltpu.make_async_copy(source, target, arrived.at[i])
        for i, (source, target) in enumerate(zip(sources, targets))
    ]
    for copy in copies:
        copy.start()
    copies[0].wait()
    copies[1].wait()
    stat, _ = normalize(x_ref[...].astype(WIDE))
    normed = (stat * norm_ref[0:1, :] + norm_ref[1:2, :]).astype(LOW)
    normed_ref[...] = normed
    copies[2].wait()
    copies[3].wait()
    weights = []
    for j in range(3):
        copies[4 + j].wait()
        weights.append(qkv_in[j].astype(LOW))
        qkv_low_ref[j] = weights[j]
    query, keys, values = project(normed, weights, cos_ref[...], sin_ref[...])
    q_ref[...], k_ref[...], v_ref[...] = query, keys, values
    attn_ref[...], mass_ref[...] = attend(query, keys, values, 0, live_ref[0])
    copies[7].wait()
    out_low = out_in[...].astype(LOW)
    out_low_ref[...] = out_low
    split_rows(attn_ref, out_low, send_ref, keep_ref, dot)


def next_kernel(
    live_ref, x_ref, norm_ref, cos_ref, sin_ref, qkv_low_ref, out_low_ref, *refs, first_row, part
):
    earlier = first_row // part
    rows = slice(first_row, first_row + part)
    k_before, v_before = refs[:earlier], refs[earlier : 2 * earlier]
    normed_ref, q_ref, k_ref, v_ref, attn_ref, mass_ref, send_ref, keep_ref = refs[2 * earlier :]
    stat, _ = normalize(x_ref[rows, :].astype(WIDE))
    normed = (stat * norm_ref[0:1, :] + norm_ref[1:2, :]).astype(LOW)
    normed_ref[...] = normed
    weights = [qkv_low_ref[j] for j in range(3)]
    query, keys, values = project(normed, weights, cos_ref[rows, :], sin_ref[rows, :])
    q_ref[...], k_ref[...], v_ref[...] = query, keys, values
    keys = jnp.concatenate([ref[...] for ref in k_before] + [keys], axis=0)
    values = jnp.concatenate([ref[...] for ref in v_before] + [values], axis=0)
    attn_ref[...], mass_ref[...] = attend(query, keys, values, first_row, live_ref[0])
    split_rows(attn_ref, out_low_ref[...], send_ref, keep_ref, dot)


def cast_kernel(wide_ref, low_ref):
    low_ref[...] = wide_ref[...].astype(LOW)


def middle_kernel(first_row, x_ref, norm_ref, mine_ref, theirs_ref, branch_ref, hidden_ref, normed_ref):
    half = mine_ref.shape[0]
    branch = mine_ref[...] + theirs_ref[...]
    branch_ref[...] = branch
    stat, _ = normalize(branch)
    inputs = x_ref[pl.ds(first_row + core_index() * half, half), :].astype(WIDE)
    hidden = inputs + stat * norm_ref[2:3, :] + norm_ref[3:4, :]
    hidden_ref[...] = hidden
    stat, _ = normalize(hidden)
    normed_ref[...] = stat * norm_ref[4:5, :] + norm_ref[5:6, :]


def mlp_kernel(own_ref, other_ref, up_w_ref, down_w_ref, normed_ref, up_ref, active_ref, send_ref, keep_ref):
    half = own_ref.shape[0]
    normed = jnp.concatenate([own_ref[...].astype(LOW), other_ref[...].astype(LOW)], axis=0)
    normed_ref[...] = normed
    step = min(256, up_w_ref.shape[1])
    total = None
    for start in range(0, up_w_ref.shape[1], step):
        block = slice(start, start + step)
        up = dot(normed, up_w_ref[:, block])
        up_ref[:, block] = up
        active = (up * gelu_mass(up)).astype(LOW)
        active_ref[:, block] = active
        product = dot(active, down_w_ref[block, :])
        total = product if total is None else total + product
    keep_ref[...] = total[:half]
    send_ref[...] = total[half:]


def loss_kernel(
    first_row, grad_ref, norm_ref, hidden_ref, mine_ref, theirs_ref, block_ref, back_ref, sums_ref
):
    half = mine_ref.shape[0]
    stat, inverse = normalize(mine_ref[...] + theirs_ref[...])
    block_ref[...] = hidden_ref[...] + stat * norm_ref[6:7, :] + norm_ref[7:8, :]
    incoming = grad_ref[pl.ds(first_row + core_index() * half, half), :].astype(WIDE)
    back, gain, offset = norm_back(incoming, stat, inverse, norm_ref[6:7, :])
    back_ref[...] = back
    sums_ref[0:1, :] = gain
    sums_ref[1:2, :] = offset


def mlp_back_kernel(
    own_ref, other_ref, up_ref, up_w_ref, down_w_ref, grad_mlp_ref, grad_up_ref, send_ref, keep_ref
):
    half = own_ref.shape[0]
    grad_mlp = jnp.concatenate([own_ref[...].astype(LOW), other_ref[...].astype(LOW)], axis=0)
    grad_mlp_ref[...] = grad_mlp
    step = min(256, up_w_ref.shape[1])
    total = None
    for start in range(0, up_w_ref.shape[1], step):
        block = slice(start, start + step)
        up = up_ref[:, block]
        slope = gelu_mass(up) + up * jnp.exp(-0.5 * up * up) * float((2.0 * np.pi) ** -0.5)
        grad_up = (dot_wide(grad_mlp, down_w_ref[block, :]) * slope).astype(LOW)
        grad_up_ref[:, block] = grad_up
        product = dot_wide(grad_up, up_w_ref[:, block])
        total = product if total is None else total + product
    keep_ref[...] = total[:half]
    send_ref[...] = total[half:]


def norms_back_kernel(
    first_row, grad_ref, norm_ref, hidden_ref, branch_ref, mine_ref, theirs_ref,
    grad_hidden_ref, back_ref, sums_ref,
):
    half = mine_ref.shape[0]
    stat, inverse = normalize(hidden_ref[...])
    back, gain, offset = norm_back(
        mine_ref[...] + theirs_ref[...], stat, inverse, norm_ref[4:5, :]
    )
    incoming = grad_ref[pl.ds(first_row + core_index() * half, half), :].astype(WIDE)
    grad_hidden = incoming + back
    grad_hidden_ref[...] = grad_hidden
    sums_ref[2:3, :] = gain
    sums_ref[3:4, :] = offset
    stat, inverse = normalize(branch_ref[...])
    back, gain, offset = norm_back(grad_hidden, stat, inverse, norm_ref[2:3, :])
    back_ref[...] = back
    sums_ref[0:1, :] = gain
    sums_ref[1:2, :] = offset


def attention_back_kernel(live_ref, out_low_ref, cos_ref, sin_ref, *refs, chunks):
    groups = [refs[i * chunks : (i + 1) * chunks] for i in range(6)]
    own, other, query_refs, key_refs, value_refs, mass_refs = groups
    grad_branch_ref, rows_ref = refs[6 * chunks : 6 * chunks + 2]
    keys_sum, values_sum = refs[6 * chunks + 2 :]
    half = own[0].shape[0]
    part = 2 * half
    core = core_index()
    live_len = live_ref[0]
    local = rows_ref.shape[1] // 3
    heads = local // HEAD_DIM
    for c in range(chunks):
        grad_branch_ref[pl.ds(c * part + core * half, half), :] = own[c][...].astype(LOW)
        grad_branch_ref[pl.ds(c * part + (1 - core) * half, half), :] = other[c][...].astype(LOW)
    keys_all = jnp.concatenate([ref[...] for ref in key_refs], axis=0)
    values_all = jnp.concatenate([ref[...] for ref in value_refs], axis=0)
    for c in range(chunks):
        reach = (c + 1) * part
        first_row = c * part
        row = first_row + lax.broadcasted_iota(jnp.int32, (part, reach), 0)
        column = lax.broadcasted_iota(jnp.int32, (part, reach), 1)
        visible = (column <= row) & (column < live_len)
        live = first_row + lax.broadcasted_iota(jnp.int32, (part, 1), 0) < live_len
        grad_attn = dot_wide(grad_branch_ref[first_row : first_row + part, :], out_low_ref[...])
        grad_mixed = jnp.where(live, grad_attn, 0.0).astype(LOW)
        query, masses = query_refs[c][...], mass_refs[c][...]
        keys, values = keys_all[:reach], values_all[:reach]
        grad_query = jnp.zeros((part, local), WIDE)
        grad_keys = jnp.zeros((reach, local), WIDE)
        grad_values = jnp.zeros((reach, local), WIDE)
        for head in range(heads):
            query_h, grad_h = of_head(query, head), of_head(grad_mixed, head)
            scores = dot_wide(query_h, keys) * HEAD_DIM ** (-0.5)
            scores = jnp.where(visible, scores, mask_fill)
            probs = jnp.exp(scores - masses[:, head : head + 1])
            grad_values = grad_values + dot_rows(probs.astype(LOW), grad_h)
            grad_probs = dot_wide(grad_h, values)
            inner = jnp.sum(grad_probs * probs, axis=-1, keepdims=True)
            grad_scores = (probs * (grad_probs - inner)).astype(LOW)
            grad_query = grad_query + dot(grad_scores, of_head(keys, head))
            grad_keys = grad_keys + dot_rows(grad_scores, query_h)
        cosine = cos_ref[first_row : first_row + part, :]
        sine = sin_ref[first_row : first_row + part, :]
        grad_query = turn(grad_query * HEAD_DIM ** (-0.5), cosine, -sine)
        rows_ref[first_row : first_row + part, 0:local] = grad_query.astype(LOW)
        if c == 0:
            keys_sum[0:reach, :] = grad_keys
            values_sum[0:reach, :] = grad_values
        else:
            keys_sum[0:first_row, :] += grad_keys[:first_row]
            keys_sum[first_row:reach, :] = grad_keys[first_row:]
            values_sum[0:first_row, :] += grad_values[:first_row]
            values_sum[first_row:reach, :] = grad_values[first_row:]
    grad_keys = turn(keys_sum[...] * HEAD_DIM ** (-0.5), cos_ref[...], -sin_ref[...])
    rows_ref[:, local : 2 * local] = grad_keys.astype(LOW)
    rows_ref[:, 2 * local : 3 * local] = values_sum[...].astype(LOW)


def picked_columns(refs, distances, own):
    rank = lax.axis_index("dp")
    blocks = []
    for distance in distances:
        start = pl.multiple_of(lax.bitwise_xor(rank, distance) * own, own)
        pieces = [ref[:, pl.ds(start, own)].astype(LOW) for ref in refs]
        blocks.append(pieces[0] if len(pieces) == 1 else jnp.concatenate(pieces, axis=0))
    return blocks[0] if len(blocks) == 1 else jnp.concatenate(blocks, axis=1)


def whole_rows(refs, window):
    pieces = [ref[:, window[0] : window[1]].astype(LOW) for ref in refs]
    return pieces[0] if len(pieces) == 1 else jnp.concatenate(pieces, axis=0)


def owned_columns_kernel(*refs, pairs, jobs, own):
    (lefts, rights), outs = pairs, refs[sum(pairs) :]
    left, right = refs[:lefts], refs[lefts : lefts + rights]
    for (distances, window), out_ref in zip(jobs, outs):
        rows = whole_rows(left, window)
        product = dot_rows(rows, picked_columns(right, distances, own))
        for place in range(len(distances)):
            out_ref[place] = product[:, place * own : (place + 1) * own]


def owned_rows_kernel(*refs, pairs, jobs, own):
    (lefts, rights), outs = pairs, refs[sum(pairs) :]
    left, right = refs[:lefts], refs[lefts : lefts + rights]
    for (distances, window), out_ref in zip(jobs, outs):
        product = dot_rows(picked_columns(left, distances, own), whole_rows(right, window))
        for place in range(len(distances)):
            out_ref[place] = product[place * own : (place + 1) * own, :]


def owned_parts_kernel(*refs, pairs, jobs, own):
    (lefts, rights), outs = pairs, refs[sum(pairs) :]
    left, right = refs[:lefts], refs[lefts : lefts + rights]
    for (distances, window), out_ref in zip(jobs, outs):
        local = out_ref.shape[3]
        columns = (window[0] * local, window[1] * local)
        product = dot_rows(picked_columns(left, distances, own), whole_rows(right, columns))
        for place in range(len(distances)):
            for j in range(window[1] - window[0]):
                out_ref[place, j] = product[
                    place * own : (place + 1) * own, j * local : (j + 1) * local
                ]


def rounded_kernel(*refs):
    refs[-1][...] = whole_rows(refs[:-1], (0, refs[0].shape[1]))


def narrow_products(line, kernel, left, right, jobs, outs, own):
    rank = lax.axis_index("dp")
    joined = []
    for arrays in (left, right):
        rows = sum(array.shape[0] for array in arrays)
        low = shaped(rows, arrays[0].shape[1], kind=LOW)
        joined.append(line.call(rounded_kernel, [low], arrays, name="rounded")[0])
    results = []
    for (distances, window), out in zip(jobs, outs):
        pick = lambda array: jnp.concatenate(
            [lax.dynamic_slice_in_dim(array, (rank ^ d) * own, own, 1) for d in distances], axis=1
        )
        if kernel is owned_columns_kernel:
            product = dot_rows(joined[0][:, window[0] : window[1]], pick(joined[1]))
            product = product.reshape(-1, len(distances), own).transpose(1, 0, 2)
        elif kernel is owned_rows_kernel:
            product = dot_rows(pick(joined[0]), joined[1][:, window[0] : window[1]])
            product = product.reshape(out.shape)
        else:
            local = out.shape[3]
            columns = joined[1][:, window[0] * local : window[1] * local]
            product = dot_rows(pick(joined[0]), columns)
            product = product.reshape(len(distances), own, -1, local).transpose(0, 2, 1, 3)
        results.append(product)
    return results


def owner_products(line, kernel, left, right, pieces, own, send, name):
    count = lax.axis_size("dp")
    jobs, outs = [], []
    for piece in pieces:
        order = chunk_order(count, piece.bits)
        order = order[count // 2 :] if send else order[: count // 2]
        jobs.append((order, piece.window))
        size = piece.window[1] - piece.window[0]
        if kernel is owned_columns_kernel:
            outs.append(shaped(len(order), size, own))
        elif kernel is owned_rows_kernel:
            outs.append(shaped(len(order), own, size))
        else:
            outs.append(shaped(len(order), size, own, right[0].shape[1] // 3))
    if own % LANES:
        return narrow_products(line, kernel, left, right, jobs, outs, own)
    return line.call(
        functools.partial(kernel, pairs=(len(left), len(right)), jobs=jobs, own=own),
        outs,
        [*left, *right],
        megabytes=20,
        name=name,
    )


def input_back_kernel(rows_ref, qkv_low_ref, send_ref, keep_ref, *, chunks):
    half = send_ref.shape[0] // chunks
    local = qkv_low_ref.shape[2]
    core = core_index()
    for c in range(chunks):
        for target, which in ((send_ref, 1 - core), (keep_ref, core)):
            rows = rows_ref[pl.ds(c * 2 * half + which * half, half), :]
            total = None
            for j in range(3):
                product = dot_wide(rows[:, j * local : (j + 1) * local], qkv_low_ref[j])
                total = product if total is None else total + product
            target[c * half : (c + 1) * half, :] = total


def input_norm_kernel(x_ref, norm_ref, mine_ref, theirs_ref, *refs, chunks):
    grad_hidden = refs[:chunks]
    rows_ref, sums_ref = refs[chunks:]
    half = mine_ref.shape[0] // chunks
    core = core_index()
    gains = offsets = None
    for c in range(chunks):
        rows = slice(c * half, (c + 1) * half)
        inputs = x_ref[pl.ds(c * 2 * half + core * half, half), :].astype(WIDE)
        stat, inverse = normalize(inputs)
        back, gain, offset = norm_back(
            mine_ref[rows, :] + theirs_ref[rows, :], stat, inverse, norm_ref[0:1, :]
        )
        rows_ref[rows, :] = grad_hidden[c][...] + back
        gains = gain if gains is None else gains + gain
        offsets = offset if offsets is None else offsets + offset
    sums_ref[0:1, :] = gains
    sums_ref[1:2, :] = offsets


def place_kernel(mine_ref, theirs_ref, out_ref, *, chunks):
    half = mine_ref.shape[0] // chunks
    core = core_index()
    for c in range(chunks):
        rows = slice(c * half, (c + 1) * half)
        out_ref[pl.ds((2 * c + core) * half, half), :] = mine_ref[rows, :].astype(LOW)
        out_ref[pl.ds((2 * c + 1 - core) * half, half), :] = theirs_ref[rows, :].astype(LOW)


def norm_sums_kernel(*refs, chunks):
    input_ref, norms, losses, out_ref = refs[0], refs[1 : 1 + chunks], refs[1 + chunks : -1], refs[-1]
    out_ref[0:2, :] = input_ref[...]
    out_ref[2:6, :] = sum(ref[...] for ref in norms[1:]) + norms[0][...]
    out_ref[6:8, :] = sum(ref[...] for ref in losses[1:]) + losses[0][...]


def norm_step_kernel(
    norm_ref, grad_ref, first_ref, second_ref, norm_new_ref, first_new_ref, second_new_ref
):
    first_new, second_new, direction = moment_step(grad_ref[...], first_ref[...], second_ref[...])
    first_new_ref[...] = first_new
    second_new_ref[...] = second_new
    norm_new_ref[...] = norm_ref[...] - learn_rate * direction


def moment_step(gradient, first_state, second_state):
    first_new = first_decay * first_state + (1.0 - first_decay) * gradient
    second_new = second_decay * second_state + (1.0 - second_decay) * gradient * gradient
    direction = (
        first_new
        / (1.0 - first_decay**STEP)
        / (jnp.sqrt(second_new / (1.0 - second_decay**STEP)) + adam_epsilon)
    )
    return (first_new, second_new, direction)


def total_of(values):
    rows = values.reshape(-1, values.shape[-1])
    return jnp.sum(jnp.sum(rows, axis=0, keepdims=True), axis=1, keepdims=True)


def moments_kernel(master_ref, first_ref, second_ref, squares_ref, *refs, row, regions, counts):
    kept_ref, update_ref, first_new_ref, second_new_ref, table_ref = refs[-5:]
    at = 0
    sizes = []
    for region, count in zip(regions, counts):
        gradient = refs[at][...]
        for term in refs[at + 1 : at + count]:
            gradient = gradient + term[...]
        at += count
        first_new, second_new, direction = moment_step(
            gradient, first_ref[region], second_ref[region]
        )
        first_new_ref[region] = first_new
        second_new_ref[region] = second_new
        master = master_ref[region]
        kept_ref[region] = master
        update = direction + decay_rate * master
        update_ref[region] = update
        sizes.append((total_of(master * master), total_of(update * update)))
    table_ref[...] = squares_ref[...]
    for place, size in ((row, 0), (row + 4, 1)):
        amount = sizes[0][size]
        for other in sizes[1:]:
            amount = amount + other[size]
        table_ref[place : place + 1, :] = jnp.broadcast_to(amount, (1, LANES))


def masters_kernel(squares_ref, *refs):
    masters, updates = refs[:4], refs[4:8]
    outs, norms_ref = refs[8:12], refs[12]
    sizes = jnp.sqrt(squares_ref[0:4, :])
    steps = jnp.sqrt(squares_ref[4:8, :] + trust_epsilon)
    norms_ref[0:4, :] = sizes
    norms_ref[4:8, :] = steps
    ratio = learn_rate * (sizes / steps)
    for index in range(4):
        scale = ratio[index : index + 1, 0:1]
        if len(masters[index].shape) == 3:
            scale = scale.reshape(1, 1, 1)
        outs[index][...] = masters[index][...] - scale * updates[index][...]


def shards(
    block_input,
    lengths,
    norm_params,
    qkv_weight,
    out_weight,
    up_weight,
    down_weight,
    qkv_first,
    qkv_second,
    out_first,
    out_second,
    up_first,
    up_second,
    down_first,
    down_second,
    norm_first,
    norm_second,
    out_grad,
):
    row_count, width = block_input.shape
    local = qkv_weight.shape[2]
    hidden_units = up_weight.shape[1]
    group_count = lax.axis_size("dp")
    own = width // group_count
    own_start = lax.axis_index("dp") * own
    part = row_count // CHUNKS
    half = part // 2
    chunks = range(CHUNKS)
    bits = list(range(log2_of(group_count)))
    along = {"A": bits, "B": [1, 0] + bits[2:], "C": bits[1:] + [0]}

    line = Line()
    qkv_parts = jnp.transpose(qkv_weight, (1, 0, 2))
    cosine, sine = rotary_tables(row_count)
    live = Raw(lengths, SMEM)

    weight_shapes = [shaped(3, width, local, kind=LOW), shaped(local, width, kind=LOW)]
    chunk_shapes = [
        shaped(part, width, kind=LOW),
        shaped(part, local, kind=LOW),
        shaped(part, local, kind=LOW),
        shaped(part, local, kind=LOW),
        shaped(part, local, kind=LOW),
        shaped(part, LANES),
        cut(half, width),
        shaped(half, width),
    ]
    outs = line.call(
        first_kernel,
        weight_shapes + chunk_shapes,
        [live]
        + [Raw(a, HBM) for a in (block_input, norm_params, cosine, sine, qkv_parts, out_weight)],
        scratch=[
            pltpu.VMEM((part, width), LOW),
            pltpu.VMEM(norm_params.shape, WIDE),
            pltpu.VMEM((part, LANES), WIDE),
            pltpu.VMEM((part, LANES), WIDE),
            pltpu.VMEM((3, width, local), WIDE),
            pltpu.VMEM((local, width), WIDE),
            pltpu.SemaphoreType.DMA((8,)),
        ],
        name="attention_first",
    )
    qkv_low, out_low = outs[:2]
    parts = [outs[2:]]
    arrived = [near(parts[0][6])]
    for c in chunks[1:]:
        before = [p[2] for p in parts] + [p[3] for p in parts]
        parts.append(
            line.call(
                functools.partial(next_kernel, first_row=c * part, part=part),
                chunk_shapes,
                [live, block_input, norm_params, cosine, sine, qkv_low, out_low] + before,
                name="attention_next",
            )
        )
        arrived.append(near(parts[c][6]))
    normed_in, query, keys, values, attn, masses, sends, keeps = zip(*parts)
    branch_terms = [sum_rows(line, keeps[c], arrived[c], "sum_branch") for c in chunks]
    up_low = line.call(
        cast_kernel, [shaped(*up_weight.shape, kind=LOW)], [Take(up_weight)], name="cast_up"
    )[0]
    down_low = line.call(
        cast_kernel, [shaped(*down_weight.shape, kind=LOW)], [Take(down_weight)], name="cast_down"
    )[0]

    branch, hidden, normed_mid, up, active, mlp_terms = [], [], [], [], [], []
    for c in chunks:
        outs = line.call(
            functools.partial(middle_kernel, c * part),
            [shaped(half, width), shaped(half, width), cut(half, width)],
            [block_input, norm_params, *branch_terms[c]],
            name="middle",
        )
        branch.append(outs[0])
        hidden.append(outs[1])
        other = near(outs[2])
        outs = line.call(
            mlp_kernel,
            [
                shaped(part, width, kind=LOW),
                shaped(part, hidden_units),
                shaped(part, hidden_units, kind=LOW),
                cut(half, width),
                shaped(half, width),
            ],
            [outs[2], other, up_low, down_low],
            name="mlp",
        )
        normed_mid.append(outs[0])
        up.append(outs[1])
        active.append(outs[2])
        mlp_terms.append(sum_rows(line, outs[4], near(outs[3]), "sum_mlp"))

    middle = hidden_units // 2
    pieces = {
        "d0": Piece("d0", (0, middle), along["A"]),
        "d1": Piece("d1", (middle, hidden_units), along["C"]),
        "u0": Piece("u0", (0, middle), along["A"]),
        "u1": Piece("u1", (middle, hidden_units), along["A"]),
        "q0": Piece("q0", (0, 1), along["A"]),
        "q1": Piece("q1", (1, 2), along["A"]),
        "q2": Piece("q2", (2, 3), along["B"]),
        "o0": Piece("o0", (0, local), along["A"]),
    }
    of = lambda letter: [piece for name, piece in pieces.items() if name[0] == letter]

    def begin(letter, kernel, left, right, name):
        for piece, send in zip(
            of(letter), owner_products(line, kernel, left, right, of(letter), own, True, name)
        ):
            piece.start(send)

    def hold(letter, kernel, left, right, name):
        for piece, keep in zip(
            of(letter), owner_products(line, kernel, left, right, of(letter), own, False, name)
        ):
            piece.hold(keep)

    def advance(*names):
        for name in names:
            if pieces[name].stage < len(bits):
                pieces[name].advance(line)

    block_rows, block_other, loss_sums, grad_final, grad_up_rows, mid_terms = [], [], [], [], [], []
    grad_blocks = lambda: [block for blocks in grad_final for block in blocks]
    for c in chunks:
        outs = line.call(
            functools.partial(loss_kernel, c * part),
            [cut(half, width), cut(half, width), shaped(2, width)],
            [out_grad, norm_params, hidden[c], *mlp_terms[c]],
            name="loss",
        )
        block_rows.append(outs[0])
        loss_sums.append(outs[2])
        grad_final += [outs[1], near(outs[1])]
        if c == CHUNKS - 1:
            begin("d", owned_columns_kernel, active, grad_blocks(), "down_send")
        outs = line.call(
            mlp_back_kernel,
            [
                shaped(part, width, kind=LOW),
                shaped(part, hidden_units, kind=LOW),
                cut(half, width),
                shaped(half, width),
            ],
            [*grad_final[-2:], up[c], up_low, down_low],
            name="mlp_back",
        )
        grad_up_rows.append(outs[1])
        crossing = near(outs[2])
        if c == CHUNKS - 1:
            begin("u", owned_rows_kernel, normed_mid, grad_up_rows, "up_send")
        mid_terms.append(sum_rows(line, outs[3], crossing, "sum_mid"))
        block_other.append(near(block_rows[c]))
    hold("d", owned_columns_kernel, active, grad_blocks(), "down_keep")
    hold("u", owned_rows_kernel, normed_mid, grad_up_rows, "up_keep")
    block_output = line.call(
        functools.partial(place_kernel, chunks=CHUNKS),
        [shaped(row_count, width, kind=LOW)],
        [sum(block_rows, []), sum(block_other, [])],
        name="place_output",
    )[0]

    grad_hidden, norms_sums, own_back, other_back = [], [], [], []
    for c in chunks:
        outs = line.call(
            functools.partial(norms_back_kernel, c * part),
            [shaped(half, width), cut(half, width), shaped(4, width)],
            [out_grad, norm_params, hidden[c], branch[c], *mid_terms[c]],
            name="norms_back",
        )
        grad_hidden.append(outs[0])
        norms_sums.append(outs[2])
        own_back.append(outs[1])
        other_back.append(near(outs[1]))
    advance("d1")
    grad_branch, grad_rows = line.call(
        functools.partial(attention_back_kernel, chunks=CHUNKS),
        [shaped(row_count, width, kind=LOW), shaped(row_count, 3 * local, kind=LOW)],
        [live, out_low, cosine, sine, *own_back, *other_back, *query, *keys, *values, *masses],
        scratch=[pltpu.VMEM((row_count, local), WIDE), pltpu.VMEM((row_count, local), WIDE)],
        name="attention_back",
    )
    begin("q", owned_parts_kernel, normed_in, [grad_rows], "qkv_send")
    begin("o", owned_columns_kernel, attn, [grad_branch], "out_send")
    send, keep = line.call(
        functools.partial(input_back_kernel, chunks=CHUNKS),
        [cut(row_count // 2, width), shaped(row_count // 2, width)],
        [grad_rows, qkv_low],
        name="input_back",
    )
    crossing = near(send)
    advance("d0")
    hold("q", owned_parts_kernel, normed_in, [grad_rows], "qkv_keep")
    hold("o", owned_columns_kernel, attn, [grad_branch], "out_keep")
    in_terms = sum_rows(line, keep, crossing, "sum_in")
    advance("d1", "u0", "d0")

    input_rows, input_sums = line.call(
        functools.partial(input_norm_kernel, chunks=CHUNKS),
        [cut(row_count // 2, width), shaped(2, width)],
        [block_input, norm_params, *in_terms, *grad_hidden],
        name="input_norm",
    )
    input_other = near(input_rows)
    advance("q2")
    input_grad = line.call(
        functools.partial(place_kernel, chunks=CHUNKS),
        [shaped(row_count, width, kind=LOW)],
        [input_rows, input_other],
        name="place_input",
    )[0]
    grad_norms = line.call(
        functools.partial(norm_sums_kernel, chunks=CHUNKS),
        [shaped(8, width)],
        [input_sums, *norms_sums, *loss_sums],
        name="norm_sums",
    )[0]
    grad_norms = line.call(
        sum_kernel,
        [shaped(8, width)],
        [grad_norms, swap(grad_norms, "tensor", 1)],
        name="sum_norms",
    )[0]
    advance("u1", "u0")
    grad_norms = sum_all(line, grad_norms, "dp", "sum_norms")
    advance("u1", "q0", "q1")
    columns = lambda: (slice(None), pl.ds(pl.multiple_of(lax.axis_index("dp") * own, own), own))
    mine = lambda array, axis: lax.dynamic_slice_in_dim(array, own_start, own, axis)
    if own % LANES:
        norm_args = [mine(norm_params, 1), mine(grad_norms, 1)]
    else:
        norm_args = [
            Take(norm_params, (8, own), columns),
            Take(grad_norms, (8, own), columns),
        ]
    norm_new, norm_first_new, norm_second_new = line.call(
        norm_step_kernel,
        [shaped(8, own)] * 3,
        [*norm_args, Take(norm_first), Take(norm_second)],
        name="norm_step",
    )

    rows = lambda: (pl.ds(pl.multiple_of(lax.axis_index("dp") * own, own), own),)
    part_rows = lambda: (slice(None), *rows())
    masters = [
        Take(qkv_parts, (3, own, local), part_rows),
        Take(mine(out_weight, 1)) if own % LANES else Take(out_weight, (local, own), columns),
        Take(up_weight, (own, hidden_units), rows),
        Take(mine(down_weight, 1)) if own % LANES else Take(down_weight, (hidden_units, own), columns),
    ]
    states = [
        (jnp.transpose(qkv_first, (1, 0, 2)), jnp.transpose(qkv_second, (1, 0, 2))),
        (out_first, out_second),
        (up_first, up_second),
        (down_first, down_second),
    ]
    everything = slice(None)
    table = jnp.zeros((8, LANES), WIDE)
    stepped = [None] * 4

    def step(index, letter):
        nonlocal table
        found = of(letter)
        for piece in found:
            while piece.stage < len(bits):
                piece.advance(line)
        if letter == "u":
            regions = [(everything, slice(*piece.window)) for piece in found]
        else:
            regions = [(slice(*piece.window),) for piece in found]
        terms = [
            Take(term, term.shape[1:], lambda: (0,)) for piece in found for term in piece.terms
        ]
        shape = masters[index].shape
        outs = line.call(
            functools.partial(
                moments_kernel,
                row=index,
                regions=regions,
                counts=[len(piece.terms) for piece in found],
            ),
            [shaped(*shape)] * 4 + [shaped(8, LANES)],
            [masters[index], *[Take(state) for state in states[index]], table, *terms],
            megabytes=16,
            name="moments_" + letter,
        )
        stepped[index] = outs[:4]
        table = outs[4]

    step(3, "d")
    advance("u1", "q0", "q1", "q2", "o0")
    step(2, "u")
    advance("q0", "q1", "q2", "o0")
    step(1, "o")
    step(0, "q")
    squares = sum_all(line, table, "tensor", "sum_squares")
    squares = sum_all(line, squares, "dp", "sum_squares")
    outs = line.call(
        masters_kernel,
        [shaped(*entry[0].shape) for entry in stepped] + [shaped(8, LANES)],
        [squares, *[entry[0] for entry in stepped], *[entry[1] for entry in stepped]],
        name="masters",
    )
    back = lambda array: jnp.transpose(array, (1, 0, 2))
    matrix_norms = jnp.stack([outs[4][0:4, 0], outs[4][4:8, 0]])
    return (
        block_output,
        input_grad,
        back(outs[0]),
        back(stepped[0][2]),
        back(stepped[0][3]),
        outs[1],
        stepped[1][2],
        stepped[1][3],
        outs[2],
        stepped[2][2],
        stepped[2][3],
        outs[3],
        stepped[3][2],
        stepped[3][3],
        norm_new,
        norm_first_new,
        norm_second_new,
        matrix_norms,
    )


def solution(mesh):
    in_specs = (
        P("dp", None),
        P("dp"),
        P(),
        P(None, None, "tensor"),
        P("tensor", None),
        P(None, "tensor"),
        P("tensor", None),
        P("dp", None, "tensor"),
        P("dp", None, "tensor"),
        P("tensor", "dp"),
        P("tensor", "dp"),
        P("dp", "tensor"),
        P("dp", "tensor"),
        P("tensor", "dp"),
        P("tensor", "dp"),
        P(None, "dp"),
        P(None, "dp"),
        P("dp", None),
    )
    out_specs = (
        P("dp", None),
        P("dp", None),
        P("dp", None, "tensor"),
        P("dp", None, "tensor"),
        P("dp", None, "tensor"),
        P("tensor", "dp"),
        P("tensor", "dp"),
        P("tensor", "dp"),
        P("dp", "tensor"),
        P("dp", "tensor"),
        P("dp", "tensor"),
        P("tensor", "dp"),
        P("tensor", "dp"),
        P("tensor", "dp"),
        P(None, "dp"),
        P(None, "dp"),
        P(None, "dp"),
        P(),
    )
    return jax.shard_map(shards, mesh=mesh, in_specs=in_specs, out_specs=out_specs, check_vma=False)
```

```python
import functools

import jax
import jax.numpy as jnp
import numpy as np
from jax import lax
from jax.experimental import pallas as pl
from jax.experimental.pallas import tpu as pltpu
from jax.sharding import PartitionSpec as P

HEAD_DIM = 64
STEP = 10
CHUNKS = 2
LANES = 128

norm_epsilon = 1e-05
rotary_base = 10000.0
mask_fill = -1000000000.0
first_decay = 0.9
second_decay = 0.999
adam_epsilon = 1e-06
trust_epsilon = 1e-06
decay_rate = 0.01
learn_rate = 0.25

CUT_ATTENTION, CUT_MIDDLE, CUT_MLP, CUT_LOSS = 2, 4, 4, 2
CUT_MID, CUT_NORMS, CUT_BACK, CUT_INPUT = 2, 2, 2, 2

LOW = jnp.bfloat16
WIDE = jnp.float32
VMEM = pl.BlockSpec(memory_space=pltpu.VMEM)
SMEM = pl.BlockSpec(memory_space=pltpu.SMEM)
HBM = pl.BlockSpec(memory_space=pltpu.HBM)


def log2_of(count):
    bits = 0
    while (1 << bits) < count:
        bits += 1
    return bits


def swap(values, axis, distance):
    count = lax.axis_size(axis)
    return lax.ppermute(values, axis, [(i, i ^ distance) for i in range(count)])


def chunk_order(count, bits):
    order = [0]
    for bit in reversed(bits):
        order = order + [distance ^ (1 << bit) for distance in order]
    return order


def normalize(values):
    center = values - jnp.mean(values, axis=-1, keepdims=True)
    inverse = lax.rsqrt(jnp.mean(center * center, axis=-1, keepdims=True) + norm_epsilon)
    return center * inverse, inverse


def norm_back(incoming, normed, inverse, gain):
    scaled = incoming * gain
    inner = (
        scaled
        - jnp.mean(scaled, axis=-1, keepdims=True)
        - normed * jnp.mean(scaled * normed, axis=-1, keepdims=True)
    )
    gain_grad = jnp.sum(incoming * normed, axis=0, keepdims=True)
    return inner * inverse, gain_grad, jnp.sum(incoming, axis=0, keepdims=True)


def rotary_tables(length):
    half = HEAD_DIM // 2
    lane = np.arange(LANES)
    frequency = (rotary_base ** (-((lane % half).astype(np.float32) * 2.0 / HEAD_DIM))).astype(np.float32)
    angles = np.arange(length, dtype=np.float32)[:, None] * frequency[None, :]
    sign = np.where(lane % HEAD_DIM < half, -1.0, 1.0)
    cosine = np.cos(angles.astype(np.float64)).astype(np.float32)
    sine = (np.sin(angles.astype(np.float64)) * sign[None, :]).astype(np.float32)
    return jnp.asarray(cosine), jnp.asarray(sine)


def turn(values, cosine, sine):
    half = HEAD_DIM // 2
    lane = lax.broadcasted_iota(jnp.int32, (1, LANES), 1)
    first = lax.rem(lane, HEAD_DIM) < half
    tiles = []
    for start in range(0, values.shape[1], LANES):
        tile = values[:, start : start + LANES]
        other = jnp.where(
            first, pltpu.roll(tile, LANES - half, 1), pltpu.roll(tile, half, 1)
        )
        tiles.append(tile * cosine + other * sine)
    return tiles[0] if len(tiles) == 1 else jnp.concatenate(tiles, axis=1)


def gelu_mass(up):
    return 0.5 * (1.0 + lax.erf(up * (0.5**0.5)))


def dot(left, right):
    return jnp.dot(left, right, preferred_element_type=WIDE)


def dot_rows(left, right):
    return lax.dot_general(left, right, (((0,), (0,)), ((), ())), preferred_element_type=WIDE)


def dot_wide(left, right):
    return lax.dot_general(left, right, (((1,), (1,)), ((), ())), preferred_element_type=WIDE)


def of_head(values, head):
    lane = lax.broadcasted_iota(jnp.int32, (1, values.shape[1]), 1)
    mine = (lane >= head * HEAD_DIM) & (lane < (head + 1) * HEAD_DIM)
    return jnp.where(mine, values, jnp.zeros_like(values))


def core_index():
    return lax.rem(lax.axis_index("tensor"), 2)


def shaped(*shape, kind=WIDE):
    return jax.ShapeDtypeStruct(shape, kind)


def cut(rows, width, count=4):
    return [shaped(rows // count, width)] * count


def near(values):
    return [swap(piece, "tensor", 1) for piece in values]


class Take:
    def __init__(self, array, shape=None, index=None):
        self.array = array
        self.shape = array.shape if shape is None else shape
        self.index = index


class Raw:
    def __init__(self, array, spec):
        self.array = array
        self.spec = spec


class Rows:
    def __init__(self, refs):
        self.refs = refs
        self.step = refs[0].shape[0]
        self.shape = (self.step * len(refs), refs[0].shape[1])

    def spans(self, key):
        first, last = 0, self.shape[0]
        if key is not Ellipsis and key[0] != slice(None):
            first, last = key[0].start, key[0].stop
        for place, ref in enumerate(self.refs):
            start, stop = max(first, place * self.step), min(last, (place + 1) * self.step)
            if start < stop:
                inside = slice(start - place * self.step, stop - place * self.step)
                yield ref, inside, slice(start - first, stop - first)

    def __getitem__(self, key):
        pieces = [ref[inside, :] for ref, inside, _ in self.spans(key)]
        return pieces[0] if len(pieces) == 1 else jnp.concatenate(pieces, axis=0)

    def __setitem__(self, key, value):
        for ref, inside, outside in self.spans(key):
            ref[inside, :] = value[outside]


class Line:
    def __init__(self):
        self.token = jnp.zeros((8, LANES), WIDE)

    def call(self, kernel, outs, args, scratch=(), megabytes=12, first=False):
        arrays, specs, buffers, layout, takes = [], [], [], [], []
        for arg in args:
            if isinstance(arg, Take):
                layout.append(0)
                takes.append((len(arrays), arg))
                arrays.append(arg.array)
                specs.append(HBM)
                buffers.append(pltpu.VMEM(arg.shape, arg.array.dtype))
            elif isinstance(arg, Raw):
                layout.append(0)
                arrays.append(arg.array)
                specs.append(arg.spec)
            elif isinstance(arg, (list, tuple)):
                layout.append(len(arg))
                arrays += arg
                specs += [VMEM] * len(arg)
            else:
                layout.append(0)
                arrays.append(arg)
                specs.append(VMEM)
        if takes:
            buffers.append(pltpu.SemaphoreType.DMA((len(takes),)))
        token = [] if first else [self.token]
        out_layout = [len(out) if isinstance(out, list) else 0 for out in outs]
        out_shapes = [o for out in outs for o in (out if isinstance(out, list) else [out])]

        def joined(refs, layout):
            refs = list(refs)
            return [
                Rows([refs.pop(0) for _ in range(count)]) if count else refs.pop(0)
                for count in layout
            ]

        def body(*refs):
            inputs = list(refs[: len(arrays)])
            rest = refs[len(arrays) + len(token) :]
            results, rest = rest[: len(out_shapes)], rest[len(out_shapes) + len(token) :]
            own, rest = rest[: len(scratch)], rest[len(scratch) :]
            copies = []
            for place, (i, take) in enumerate(takes):
                source = inputs[i]
                if take.index is not None:
                    source = source.at[take.index()]
                copies.append(pltpu.make_async_copy(source, rest[place], rest[-1].at[place]))
                inputs[i] = rest[place]
            for copy in copies:
                copy.start()
            for copy in copies:
                copy.wait()
            kernel(*joined(inputs, layout), *joined(results, out_layout), *own)

        results = pl.pallas_call(
            body,
            out_shape=(*out_shapes, *[shaped(8, LANES) for _ in token]),
            in_specs=[*specs, *[HBM for _ in token]],
            out_specs=tuple([VMEM] * len(out_shapes) + [HBM for _ in token]),
            scratch_shapes=[*scratch, *buffers],
            input_output_aliases={len(arrays): len(out_shapes)} if token else {},
            compiler_params=pltpu.CompilerParams(vmem_limit_bytes=megabytes * 1024 * 1024),
            cost_estimate=pl.CostEstimate(flops=0, bytes_accessed=0, transcendentals=0),
        )(*arrays, *token)
        found = list(results)
        if token:
            self.token = found.pop()
        return [
            [found.pop(0) for _ in range(count)] if count else found.pop(0) for count in out_layout
        ]


def sum_kernel(*refs):
    total = refs[0][...]
    for ref in refs[1:-1]:
        total = total + ref[...]
    refs[-1][...] = total


def pairs_kernel(*refs):
    terms = [ref[...] for ref in refs[:-1]]
    while len(terms) > 1:
        terms = [terms[i] + terms[i + 1] for i in range(0, len(terms), 2)]
    refs[-1][...] = terms[0]


def sum_rows(line, keep, arrived, count=1):
    mine, theirs = keep, arrived
    for bit in range(1, log2_of(lax.axis_size("tensor"))):
        mine = line.call(sum_kernel, [cut(*keep.shape, count)], [mine, theirs])[0]
        theirs = [swap(piece, "tensor", 1 << bit) for piece in mine]
    return mine, theirs


def sum_terms(values, axis, start, taken):
    return [values] + [swap(values, axis, distance << start) for distance in range(1, 1 << taken)]


class Piece:
    def __init__(self, weight, window, bits):
        self.weight, self.window, self.bits = weight, window, bits
        self.terms, self.stage = [], 0

    def start(self):
        send = self.weight.products([self], True)[0]
        self.terms.append(swap(send, "dp", 1 << self.bits[0]))
        self.stage = 1

    def advance(self):
        if self.stage == len(self.bits):
            return
        size = self.terms[0].shape[0] >> self.stage
        shape = (size,) + self.terms[0].shape[1:]
        index = lambda: (pl.ds(size, size),)
        outgoing = self.weight.line.call(
            sum_kernel, [shaped(*shape)], [Take(term, shape, index) for term in self.terms]
        )[0]
        self.terms.append(swap(outgoing, "dp", 1 << self.bits[self.stage]))
        self.stage += 1


class Weight:
    tables = {}

    def __init__(self, line, row, size, kernel, factors, master, states):
        self.line, self.row, self.size, self.kernel = line, row, size, kernel
        self.factors, self.master, self.states = factors, master, states
        self.pieces = []

    def piece(self, first, last, count, bits):
        found = Piece(self, (self.size * first // count, self.size * last // count), bits)
        self.pieces.append(found)
        return found

    def products(self, pieces, send):
        own = self.line.own
        return owner_products(self.line, self.kernel, *self.factors(), pieces, own, send)

    def hold(self):
        for piece, keep in zip(self.pieces, self.products(self.pieces, False)):
            piece.terms.insert(0, keep)

    def stage(self):
        before = [self.master, *[Take(state) for state in self.states]]
        self.master, *self.states = self.line.call(
            copy_kernel, [shaped(*self.master.shape)] * 3, before
        )

    def moments(self):
        for piece in self.pieces:
            while piece.stage < len(piece.bits):
                piece.advance()
        everything = slice(None)
        if self.kernel is owned_rows_kernel:
            regions = [(everything, slice(*piece.window)) for piece in self.pieces]
        else:
            regions = [(slice(*piece.window),) for piece in self.pieces]
        terms = [
            Take(term, term.shape[1:], lambda: (0,))
            for piece in self.pieces
            for term in piece.terms
        ]
        states = self.states
        if isinstance(self.master, Take):
            states = [Take(state) for state in states]
        outs = self.line.call(
            functools.partial(
                moments_kernel,
                row=self.row,
                regions=regions,
                counts=[len(piece.terms) for piece in self.pieces],
            ),
            [shaped(*self.master.shape)] * 4 + [shaped(8, LANES)],
            [self.master, *states, self.line.table, *terms],
            megabytes=16,
        )
        self.kept, self.update, self.first_new, self.second_new, self.line.table = outs


def project(normed, weights, cosine, sine):
    query = turn(dot(normed, weights[0]), cosine, sine).astype(LOW)
    keys = turn(dot(normed, weights[1]), cosine, sine).astype(LOW)
    return query, keys, dot(normed, weights[2]).astype(LOW)


def attend(query, keys, values, first_row, live_len):
    rows, reach = query.shape[0], keys.shape[0]
    row = first_row + lax.broadcasted_iota(jnp.int32, (rows, reach), 0)
    column = lax.broadcasted_iota(jnp.int32, (rows, reach), 1)
    visible = (column <= row) & (column < live_len)
    lane = lax.broadcasted_iota(jnp.int32, (1, LANES), 1)
    mixed = jnp.zeros((rows, query.shape[1]), WIDE)
    masses = jnp.zeros((rows, LANES), WIDE)
    for head in range(query.shape[1] // HEAD_DIM):
        scores = dot_wide(of_head(query, head), keys) * HEAD_DIM ** (-0.5)
        scores = jnp.where(visible, scores, mask_fill)
        top = jnp.max(scores, axis=-1, keepdims=True)
        expo = jnp.exp(scores - top)
        total = jnp.sum(expo, axis=-1, keepdims=True)
        probs = (expo * (1.0 / total)).astype(LOW)
        mixed = mixed + dot(probs, of_head(values, head))
        masses = jnp.where(lane == head, top + jnp.log(total), masses)
    live = first_row + lax.broadcasted_iota(jnp.int32, (rows, 1), 0) < live_len
    return jnp.where(live, mixed, 0.0).astype(LOW), masses


def split_rows(left_ref, right, send_ref, keep_ref, how):
    half = send_ref.shape[0]
    core = core_index()
    send_ref[...] = how(left_ref[pl.ds((1 - core) * half, half), :], right)
    keep_ref[...] = how(left_ref[pl.ds(core * half, half), :], right)


def first_kernel(
    live_ref, x_any, norm_any, cos_any, sin_any, qkv_any, out_any,
    qkv_low_ref, out_low_ref, normed_ref, q_ref, k_ref, v_ref, attn_ref, mass_ref, send_ref, keep_ref,
    x_ref, norm_ref, cos_ref, sin_ref, qkv_in, out_in, arrived,
):
    part = x_ref.shape[0]
    sources = [x_any.at[pl.ds(0, part)], norm_any, cos_any.at[pl.ds(0, part)], sin_any.at[pl.ds(0, part)]]
    targets = [x_ref, norm_ref, cos_ref, sin_ref]
    sources += [qkv_any.at[j] for j in range(3)] + [out_any]
    targets += [qkv_in.at[j] for j in range(3)] + [out_in]
    copies = [
        pltpu.make_async_copy(source, target, arrived.at[i])
        for i, (source, target) in enumerate(zip(sources, targets))
    ]
    for copy in copies:
        copy.start()
    copies[0].wait()
    copies[1].wait()
    stat, _ = normalize(x_ref[...].astype(WIDE))
    normed = (stat * norm_ref[0:1, :] + norm_ref[1:2, :]).astype(LOW)
    normed_ref[...] = normed
    copies[2].wait()
    copies[3].wait()
    weights = []
    for j in range(3):
        copies[4 + j].wait()
        weights.append(qkv_in[j].astype(LOW))
        qkv_low_ref[j] = weights[j]
    query, keys, values = project(normed, weights, cos_ref[...], sin_ref[...])
    q_ref[...], k_ref[...], v_ref[...] = query, keys, values
    attn_ref[...], mass_ref[...] = attend(query, keys, values, 0, live_ref[0])
    copies[7].wait()
    out_low = out_in[...].astype(LOW)
    out_low_ref[...] = out_low
    split_rows(attn_ref, out_low, send_ref, keep_ref, dot)


def next_kernel(
    live_ref, x_ref, norm_ref, cos_ref, sin_ref, qkv_low_ref, out_low_ref, *refs, first_row, part
):
    earlier = first_row // part
    rows = slice(first_row, first_row + part)
    k_before, v_before = refs[:earlier], refs[earlier : 2 * earlier]
    normed_ref, q_ref, k_ref, v_ref, attn_ref, mass_ref, send_ref, keep_ref = refs[2 * earlier :]
    stat, _ = normalize(x_ref[rows, :].astype(WIDE))
    normed = (stat * norm_ref[0:1, :] + norm_ref[1:2, :]).astype(LOW)
    normed_ref[...] = normed
    weights = [qkv_low_ref[j] for j in range(3)]
    query, keys, values = project(normed, weights, cos_ref[rows, :], sin_ref[rows, :])
    q_ref[...], k_ref[...], v_ref[...] = query, keys, values
    keys = jnp.concatenate([ref[...] for ref in k_before] + [keys], axis=0)
    values = jnp.concatenate([ref[...] for ref in v_before] + [values], axis=0)
    attn_ref[...], mass_ref[...] = attend(query, keys, values, first_row, live_ref[0])
    split_rows(attn_ref, out_low_ref[...], send_ref, keep_ref, dot)


def cast_kernel(wide_ref, low_ref):
    low_ref[...] = wide_ref[...].astype(LOW)


def middle_kernel(first_row, x_ref, norm_ref, mine_ref, theirs_ref, branch_ref, hidden_ref, normed_ref):
    half = mine_ref.shape[0]
    branch = mine_ref[...] + theirs_ref[...]
    branch_ref[...] = branch
    stat, _ = normalize(branch)
    inputs = x_ref[pl.ds(first_row + core_index() * half, half), :].astype(WIDE)
    hidden = inputs + stat * norm_ref[2:3, :] + norm_ref[3:4, :]
    hidden_ref[...] = hidden
    stat, _ = normalize(hidden)
    normed_ref[...] = stat * norm_ref[4:5, :] + norm_ref[5:6, :]


def mlp_kernel(own_ref, other_ref, up_w_ref, down_w_ref, normed_ref, up_ref, active_ref, send_ref, keep_ref):
    half = own_ref.shape[0]
    normed = jnp.concatenate([own_ref[...].astype(LOW), other_ref[...].astype(LOW)], axis=0)
    normed_ref[...] = normed
    step = min(256, up_w_ref.shape[1])
    total = None
    for start in range(0, up_w_ref.shape[1], step):
        block = slice(start, start + step)
        up = dot(normed, up_w_ref[:, block])
        up_ref[:, block] = up
        active = (up * gelu_mass(up)).astype(LOW)
        active_ref[:, block] = active
        product = dot(active, down_w_ref[block, :])
        total = product if total is None else total + product
    keep_ref[...] = total[:half]
    send_ref[...] = total[half:]


def loss_kernel(
    first_row, grad_ref, norm_ref, hidden_ref, mine_ref, theirs_ref, block_ref, back_ref, sums_ref
):
    half = mine_ref.shape[0]
    stat, inverse = normalize(mine_ref[...] + theirs_ref[...])
    block_ref[...] = hidden_ref[...] + stat * norm_ref[6:7, :] + norm_ref[7:8, :]
    incoming = grad_ref[pl.ds(first_row + core_index() * half, half), :].astype(WIDE)
    back, gain, offset = norm_back(incoming, stat, inverse, norm_ref[6:7, :])
    back_ref[...] = back
    sums_ref[0:1, :] = gain
    sums_ref[1:2, :] = offset


def mlp_back_kernel(
    own_ref, other_ref, up_ref, up_w_ref, down_w_ref, grad_mlp_ref, grad_up_ref, send_ref, keep_ref
):
    half = own_ref.shape[0]
    grad_mlp = jnp.concatenate([own_ref[...].astype(LOW), other_ref[...].astype(LOW)], axis=0)
    grad_mlp_ref[...] = grad_mlp
    step = min(256, up_w_ref.shape[1])
    total = None
    for start in range(0, up_w_ref.shape[1], step):
        block = slice(start, start + step)
        up = up_ref[:, block]
        slope = gelu_mass(up) + up * jnp.exp(-0.5 * up * up) * float((2.0 * np.pi) ** -0.5)
        grad_up = (dot_wide(grad_mlp, down_w_ref[block, :]) * slope).astype(LOW)
        grad_up_ref[:, block] = grad_up
        product = dot_wide(grad_up, up_w_ref[:, block])
        total = product if total is None else total + product
    keep_ref[...] = total[:half]
    send_ref[...] = total[half:]


def norms_back_kernel(
    first_row, grad_ref, norm_ref, hidden_ref, branch_ref, mine_ref, theirs_ref,
    grad_hidden_ref, back_ref, sums_ref,
):
    half = mine_ref.shape[0]
    stat, inverse = normalize(hidden_ref[...])
    back, gain, offset = norm_back(
        mine_ref[...] + theirs_ref[...], stat, inverse, norm_ref[4:5, :]
    )
    incoming = grad_ref[pl.ds(first_row + core_index() * half, half), :].astype(WIDE)
    grad_hidden = incoming + back
    grad_hidden_ref[...] = grad_hidden
    sums_ref[2:3, :] = gain
    sums_ref[3:4, :] = offset
    stat, inverse = normalize(branch_ref[...])
    back, gain, offset = norm_back(grad_hidden, stat, inverse, norm_ref[2:3, :])
    back_ref[...] = back
    sums_ref[0:1, :] = gain
    sums_ref[1:2, :] = offset


def attention_back_kernel(live_ref, out_low_ref, cos_ref, sin_ref, *refs, chunks):
    groups = [refs[i * chunks : (i + 1) * chunks] for i in range(6)]
    own, other, query_refs, key_refs, value_refs, mass_refs = groups
    grad_branch_ref, rows_ref = refs[6 * chunks : 6 * chunks + 2]
    keys_sum, values_sum = refs[6 * chunks + 2 :]
    half = own[0].shape[0]
    part = 2 * half
    core = core_index()
    live_len = live_ref[0]
    local = rows_ref.shape[1] // 3
    heads = local // HEAD_DIM
    for c in range(chunks):
        grad_branch_ref[pl.ds(c * part + core * half, half), :] = own[c][...].astype(LOW)
        grad_branch_ref[pl.ds(c * part + (1 - core) * half, half), :] = other[c][...].astype(LOW)
    keys_all = jnp.concatenate([ref[...] for ref in key_refs], axis=0)
    values_all = jnp.concatenate([ref[...] for ref in value_refs], axis=0)
    for c in range(chunks):
        reach = (c + 1) * part
        first_row = c * part
        row = first_row + lax.broadcasted_iota(jnp.int32, (part, reach), 0)
        column = lax.broadcasted_iota(jnp.int32, (part, reach), 1)
        visible = (column <= row) & (column < live_len)
        live = first_row + lax.broadcasted_iota(jnp.int32, (part, 1), 0) < live_len
        grad_attn = dot_wide(grad_branch_ref[first_row : first_row + part, :], out_low_ref[...])
        grad_mixed = jnp.where(live, grad_attn, 0.0).astype(LOW)
        query, masses = query_refs[c][...], mass_refs[c][...]
        keys, values = keys_all[:reach], values_all[:reach]
        grad_query = jnp.zeros((part, local), WIDE)
        grad_keys = jnp.zeros((reach, local), WIDE)
        grad_values = jnp.zeros((reach, local), WIDE)
        for head in range(heads):
            query_h, grad_h = of_head(query, head), of_head(grad_mixed, head)
            scores = dot_wide(query_h, keys) * HEAD_DIM ** (-0.5)
            scores = jnp.where(visible, scores, mask_fill)
            probs = jnp.exp(scores - masses[:, head : head + 1])
            grad_values = grad_values + dot_rows(probs.astype(LOW), grad_h)
            grad_probs = dot_wide(grad_h, values)
            inner = jnp.sum(grad_probs * probs, axis=-1, keepdims=True)
            grad_scores = (probs * (grad_probs - inner)).astype(LOW)
            grad_query = grad_query + dot(grad_scores, of_head(keys, head))
            grad_keys = grad_keys + dot_rows(grad_scores, query_h)
        cosine = cos_ref[first_row : first_row + part, :]
        sine = sin_ref[first_row : first_row + part, :]
        grad_query = turn(grad_query * HEAD_DIM ** (-0.5), cosine, -sine)
        rows_ref[first_row : first_row + part, 0:local] = grad_query.astype(LOW)
        if c == 0:
            keys_sum[0:reach, :] = grad_keys
            values_sum[0:reach, :] = grad_values
        else:
            keys_sum[0:first_row, :] += grad_keys[:first_row]
            keys_sum[first_row:reach, :] = grad_keys[first_row:]
            values_sum[0:first_row, :] += grad_values[:first_row]
            values_sum[first_row:reach, :] = grad_values[first_row:]
    grad_keys = turn(keys_sum[...] * HEAD_DIM ** (-0.5), cos_ref[...], -sin_ref[...])
    rows_ref[:, local : 2 * local] = grad_keys.astype(LOW)
    rows_ref[:, 2 * local : 3 * local] = values_sum[...].astype(LOW)


def picked_columns(refs, distances, own):
    rank = lax.axis_index("dp")
    blocks = []
    for distance in distances:
        start = pl.multiple_of(lax.bitwise_xor(rank, distance) * own, own)
        pieces = [ref[:, pl.ds(start, own)].astype(LOW) for ref in refs]
        blocks.append(pieces[0] if len(pieces) == 1 else jnp.concatenate(pieces, axis=0))
    return blocks[0] if len(blocks) == 1 else jnp.concatenate(blocks, axis=1)


def whole_rows(refs, window):
    pieces = [ref[:, window[0] : window[1]].astype(LOW) for ref in refs]
    return pieces[0] if len(pieces) == 1 else jnp.concatenate(pieces, axis=0)


def owned_columns_kernel(*refs, pairs, jobs, own):
    (lefts, rights), outs = pairs, refs[sum(pairs) :]
    left, right = refs[:lefts], refs[lefts : lefts + rights]
    for (distances, window), out_ref in zip(jobs, outs):
        rows = whole_rows(left, window)
        product = dot_rows(rows, picked_columns(right, distances, own))
        for place in range(len(distances)):
            out_ref[place] = product[:, place * own : (place + 1) * own]


def owned_rows_kernel(*refs, pairs, jobs, own):
    (lefts, rights), outs = pairs, refs[sum(pairs) :]
    left, right = refs[:lefts], refs[lefts : lefts + rights]
    for (distances, window), out_ref in zip(jobs, outs):
        product = dot_rows(picked_columns(left, distances, own), whole_rows(right, window))
        for place in range(len(distances)):
            out_ref[place] = product[place * own : (place + 1) * own, :]


def owned_parts_kernel(*refs, pairs, jobs, own):
    (lefts, rights), outs = pairs, refs[sum(pairs) :]
    left, right = refs[:lefts], refs[lefts : lefts + rights]
    for (distances, window), out_ref in zip(jobs, outs):
        local = out_ref.shape[3]
        columns = (window[0] * local, window[1] * local)
        product = dot_rows(picked_columns(left, distances, own), whole_rows(right, columns))
        for place in range(len(distances)):
            for j in range(window[1] - window[0]):
                out_ref[place, j] = product[
                    place * own : (place + 1) * own, j * local : (j + 1) * local
                ]


def rounded_kernel(*refs):
    refs[-1][...] = whole_rows(refs[:-1], (0, refs[0].shape[1]))


def narrow_products(line, kernel, left, right, jobs, outs, own):
    rank = lax.axis_index("dp")
    joined = []
    for arrays in (left, right):
        rows = sum(array.shape[0] for array in arrays)
        low = shaped(rows, arrays[0].shape[1], kind=LOW)
        joined.append(line.call(rounded_kernel, [low], arrays)[0])
    results = []
    for (distances, window), out in zip(jobs, outs):
        pick = lambda array: jnp.concatenate(
            [lax.dynamic_slice_in_dim(array, (rank ^ d) * own, own, 1) for d in distances], axis=1
        )
        if kernel is owned_columns_kernel:
            product = dot_rows(joined[0][:, window[0] : window[1]], pick(joined[1]))
            product = product.reshape(-1, len(distances), own).transpose(1, 0, 2)
        elif kernel is owned_rows_kernel:
            product = dot_rows(pick(joined[0]), joined[1][:, window[0] : window[1]])
            product = product.reshape(out.shape)
        else:
            local = out.shape[3]
            columns = joined[1][:, window[0] * local : window[1] * local]
            product = dot_rows(pick(joined[0]), columns)
            product = product.reshape(len(distances), own, -1, local).transpose(0, 2, 1, 3)
        results.append(product)
    return results


def owner_products(line, kernel, left, right, pieces, own, send):
    count = lax.axis_size("dp")
    jobs, outs = [], []
    for piece in pieces:
        order = chunk_order(count, piece.bits)
        order = order[count // 2 :] if send else order[: count // 2]
        jobs.append((order, piece.window))
        size = piece.window[1] - piece.window[0]
        if kernel is owned_columns_kernel:
            outs.append(shaped(len(order), size, own))
        elif kernel is owned_rows_kernel:
            outs.append(shaped(len(order), own, size))
        else:
            outs.append(shaped(len(order), size, own, right[0].shape[1] // 3))
    if own % LANES:
        return narrow_products(line, kernel, left, right, jobs, outs, own)
    return line.call(
        functools.partial(kernel, pairs=(len(left), len(right)), jobs=jobs, own=own),
        outs,
        [*left, *right],
        megabytes=20,
    )


def input_back_kernel(rows_ref, qkv_low_ref, send_ref, keep_ref, *, chunks):
    half = send_ref.shape[0] // chunks
    local = qkv_low_ref.shape[2]
    core = core_index()
    for c in range(chunks):
        for target, which in ((send_ref, 1 - core), (keep_ref, core)):
            rows = rows_ref[pl.ds(c * 2 * half + which * half, half), :]
            total = None
            for j in range(3):
                product = dot_wide(rows[:, j * local : (j + 1) * local], qkv_low_ref[j])
                total = product if total is None else total + product
            target[c * half : (c + 1) * half, :] = total


def input_norm_kernel(x_ref, norm_ref, mine_ref, theirs_ref, *refs, chunks):
    grad_hidden = refs[:chunks]
    rows_ref, sums_ref = refs[chunks:]
    half = mine_ref.shape[0] // chunks
    core = core_index()
    gains = offsets = None
    for c in range(chunks):
        rows = slice(c * half, (c + 1) * half)
        inputs = x_ref[pl.ds(c * 2 * half + core * half, half), :].astype(WIDE)
        stat, inverse = normalize(inputs)
        back, gain, offset = norm_back(
            mine_ref[rows, :] + theirs_ref[rows, :], stat, inverse, norm_ref[0:1, :]
        )
        rows_ref[rows, :] = grad_hidden[c][...] + back
        gains = gain if gains is None else gains + gain
        offsets = offset if offsets is None else offsets + offset
    sums_ref[0:1, :] = gains
    sums_ref[1:2, :] = offsets


def place_kernel(mine_ref, theirs_ref, out_ref, *, chunks):
    half = mine_ref.shape[0] // chunks
    core = core_index()
    for c in range(chunks):
        rows = slice(c * half, (c + 1) * half)
        out_ref[pl.ds((2 * c + core) * half, half), :] = mine_ref[rows, :].astype(LOW)
        out_ref[pl.ds((2 * c + 1 - core) * half, half), :] = theirs_ref[rows, :].astype(LOW)


def norm_sums_kernel(*refs, chunks):
    input_ref, norms, losses, out_ref = refs[0], refs[1 : 1 + chunks], refs[1 + chunks : -1], refs[-1]
    out_ref[0:2, :] = input_ref[...]
    out_ref[2:6, :] = sum(ref[...] for ref in norms[1:]) + norms[0][...]
    out_ref[6:8, :] = sum(ref[...] for ref in losses[1:]) + losses[0][...]


def copy_kernel(*refs):
    half = len(refs) // 2
    for source, target in zip(refs[:half], refs[half:]):
        target[...] = source[...]


def moment_step(gradient, first_state, second_state):
    first_new = first_decay * first_state + (1.0 - first_decay) * gradient
    second_new = second_decay * second_state + (1.0 - second_decay) * gradient * gradient
    direction = (
        first_new
        / (1.0 - first_decay**STEP)
        / (jnp.sqrt(second_new / (1.0 - second_decay**STEP)) + adam_epsilon)
    )
    return (first_new, second_new, direction)


def total_of(values):
    rows = values.reshape(-1, values.shape[-1])
    return jnp.sum(jnp.sum(rows, axis=0, keepdims=True), axis=1, keepdims=True)


def moments_kernel(master_ref, first_ref, second_ref, squares_ref, *refs, row, regions, counts):
    kept_ref, update_ref, first_new_ref, second_new_ref, table_ref = refs[-5:]
    at = 0
    sizes = []
    for region, count in zip(regions, counts):
        gradient = refs[at][...]
        for term in refs[at + 1 : at + count]:
            gradient = gradient + term[...]
        at += count
        first_new, second_new, direction = moment_step(
            gradient, first_ref[region], second_ref[region]
        )
        first_new_ref[region] = first_new
        second_new_ref[region] = second_new
        master = master_ref[region]
        kept_ref[region] = master
        update = direction + decay_rate * master
        update_ref[region] = update
        sizes.append((total_of(master * master), total_of(update * update)))
    table_ref[...] = squares_ref[...]
    for place, size in ((row, 0), (row + 4, 1)):
        amount = sizes[0][size]
        for other in sizes[1:]:
            amount = amount + other[size]
        table_ref[place : place + 1, :] = jnp.broadcast_to(amount, (1, LANES))


def join_kernel(*refs):
    terms, norms_ref, out_ref = refs[:-2], refs[-2], refs[-1]
    terms = [ref[...] for ref in terms]
    while len(terms) > 1:
        terms = [terms[i] + terms[i + 1] for i in range(0, len(terms), 2)]
    out_ref[:, 0:LANES] = terms[0]
    out_ref[:, LANES:] = norms_ref[...]


def masters_kernel(norm_ref, first_ref, second_ref, *refs, terms, own):
    sums, refs = refs[:terms], refs[terms:]
    masters, updates, outs = refs[:4], refs[4:8], refs[8:12]
    norms_ref, norm_new_ref, first_new_ref, second_new_ref = refs[12:]
    total = sums[0][:, 0:LANES]
    for ref in sums[1:]:
        total = total + ref[:, 0:LANES]
    sizes = jnp.sqrt(total[0:4, :])
    steps = jnp.sqrt(total[4:8, :] + trust_epsilon)
    lane = lax.broadcasted_iota(jnp.int32, (1, 4), 1)
    for place, found in ((0, sizes), (1, steps)):
        row = jnp.zeros((1, 4), WIDE)
        for index in range(4):
            row = jnp.where(lane == index, found[index : index + 1, 0:1], row)
        norms_ref[place : place + 1, :] = row
    ratio = learn_rate * (sizes / steps)
    for index in range(4):
        scale = ratio[index : index + 1, 0:1]
        if len(masters[index].shape) == 3:
            scale = scale.reshape(1, 1, 1)
        outs[index][...] = masters[index][...] - scale * updates[index][...]
    if own % LANES:
        gradient = sums[0][:, LANES:]
        for ref in sums[1:]:
            gradient = gradient + ref[:, LANES:]
        norm_new_ref[...] = gradient
        return
    start = pl.multiple_of(lax.axis_index("dp") * own, own)
    gradient = sums[0][:, pl.ds(LANES + start, own)]
    for ref in sums[1:]:
        gradient = gradient + ref[:, pl.ds(LANES + start, own)]
    first_new, second_new, direction = moment_step(gradient, first_ref[...], second_ref[...])
    first_new_ref[...] = first_new
    second_new_ref[...] = second_new
    norm_new_ref[...] = norm_ref[:, pl.ds(start, own)] - learn_rate * direction


def shards(
    block_input,
    lengths,
    norm_params,
    qkv_weight,
    out_weight,
    up_weight,
    down_weight,
    qkv_first,
    qkv_second,
    out_first,
    out_second,
    up_first,
    up_second,
    down_first,
    down_second,
    norm_first,
    norm_second,
    out_grad,
):
    row_count, width = block_input.shape
    local = qkv_weight.shape[2]
    hidden_units = up_weight.shape[1]
    group_count = lax.axis_size("dp")
    own = width // group_count
    own_start = lax.axis_index("dp") * own
    part = row_count // CHUNKS
    half = part // 2
    chunks = range(CHUNKS)
    bits = list(range(log2_of(group_count)))

    line = Line()
    qkv_parts = jnp.transpose(qkv_weight, (1, 0, 2))
    cosine, sine = rotary_tables(row_count)
    live = Raw(lengths, SMEM)

    weight_shapes = [shaped(3, width, local, kind=LOW), shaped(local, width, kind=LOW)]
    chunk_shapes = [
        shaped(part, width, kind=LOW),
        shaped(part, local, kind=LOW),
        shaped(part, local, kind=LOW),
        shaped(part, local, kind=LOW),
        shaped(part, local, kind=LOW),
        shaped(part, LANES),
        cut(half, width, CUT_ATTENTION),
        shaped(half, width),
    ]
    outs = line.call(
        first_kernel,
        weight_shapes + chunk_shapes,
        [live]
        + [Raw(a, HBM) for a in (block_input, norm_params, cosine, sine, qkv_parts, out_weight)],
        scratch=[
            pltpu.VMEM((part, width), LOW),
            pltpu.VMEM(norm_params.shape, WIDE),
            pltpu.VMEM((part, LANES), WIDE),
            pltpu.VMEM((part, LANES), WIDE),
            pltpu.VMEM((3, width, local), WIDE),
            pltpu.VMEM((local, width), WIDE),
            pltpu.SemaphoreType.DMA((8,)),
        ],
        megabytes=60,
        first=True,
    )
    qkv_low, out_low = outs[:2]
    parts = [outs[2:]]
    branch_terms = [sum_rows(line, parts[0][7], near(parts[0][6]))]
    for c in chunks[1:]:
        before = [p[2] for p in parts] + [p[3] for p in parts]
        parts.append(
            line.call(
                functools.partial(next_kernel, first_row=c * part, part=part),
                chunk_shapes,
                [live, block_input, norm_params, cosine, sine, qkv_low, out_low] + before,
            )
        )
        branch_terms.append(sum_rows(line, parts[c][7], near(parts[c][6])))
    normed_in, query, keys, values, attn, masses, _, _ = zip(*parts)
    up_low = line.call(
        cast_kernel, [shaped(*up_weight.shape, kind=LOW)], [Take(up_weight)]
    )[0]
    down_low = line.call(
        cast_kernel, [shaped(*down_weight.shape, kind=LOW)], [Take(down_weight)]
    )[0]

    branch, hidden, normed_mid, up, active, mlp_terms = [], [], [], [], [], []
    for c in chunks:
        outs = line.call(
            functools.partial(middle_kernel, c * part),
            [shaped(half, width), shaped(half, width), cut(half, width, CUT_MIDDLE)],
            [block_input, norm_params, *branch_terms[c]],
        )
        branch.append(outs[0])
        hidden.append(outs[1])
        other = near(outs[2])
        outs = line.call(
            mlp_kernel,
            [
                shaped(part, width, kind=LOW),
                shaped(part, hidden_units),
                shaped(part, hidden_units, kind=LOW),
                cut(half, width, CUT_MLP),
                shaped(half, width),
            ],
            [outs[2], other, up_low, down_low],
        )
        normed_mid.append(outs[0])
        up.append(outs[1])
        active.append(outs[2])
        mlp_terms.append(sum_rows(line, outs[4], near(outs[3])))

    line.own, line.table = own, jnp.zeros((8, LANES), WIDE)
    along_a, along_b, along_c, along_d = bits, bits, bits, bits
    if len(bits) > 1:
        along_b, along_c, along_d = [1, 0] + bits[2:], bits[1:] + [0], [0] + bits[:0:-1]
    columns = lambda: (slice(None), pl.ds(pl.multiple_of(lax.axis_index("dp") * own, own), own))
    rows = lambda: (pl.ds(pl.multiple_of(lax.axis_index("dp") * own, own), own),)
    part_rows = lambda: (slice(None), *rows())
    mine = lambda array, axis: lax.dynamic_slice_in_dim(array, own_start, own, axis)
    block_rows, loss_sums, grad_final, grad_up_rows, mid_terms = [], [], [], [], []
    grad_hidden, norms_sums, own_back, other_back = [], [], [], []
    flip = lambda array: jnp.transpose(array, (1, 0, 2))
    qkv = Weight(
        line,
        0,
        3,
        owned_parts_kernel,
        lambda: (normed_in, [grad_rows]),
        Take(qkv_parts, (3, own, local), part_rows),
        [flip(qkv_first), flip(qkv_second)],
    )
    out = Weight(
        line,
        1,
        local,
        owned_columns_kernel,
        lambda: (attn, [grad_branch]),
        Take(mine(out_weight, 1)) if own % LANES else Take(out_weight, (local, own), columns),
        [out_first, out_second],
    )
    up_matrix = Weight(
        line,
        2,
        hidden_units,
        owned_rows_kernel,
        lambda: (normed_mid, grad_up_rows),
        Take(up_weight, (own, hidden_units), rows),
        [up_first, up_second],
    )
    down = Weight(
        line,
        3,
        hidden_units,
        owned_columns_kernel,
        lambda: (active, sum(grad_final, [])),
        Take(mine(down_weight, 1))
        if own % LANES
        else Take(down_weight, (hidden_units, own), columns),
        [down_first, down_second],
    )
    d0 = down.piece(0, 8, 8, along_a)
    u0 = up_matrix.piece(0, 8, 8, along_b)
    q0 = qkv.piece(0, 1, 3, along_b)
    q1 = qkv.piece(1, 2, 3, along_a)
    q2 = qkv.piece(2, 3, 3, along_d)
    o0 = out.piece(0, 1, 1, along_a)

    def loss(c):
        outs = line.call(
            functools.partial(loss_kernel, c * part),
            [cut(half, width, 1), cut(half, width, CUT_LOSS), shaped(2, width)],
            [out_grad, norm_params, hidden[c], *mlp_terms[c]],
        )
        block_rows.append(outs[0])
        loss_sums.append(outs[2])
        grad_final.extend([outs[1], near(outs[1])])

    def mlp_back(c):
        outs = line.call(
            mlp_back_kernel,
            [
                shaped(part, width, kind=LOW),
                shaped(part, hidden_units, kind=LOW),
                cut(half, width, CUT_MLP if c < CHUNKS - 1 else CUT_MID),
                shaped(half, width),
            ],
            [*grad_final[-2:], up[c], up_low, down_low],
        )
        grad_up_rows.append(outs[1])
        mid_terms.append((outs[3], near(outs[2])))

    def sum_mid(c):
        mid_terms[c] = sum_rows(line, *mid_terms[c])

    def norms(c):
        outs = line.call(
            functools.partial(norms_back_kernel, c * part),
            [shaped(half, width), cut(half, width, CUT_NORMS), shaped(4, width)],
            [out_grad, norm_params, hidden[c], branch[c], *mid_terms[c]],
        )
        grad_hidden.append(outs[0])
        norms_sums.append(outs[2])
        own_back.append(outs[1])
        other_back.append(near(outs[1]))

    def norms_before():
        for c in chunks[:-1]:
            norms(c)

    def attention_back():
        return line.call(
            functools.partial(attention_back_kernel, chunks=CHUNKS),
            [shaped(row_count, width, kind=LOW), shaped(row_count, 3 * local, kind=LOW)],
            [live, out_low, cosine, sine, *own_back, *other_back, *query, *keys, *values, *masses],
            scratch=[pltpu.VMEM((row_count, local), WIDE), pltpu.VMEM((row_count, local), WIDE)],
        )

    def input_back():
        return line.call(
            functools.partial(input_back_kernel, chunks=CHUNKS),
            [cut(row_count // 2, width, CUT_BACK), shaped(row_count // 2, width)],
            [grad_rows, qkv_low],
        )

    def input_norm():
        return line.call(
            functools.partial(input_norm_kernel, chunks=CHUNKS),
            [cut(row_count // 2, width, CUT_INPUT), shaped(2, width)],
            [block_input, norm_params, *in_terms, *grad_hidden],
        )

    def place(blocks):
        return line.call(
            functools.partial(place_kernel, chunks=CHUNKS),
            [shaped(row_count, width, kind=LOW)],
            [blocks, near(blocks)],
        )[0]

    def norm_sums():
        return line.call(
            functools.partial(norm_sums_kernel, chunks=CHUNKS),
            [shaped(8, width)],
            [input_sums, *norms_sums, *loss_sums],
        )[0]

    def sum_norms():
        return line.call(
            sum_kernel, [shaped(8, width)], [grad_norms, swap(grad_norms, "tensor", 1)]
        )[0]

    last = CHUNKS - 1
    for c in chunks[:-1]:
        loss(c)
        mlp_back(c)
        sum_mid(c)
    loss(last)
    d0.start()
    mlp_back(last)
    u0.start()
    up_matrix.hold()
    sum_mid(last)
    norms_before()
    norms(last)
    down.hold()
    block_output = place(sum(block_rows, []))
    grad_branch, grad_rows = attention_back()
    send, keep = input_back()
    q2.start()
    d0.advance()
    q0.start()
    qkv.hold()
    out.hold()
    q1.start()
    o0.start()
    q2.advance()
    u0.advance()
    in_terms = sum_rows(line, keep, near(send))
    d0.advance()
    u0.advance()
    q2.advance()
    q1.advance()
    input_rows, input_sums = input_norm()
    down.moments()
    grad_norms = norm_sums()
    q1.advance()
    grad_norms = sum_norms()
    q0.advance()
    o0.advance()
    q0.advance()
    o0.advance()
    out.moments()
    up_matrix.moments()
    input_grad = place(input_rows)
    qkv.stage()
    qkv.moments()

    tensor_bits = log2_of(lax.axis_size("tensor"))
    found = line.table
    for start in range(0, tensor_bits, 2):
        terms = sum_terms(found, "tensor", start, min(2, tensor_bits - start))
        if start + 2 >= tensor_bits:
            found = line.call(join_kernel, [shaped(8, LANES + width)], [*terms, grad_norms])[0]
        else:
            found = line.call(pairs_kernel, [shaped(8, LANES)], terms)[0]
    for start in range(0, len(bits), 2):
        terms = sum_terms(found, "dp", start, min(2, len(bits) - start))
        if start + 2 < len(bits) or len(terms) > 2:
            found = line.call(pairs_kernel, [shaped(8, LANES + width)], terms)[0]
            terms = [found]
    weights = (qkv, out, up_matrix, down)
    outs = line.call(
        functools.partial(masters_kernel, terms=len(terms), own=own),
        [shaped(*weight.kept.shape) for weight in weights]
        + [shaped(2, 4), shaped(8, width if own % LANES else own), shaped(8, own), shaped(8, own)],
        [
            norm_params,
            norm_first,
            norm_second,
            *terms,
            *[weight.kept for weight in weights],
            *[weight.update for weight in weights],
        ],
    )
    matrix_norms, norm_new, norm_first_new, norm_second_new = outs[4:]
    if own % LANES:
        norm_first_new, norm_second_new, direction = moment_step(
            mine(norm_new, 1), norm_first, norm_second
        )
        norm_new = mine(norm_params, 1) - learn_rate * direction
    return (
        block_output,
        input_grad,
        flip(outs[0]),
        flip(qkv.first_new),
        flip(qkv.second_new),
        outs[1],
        out.first_new,
        out.second_new,
        outs[2],
        up_matrix.first_new,
        up_matrix.second_new,
        outs[3],
        down.first_new,
        down.second_new,
        norm_new,
        norm_first_new,
        norm_second_new,
        matrix_norms,
    )


def solution(mesh):
    in_specs = (
        P("dp", None),
        P("dp"),
        P(),
        P(None, None, "tensor"),
        P("tensor", None),
        P(None, "tensor"),
        P("tensor", None),
        P("dp", None, "tensor"),
        P("dp", None, "tensor"),
        P("tensor", "dp"),
        P("tensor", "dp"),
        P("dp", "tensor"),
        P("dp", "tensor"),
        P("tensor", "dp"),
        P("tensor", "dp"),
        P(None, "dp"),
        P(None, "dp"),
        P("dp", None),
    )
    out_specs = (
        P("dp", None),
        P("dp", None),
        P("dp", None, "tensor"),
        P("dp", None, "tensor"),
        P("dp", None, "tensor"),
        P("tensor", "dp"),
        P("tensor", "dp"),
        P("tensor", "dp"),
        P("dp", "tensor"),
        P("dp", "tensor"),
        P("dp", "tensor"),
        P("tensor", "dp"),
        P("tensor", "dp"),
        P("tensor", "dp"),
        P(None, "dp"),
        P(None, "dp"),
        P(None, "dp"),
        P(),
    )
    return jax.shard_map(shards, mesh=mesh, in_specs=in_specs, out_specs=out_specs, check_vma=False)
```

```python
import functools

import jax
import jax.numpy as jnp
import numpy as np
from jax import lax
from jax.experimental import pallas as pl
from jax.experimental.pallas import tpu as pltpu
from jax.sharding import PartitionSpec as P

HEAD_DIM = 64
STEP = 10
CHUNKS = 2
LANES = 128

norm_epsilon = 1e-05
rotary_base = 10000.0
mask_fill = -1000000000.0
first_decay = 0.9
second_decay = 0.999
adam_epsilon = 1e-06
trust_epsilon = 1e-06
decay_rate = 0.01
learn_rate = 0.25

CUT_ATTENTION, CUT_MIDDLE, CUT_MLP, CUT_LOSS = 4, 4, 4, 2
CUT_RELAY = 2
CUT_MID, CUT_NORMS, CUT_BACK, CUT_INPUT, CUT_OUTPUT = 4, 1, 4, 1, 1

LOW = jnp.bfloat16
WIDE = jnp.float32
VMEM = pl.BlockSpec(memory_space=pltpu.VMEM)
SMEM = pl.BlockSpec(memory_space=pltpu.SMEM)
HBM = pl.BlockSpec(memory_space=pltpu.HBM)


def log2_of(count):
    bits = 0
    while (1 << bits) < count:
        bits += 1
    return bits


def swap(values, axis, distance):
    count = lax.axis_size(axis)
    return lax.ppermute(values, axis, [(i, i ^ distance) for i in range(count)])


class Route:
    def __init__(self, order, steps, held):
        self.order, self.steps, self.held = order, steps, held


HALF, CROSS, BACK = range(3)


def apart(count, distance, among=None):
    return [(i, i ^ distance) for i in (range(count) if among is None else among)]


def outside(rank):
    place = lax.div(rank, 2)
    return (place == 0) | (place == 3)


def line_chunks(rank):
    place = lax.div(rank, 2)
    beside, side = lax.bitwise_xor(place, 1), lax.div(place, 2)
    near, far = (place, beside), (2 - side, 3 - 3 * side)
    end = outside(rank)
    keep = [jnp.where(end, a, b) for a, b in zip(near, far)]
    send = [jnp.where(end, a, b) for a, b in zip(far, (beside, place))]
    return keep, send


def routes(count):
    if count == 8:

        def across_first(rank):
            keep, send = line_chunks(rank)
            row = lax.rem(rank, 2)
            return [place * 2 + y for y in (row, 1 - row) for place in keep + send]

        def along_first(rank):
            keep, send = line_chunks(rank)
            row = lax.rem(rank, 2)
            return [place * 2 + y for part in (keep, send) for y in (row, 1 - row) for place in part]

        def joined(rank):
            keep, _ = line_chunks(rank)
            row = lax.rem(rank, 2)
            return [place * 2 + y for y in (row, 1 - row) for place in keep]

        across = (HALF, apart(8, 1))
        along, back = (HALF, apart(8, 2)), (BACK, apart(8, 2))
        cross = (CROSS, apart(8, 6, range(2, 6)))
        return (
            Route(across_first, [across, along, cross, back], 8),
            Route(along_first, [along, across, cross, back], 8),
            Route(joined, [across, cross, back], 4),
        )
    order = [0]
    bits = range(log2_of(count))
    for bit in reversed(bits):
        order = order + [distance ^ (1 << bit) for distance in order]
    found = Route(
        lambda rank: [lax.bitwise_xor(rank, distance) for distance in order],
        [(HALF, apart(count, 1 << bit)) for bit in bits],
        count,
    )
    return found, found, found


def normalize(values):
    center = values - jnp.mean(values, axis=-1, keepdims=True)
    inverse = lax.rsqrt(jnp.mean(center * center, axis=-1, keepdims=True) + norm_epsilon)
    return center * inverse, inverse


def norm_back(incoming, normed, inverse, gain):
    scaled = incoming * gain
    inner = (
        scaled
        - jnp.mean(scaled, axis=-1, keepdims=True)
        - normed * jnp.mean(scaled * normed, axis=-1, keepdims=True)
    )
    gain_grad = jnp.sum(incoming * normed, axis=0, keepdims=True)
    return inner * inverse, gain_grad, jnp.sum(incoming, axis=0, keepdims=True)


def rotary_tables(length):
    half = HEAD_DIM // 2
    lane = np.arange(LANES)
    frequency = (rotary_base ** (-((lane % half).astype(np.float32) * 2.0 / HEAD_DIM))).astype(np.float32)
    angles = np.arange(length, dtype=np.float32)[:, None] * frequency[None, :]
    sign = np.where(lane % HEAD_DIM < half, -1.0, 1.0)
    cosine = np.cos(angles.astype(np.float64)).astype(np.float32)
    sine = (np.sin(angles.astype(np.float64)) * sign[None, :]).astype(np.float32)
    return jnp.asarray(cosine), jnp.asarray(sine)


def turn(values, cosine, sine):
    half = HEAD_DIM // 2
    lane = lax.broadcasted_iota(jnp.int32, (1, LANES), 1)
    first = lax.rem(lane, HEAD_DIM) < half
    tiles = []
    for start in range(0, values.shape[1], LANES):
        tile = values[:, start : start + LANES]
        other = jnp.where(
            first, pltpu.roll(tile, LANES - half, 1), pltpu.roll(tile, half, 1)
        )
        tiles.append(tile * cosine + other * sine)
    return tiles[0] if len(tiles) == 1 else jnp.concatenate(tiles, axis=1)


def gelu_mass(up):
    return 0.5 * (1.0 + lax.erf(up * (0.5**0.5)))


def gelu_slope(up, mass):
    return mass + up * jnp.exp(-0.5 * up * up) * float((2.0 * np.pi) ** -0.5)


def dot(left, right):
    return jnp.dot(left, right, preferred_element_type=WIDE)


def dot_rows(left, right):
    return lax.dot_general(left, right, (((0,), (0,)), ((), ())), preferred_element_type=WIDE)


def dot_wide(left, right):
    return lax.dot_general(left, right, (((1,), (1,)), ((), ())), preferred_element_type=WIDE)


def of_head(values, head):
    lane = lax.broadcasted_iota(jnp.int32, (1, values.shape[1]), 1)
    mine = (lane >= head * HEAD_DIM) & (lane < (head + 1) * HEAD_DIM)
    return jnp.where(mine, values, jnp.zeros_like(values))


def core_index():
    return lax.rem(lax.axis_index("tensor"), 2)


def shaped(*shape, kind=WIDE):
    return jax.ShapeDtypeStruct(shape, kind)


def cut(rows, width, count=4):
    return [shaped(rows // count, width)] * count


def near(values):
    return [swap(piece, "tensor", 1) for piece in values]


class Take:
    def __init__(self, array, shape=None, index=None):
        self.array = array
        self.shape = array.shape if shape is None else shape
        self.index = index


class Raw:
    def __init__(self, array, spec):
        self.array = array
        self.spec = spec


class Rows:
    def __init__(self, refs):
        self.refs = refs
        self.step = refs[0].shape[0]
        self.shape = (self.step * len(refs), refs[0].shape[1])

    def spans(self, key):
        first, last = 0, self.shape[0]
        if key is not Ellipsis and key[0] != slice(None):
            first, last = key[0].start, key[0].stop
        for place, ref in enumerate(self.refs):
            start, stop = max(first, place * self.step), min(last, (place + 1) * self.step)
            if start < stop:
                inside = slice(start - place * self.step, stop - place * self.step)
                yield ref, inside, slice(start - first, stop - first)

    def __getitem__(self, key):
        pieces = [ref[inside, :] for ref, inside, _ in self.spans(key)]
        return pieces[0] if len(pieces) == 1 else jnp.concatenate(pieces, axis=0)

    def __setitem__(self, key, value):
        for ref, inside, outside in self.spans(key):
            ref[inside, :] = value[outside]


class Line:
    def __init__(self):
        self.token = jnp.zeros((8, LANES), WIDE)

    def call(self, kernel, outs, args, scratch=(), megabytes=12, first=False):
        arrays, specs, buffers, layout, takes = [], [], [], [], []
        for arg in args:
            if isinstance(arg, Take):
                layout.append(0)
                takes.append((len(arrays), arg))
                arrays.append(arg.array)
                specs.append(HBM)
                buffers.append(pltpu.VMEM(arg.shape, arg.array.dtype))
            elif isinstance(arg, Raw):
                layout.append(0)
                arrays.append(arg.array)
                specs.append(arg.spec)
            elif isinstance(arg, (list, tuple)):
                layout.append(len(arg))
                arrays += arg
                specs += [VMEM] * len(arg)
            else:
                layout.append(0)
                arrays.append(arg)
                specs.append(VMEM)
        if takes:
            buffers.append(pltpu.SemaphoreType.DMA((len(takes),)))
        token = [] if first else [self.token]
        out_layout = [len(out) if isinstance(out, list) else 0 for out in outs]
        out_shapes = [o for out in outs for o in (out if isinstance(out, list) else [out])]

        def joined(refs, layout):
            refs = list(refs)
            return [
                Rows([refs.pop(0) for _ in range(count)]) if count else refs.pop(0)
                for count in layout
            ]

        def body(*refs):
            inputs = list(refs[: len(arrays)])
            rest = refs[len(arrays) + len(token) :]
            results, rest = rest[: len(out_shapes)], rest[len(out_shapes) + len(token) :]
            own, rest = rest[: len(scratch)], rest[len(scratch) :]
            copies = []
            for place, (i, take) in enumerate(takes):
                source = inputs[i]
                if take.index is not None:
                    source = source.at[take.index()]
                copies.append(pltpu.make_async_copy(source, rest[place], rest[-1].at[place]))
                inputs[i] = rest[place]
            for copy in copies:
                copy.start()
            for copy in copies:
                copy.wait()
            kernel(*joined(inputs, layout), *joined(results, out_layout), *own)

        results = pl.pallas_call(
            body,
            out_shape=(*out_shapes, *[shaped(8, LANES) for _ in token]),
            in_specs=[*specs, *[HBM for _ in token]],
            out_specs=tuple([VMEM] * len(out_shapes) + [HBM for _ in token]),
            scratch_shapes=[*scratch, *buffers],
            input_output_aliases={len(arrays): len(out_shapes)} if token else {},
            compiler_params=pltpu.CompilerParams(vmem_limit_bytes=megabytes * 1024 * 1024),
            cost_estimate=pl.CostEstimate(flops=0, bytes_accessed=0, transcendentals=0),
        )(*arrays, *token)
        found = list(results)
        if token:
            self.token = found.pop()
        return [
            [found.pop(0) for _ in range(count)] if count else found.pop(0) for count in out_layout
        ]


def sum_kernel(*refs):
    total = refs[0][...]
    for ref in refs[1:-1]:
        total = total + ref[...]
    refs[-1][...] = total


def pairs_kernel(*refs):
    terms = [ref[...] for ref in refs[:-1]]
    while len(terms) > 1:
        terms = [terms[i] + terms[i + 1] for i in range(0, len(terms), 2)]
    refs[-1][...] = terms[0]


def sum_rows(line, keep, arrived, count=1):
    mine, theirs = keep, arrived
    for bit in range(1, log2_of(lax.axis_size("tensor"))):
        mine = line.call(sum_kernel, [cut(*keep.shape, count)], [mine, theirs])[0]
        theirs = [swap(piece, "tensor", 1 << bit) for piece in mine]
    return mine, theirs


def sum_terms(values, axis, start, taken):
    return [values] + [swap(values, axis, distance << start) for distance in range(1, 1 << taken)]


def gathered(values, crossed):
    if crossed:
        first = jnp.where(outside(lax.axis_index("dp")), values[0], values[1])
        values = [first, *values[2:]]
    total = values[0]
    for value in values[1:]:
        total = total + value
    return total


def gather_kernel(*refs, crossed):
    refs[-1][...] = gathered([ref[...] for ref in refs[:-1]], crossed)


class Piece:
    def __init__(self, weight, window, route):
        self.weight, self.window, self.route = weight, window, route
        self.terms, self.stage, self.crossed = [], 0, False

    def exchange(self, values):
        self.terms.append(lax.ppermute(values, "dp", self.route.steps[self.stage][1]))
        self.stage += 1

    def start(self):
        self.size = self.route.held // 2
        self.exchange(self.weight.products([self], True)[0])

    def sum_of(self, first, size):
        shape = (size,) + self.terms[0].shape[1:]
        index = lambda: (pl.ds(first, size),)
        return self.weight.line.call(
            functools.partial(gather_kernel, crossed=self.crossed),
            [shaped(*shape)],
            [Take(term, shape, index) for term in self.terms],
        )[0]

    def advance(self):
        if self.stage == len(self.route.steps):
            return
        if self.route.steps[self.stage][0] == CROSS:
            self.terms = [self.sum_of(0, self.size)]
            self.exchange(self.terms[0])
            self.crossed = True
        else:
            self.size //= 2
            self.exchange(self.sum_of(self.size, self.size))


class Weight:
    tables = {}

    def __init__(self, line, row, size, kernel, factors, master, states):
        self.line, self.row, self.size, self.kernel = line, row, size, kernel
        self.factors, self.master, self.states = factors, master, states
        self.pieces = []

    def piece(self, first, last, count, route):
        found = Piece(self, (self.size * first // count, self.size * last // count), route)
        self.pieces.append(found)
        return found

    def products(self, pieces, send):
        own = self.line.own
        return owner_products(self.line, self.kernel, *self.factors(), pieces, own, send)

    def hold(self):
        for piece, keep in zip(self.pieces, self.products(self.pieces, False)):
            piece.terms.insert(0, keep)

    def stage(self):
        before = [self.master, *[Take(state) for state in self.states]]
        terms = [
            Take(term, term.shape[1:], lambda: (0,))
            for piece in self.pieces
            for term in piece.terms[:-1]
        ]
        crossed = [piece.crossed for piece in self.pieces]
        shapes = [shaped(*piece.terms[0].shape[1:]) for piece in self.pieces]
        counts = [len(piece.terms) - 1 for piece in self.pieces]
        self.master, *outs = self.line.call(
            functools.partial(stage_kernel, counts=counts, crossed=crossed),
            [shaped(*self.master.shape)] * 3 + shapes,
            before + terms,
        )
        self.states = outs[:2]
        self.partial = outs[2:]

    def moments(self):
        for piece in self.pieces:
            while piece.stage < len(piece.route.steps):
                piece.advance()
        everything = slice(None)
        if self.kernel is owned_rows_kernel:
            regions = [(everything, slice(*piece.window)) for piece in self.pieces]
        else:
            regions = [(slice(*piece.window),) for piece in self.pieces]
        late = not isinstance(self.master, Take)
        states, terms, counts, crossed = self.states, [], [], []
        if not late:
            states = [Take(state) for state in states]
        for index, piece in enumerate(self.pieces):
            found = [self.partial[index]] if late else []
            for term in piece.terms[-1:] if late else piece.terms:
                found.append(Take(term, term.shape[1:], lambda: (0,)))
            terms += found
            counts.append(len(found))
            crossed.append(piece.crossed and not late)
        shape = shaped(*self.master.shape)
        outs = self.line.call(
            functools.partial(
                moments_kernel,
                row=self.row,
                regions=regions,
                counts=counts,
                crossed=crossed,
                late=late,
            ),
            [shape, shape] + [shape] * (1 if late else 2) + [shaped(8, LANES)],
            [self.master, *states, self.line.table, *terms],
            megabytes=16,
        )
        self.kept, self.update, *self.found, self.line.table = outs
        if not late:
            self.first_new, self.second_new = self.found

    def finish(self):
        self.first_new, self.second_new = self.line.call(
            finish_kernel, [shaped(*self.master.shape)] * 2, [*self.found, *self.states]
        )


def project(normed, weights, cosine, sine):
    query = turn(dot(normed, weights[0]), cosine, sine).astype(LOW)
    keys = turn(dot(normed, weights[1]), cosine, sine).astype(LOW)
    return query, keys, dot(normed, weights[2]).astype(LOW)


def attend(query, keys, values, first_row, live_len):
    rows, reach = query.shape[0], keys.shape[0]
    row = first_row + lax.broadcasted_iota(jnp.int32, (rows, reach), 0)
    column = lax.broadcasted_iota(jnp.int32, (rows, reach), 1)
    visible = (column <= row) & (column < live_len)
    lane = lax.broadcasted_iota(jnp.int32, (1, LANES), 1)
    mixed = jnp.zeros((rows, query.shape[1]), WIDE)
    masses = jnp.zeros((rows, LANES), WIDE)
    for head in range(query.shape[1] // HEAD_DIM):
        scores = dot_wide(of_head(query, head), keys) * HEAD_DIM ** (-0.5)
        scores = jnp.where(visible, scores, mask_fill)
        top = jnp.max(scores, axis=-1, keepdims=True)
        expo = jnp.exp(scores - top)
        total = jnp.sum(expo, axis=-1, keepdims=True)
        probs = (expo * (1.0 / total)).astype(LOW)
        mixed = mixed + dot(probs, of_head(values, head))
        masses = jnp.where(lane == head, top + jnp.log(total), masses)
    live = first_row + lax.broadcasted_iota(jnp.int32, (rows, 1), 0) < live_len
    return jnp.where(live, mixed, 0.0).astype(LOW), masses


def split_rows(left_ref, right, send_ref, keep_ref, how):
    half = send_ref.shape[0]
    core = core_index()
    send_ref[...] = how(left_ref[pl.ds((1 - core) * half, half), :], right)
    keep_ref[...] = how(left_ref[pl.ds(core * half, half), :], right)


def first_kernel(
    live_ref, x_any, norm_any, cos_any, sin_any, qkv_any, out_any,
    qkv_low_ref, out_low_ref, normed_ref, q_ref, k_ref, v_ref, attn_ref, mass_ref, send_ref, keep_ref,
    x_ref, norm_ref, cos_ref, sin_ref, qkv_in, out_in, arrived,
):
    part = x_ref.shape[0]
    sources = [x_any.at[pl.ds(0, part)], norm_any, cos_any.at[pl.ds(0, part)], sin_any.at[pl.ds(0, part)]]
    targets = [x_ref, norm_ref, cos_ref, sin_ref]
    sources += [qkv_any.at[j] for j in range(3)] + [out_any]
    targets += [qkv_in.at[j] for j in range(3)] + [out_in]
    copies = [
        pltpu.make_async_copy(source, target, arrived.at[i])
        for i, (source, target) in enumerate(zip(sources, targets))
    ]
    for copy in copies:
        copy.start()
    copies[0].wait()
    copies[1].wait()
    stat, _ = normalize(x_ref[...].astype(WIDE))
    normed = (stat * norm_ref[0:1, :] + norm_ref[1:2, :]).astype(LOW)
    normed_ref[...] = normed
    copies[2].wait()
    copies[3].wait()
    weights = []
    for j in range(3):
        copies[4 + j].wait()
        weights.append(qkv_in[j].astype(LOW))
        qkv_low_ref[j] = weights[j]
    query, keys, values = project(normed, weights, cos_ref[...], sin_ref[...])
    q_ref[...], k_ref[...], v_ref[...] = query, keys, values
    attn_ref[...], mass_ref[...] = attend(query, keys, values, 0, live_ref[0])
    copies[7].wait()
    out_low = out_in[...].astype(LOW)
    out_low_ref[...] = out_low
    split_rows(attn_ref, out_low, send_ref, keep_ref, dot)


def next_kernel(
    live_ref, x_ref, norm_ref, cos_ref, sin_ref, qkv_low_ref, out_low_ref, *refs, first_row, part
):
    earlier = first_row // part
    rows = slice(first_row, first_row + part)
    k_before, v_before = refs[:earlier], refs[earlier : 2 * earlier]
    normed_ref, q_ref, k_ref, v_ref, attn_ref, mass_ref, send_ref, keep_ref = refs[2 * earlier :]
    stat, _ = normalize(x_ref[rows, :].astype(WIDE))
    normed = (stat * norm_ref[0:1, :] + norm_ref[1:2, :]).astype(LOW)
    normed_ref[...] = normed
    weights = [qkv_low_ref[j] for j in range(3)]
    query, keys, values = project(normed, weights, cos_ref[rows, :], sin_ref[rows, :])
    q_ref[...], k_ref[...], v_ref[...] = query, keys, values
    keys = jnp.concatenate([ref[...] for ref in k_before] + [keys], axis=0)
    values = jnp.concatenate([ref[...] for ref in v_before] + [values], axis=0)
    attn_ref[...], mass_ref[...] = attend(query, keys, values, first_row, live_ref[0])
    split_rows(attn_ref, out_low_ref[...], send_ref, keep_ref, dot)


def cast_kernel(wide_ref, low_ref):
    low_ref[...] = wide_ref[...].astype(LOW)


def middle_kernel(
    first_row, x_ref, norm_ref, mine_ref, theirs_ref, branch_ref, hidden_ref, *normed_refs
):
    half = mine_ref.shape[0]
    branch = mine_ref[...] + theirs_ref[...]
    branch_ref[...] = branch
    stat, _ = normalize(branch)
    inputs = x_ref[pl.ds(first_row + core_index() * half, half), :].astype(WIDE)
    hidden = inputs + stat * norm_ref[2:3, :] + norm_ref[3:4, :]
    hidden_ref[...] = hidden
    stat, _ = normalize(hidden)
    normed = stat * norm_ref[4:5, :] + norm_ref[5:6, :]
    for normed_ref in normed_refs:
        normed_ref[...] = normed


def mlp_kernel(own_ref, other_ref, up_w_ref, down_w_ref, normed_ref, up_ref, active_ref, send_ref, keep_ref):
    half = own_ref.shape[0]
    normed = jnp.concatenate([own_ref[...].astype(LOW), other_ref[...].astype(LOW)], axis=0)
    normed_ref[...] = normed
    step = min(256, up_w_ref.shape[1])
    total = None
    for start in range(0, up_w_ref.shape[1], step):
        block = slice(start, start + step)
        up = dot(normed, up_w_ref[:, block])
        up_ref[:, block] = up
        active = (up * gelu_mass(up)).astype(LOW)
        active_ref[:, block] = active
        product = dot(active, down_w_ref[block, :])
        total = product if total is None else total + product
    keep_ref[...] = total[:half]
    send_ref[...] = total[half:]


def again_kernel(own_ref, other_ref, up_w_ref, normed_ref, active_ref, slope_ref):
    normed = jnp.concatenate([own_ref[...].astype(LOW), other_ref[...].astype(LOW)], axis=0)
    normed_ref[...] = normed
    step = min(256, up_w_ref.shape[1])
    for start in range(0, up_w_ref.shape[1], step):
        block = slice(start, start + step)
        up = dot(normed, up_w_ref[:, block])
        mass = gelu_mass(up)
        active_ref[:, block] = (up * mass).astype(LOW)
        slope_ref[:, block] = gelu_slope(up, mass)


def back_again_kernel(own_ref, other_ref, slope_ref, down_w_ref, grad_mlp_ref, grad_up_ref):
    grad_mlp = jnp.concatenate([own_ref[...].astype(LOW), other_ref[...].astype(LOW)], axis=0)
    grad_mlp_ref[...] = grad_mlp
    step = min(256, slope_ref.shape[1])
    for start in range(0, slope_ref.shape[1], step):
        block = slice(start, start + step)
        grad_up = dot_wide(grad_mlp, down_w_ref[block, :]) * slope_ref[:, block]
        grad_up_ref[:, block] = grad_up.astype(LOW)


def loss_kernel(
    first_row, grad_ref, norm_ref, hidden_ref, mine_ref, theirs_ref, block_ref, sums_ref, *back_refs
):
    half = mine_ref.shape[0]
    stat, inverse = normalize(mine_ref[...] + theirs_ref[...])
    block_ref[...] = hidden_ref[...] + stat * norm_ref[6:7, :] + norm_ref[7:8, :]
    incoming = grad_ref[pl.ds(first_row + core_index() * half, half), :].astype(WIDE)
    back, gain, offset = norm_back(incoming, stat, inverse, norm_ref[6:7, :])
    for back_ref in back_refs:
        back_ref[...] = back
    sums_ref[0:1, :] = gain
    sums_ref[1:2, :] = offset


def mlp_back_kernel(
    own_ref, other_ref, up_ref, up_w_ref, down_w_ref, grad_mlp_ref, grad_up_ref, send_ref, keep_ref
):
    half = own_ref.shape[0]
    grad_mlp = jnp.concatenate([own_ref[...].astype(LOW), other_ref[...].astype(LOW)], axis=0)
    grad_mlp_ref[...] = grad_mlp
    step = min(256, up_w_ref.shape[1])
    total = None
    for start in range(0, up_w_ref.shape[1], step):
        block = slice(start, start + step)
        up = up_ref[:, block]
        slope = gelu_slope(up, gelu_mass(up))
        grad_up = (dot_wide(grad_mlp, down_w_ref[block, :]) * slope).astype(LOW)
        grad_up_ref[:, block] = grad_up
        product = dot_wide(grad_up, up_w_ref[:, block])
        total = product if total is None else total + product
    keep_ref[...] = total[:half]
    send_ref[...] = total[half:]


def norms_back_kernel(
    first_row, grad_ref, norm_ref, hidden_ref, branch_ref, mine_ref, theirs_ref,
    grad_hidden_ref, back_ref, sums_ref,
):
    half = mine_ref.shape[0]
    stat, inverse = normalize(hidden_ref[...])
    back, gain, offset = norm_back(
        mine_ref[...] + theirs_ref[...], stat, inverse, norm_ref[4:5, :]
    )
    incoming = grad_ref[pl.ds(first_row + core_index() * half, half), :].astype(WIDE)
    grad_hidden = incoming + back
    grad_hidden_ref[...] = grad_hidden
    sums_ref[2:3, :] = gain
    sums_ref[3:4, :] = offset
    stat, inverse = normalize(branch_ref[...])
    back, gain, offset = norm_back(grad_hidden, stat, inverse, norm_ref[2:3, :])
    back_ref[...] = back
    sums_ref[0:1, :] = gain
    sums_ref[1:2, :] = offset


def attention_back_kernel(live_ref, out_low_ref, cos_ref, sin_ref, *refs, chunks):
    groups = [refs[i * chunks : (i + 1) * chunks] for i in range(6)]
    own, other, query_refs, key_refs, value_refs, mass_refs = groups
    grad_branch_ref, rows_ref = refs[6 * chunks : 6 * chunks + 2]
    keys_sum, values_sum = refs[6 * chunks + 2 :]
    half = own[0].shape[0]
    part = 2 * half
    core = core_index()
    live_len = live_ref[0]
    local = rows_ref.shape[1] // 3
    heads = local // HEAD_DIM
    for c in range(chunks):
        grad_branch_ref[pl.ds(c * part + core * half, half), :] = own[c][...].astype(LOW)
        grad_branch_ref[pl.ds(c * part + (1 - core) * half, half), :] = other[c][...].astype(LOW)
    keys_all = jnp.concatenate([ref[...] for ref in key_refs], axis=0)
    values_all = jnp.concatenate([ref[...] for ref in value_refs], axis=0)
    for c in range(chunks):
        reach = (c + 1) * part
        first_row = c * part
        row = first_row + lax.broadcasted_iota(jnp.int32, (part, reach), 0)
        column = lax.broadcasted_iota(jnp.int32, (part, reach), 1)
        visible = (column <= row) & (column < live_len)
        live = first_row + lax.broadcasted_iota(jnp.int32, (part, 1), 0) < live_len
        grad_attn = dot_wide(grad_branch_ref[first_row : first_row + part, :], out_low_ref[...])
        grad_mixed = jnp.where(live, grad_attn, 0.0).astype(LOW)
        query, masses = query_refs[c][...], mass_refs[c][...]
        keys, values = keys_all[:reach], values_all[:reach]
        grad_query = jnp.zeros((part, local), WIDE)
        grad_keys = jnp.zeros((reach, local), WIDE)
        grad_values = jnp.zeros((reach, local), WIDE)
        for head in range(heads):
            query_h, grad_h = of_head(query, head), of_head(grad_mixed, head)
            scores = dot_wide(query_h, keys) * HEAD_DIM ** (-0.5)
            scores = jnp.where(visible, scores, mask_fill)
            probs = jnp.exp(scores - masses[:, head : head + 1])
            grad_values = grad_values + dot_rows(probs.astype(LOW), grad_h)
            grad_probs = dot_wide(grad_h, values)
            inner = jnp.sum(grad_probs * probs, axis=-1, keepdims=True)
            grad_scores = (probs * (grad_probs - inner)).astype(LOW)
            grad_query = grad_query + dot(grad_scores, of_head(keys, head))
            grad_keys = grad_keys + dot_rows(grad_scores, query_h)
        cosine = cos_ref[first_row : first_row + part, :]
        sine = sin_ref[first_row : first_row + part, :]
        grad_query = turn(grad_query * HEAD_DIM ** (-0.5), cosine, -sine)
        rows_ref[first_row : first_row + part, 0:local] = grad_query.astype(LOW)
        if c == 0:
            keys_sum[0:reach, :] = grad_keys
            values_sum[0:reach, :] = grad_values
        else:
            keys_sum[0:first_row, :] += grad_keys[:first_row]
            keys_sum[first_row:reach, :] = grad_keys[first_row:]
            values_sum[0:first_row, :] += grad_values[:first_row]
            values_sum[first_row:reach, :] = grad_values[first_row:]
    grad_keys = turn(keys_sum[...] * HEAD_DIM ** (-0.5), cos_ref[...], -sin_ref[...])
    rows_ref[:, local : 2 * local] = grad_keys.astype(LOW)
    rows_ref[:, 2 * local : 3 * local] = values_sum[...].astype(LOW)


def picked_columns(refs, chunks, own):
    blocks = []
    for chunk in chunks:
        start = pl.multiple_of(chunk * own, own)
        pieces = [ref[:, pl.ds(start, own)].astype(LOW) for ref in refs]
        blocks.append(pieces[0] if len(pieces) == 1 else jnp.concatenate(pieces, axis=0))
    return blocks[0] if len(blocks) == 1 else jnp.concatenate(blocks, axis=1)


def whole_rows(refs, window):
    pieces = [ref[:, window[0] : window[1]].astype(LOW) for ref in refs]
    return pieces[0] if len(pieces) == 1 else jnp.concatenate(pieces, axis=0)


def owned_columns_kernel(*refs, pairs, jobs, own):
    (lefts, rights), outs = pairs, refs[sum(pairs) :]
    left, right = refs[:lefts], refs[lefts : lefts + rights]
    for (order, window), out_ref in zip(jobs, outs):
        chunks = order(lax.axis_index("dp"))
        rows = whole_rows(left, window)
        product = dot_rows(rows, picked_columns(right, chunks, own))
        for place in range(len(chunks)):
            out_ref[place] = product[:, place * own : (place + 1) * own]


def owned_rows_kernel(*refs, pairs, jobs, own):
    (lefts, rights), outs = pairs, refs[sum(pairs) :]
    left, right = refs[:lefts], refs[lefts : lefts + rights]
    for (order, window), out_ref in zip(jobs, outs):
        chunks = order(lax.axis_index("dp"))
        product = dot_rows(picked_columns(left, chunks, own), whole_rows(right, window))
        for place in range(len(chunks)):
            out_ref[place] = product[place * own : (place + 1) * own, :]


def owned_parts_kernel(*refs, pairs, jobs, own):
    (lefts, rights), outs = pairs, refs[sum(pairs) :]
    left, right = refs[:lefts], refs[lefts : lefts + rights]
    for (order, window), out_ref in zip(jobs, outs):
        chunks = order(lax.axis_index("dp"))
        local = out_ref.shape[3]
        columns = (window[0] * local, window[1] * local)
        product = dot_rows(picked_columns(left, chunks, own), whole_rows(right, columns))
        for place in range(len(chunks)):
            for j in range(window[1] - window[0]):
                out_ref[place, j] = product[
                    place * own : (place + 1) * own, j * local : (j + 1) * local
                ]


def rounded_kernel(*refs):
    refs[-1][...] = whole_rows(refs[:-1], (0, refs[0].shape[1]))


def narrow_products(line, kernel, left, right, jobs, outs, own):
    joined = []
    for arrays in (left, right):
        rows = sum(array.shape[0] for array in arrays)
        low = shaped(rows, arrays[0].shape[1], kind=LOW)
        joined.append(line.call(rounded_kernel, [low], arrays)[0])
    results = []
    for (order, window), out in zip(jobs, outs):
        chunks = order(lax.axis_index("dp"))
        pick = lambda array: jnp.concatenate(
            [lax.dynamic_slice_in_dim(array, chunk * own, own, 1) for chunk in chunks], axis=1
        )
        if kernel is owned_columns_kernel:
            product = dot_rows(joined[0][:, window[0] : window[1]], pick(joined[1]))
            product = product.reshape(-1, len(chunks), own).transpose(1, 0, 2)
        elif kernel is owned_rows_kernel:
            product = dot_rows(pick(joined[0]), joined[1][:, window[0] : window[1]])
            product = product.reshape(out.shape)
        else:
            local = out.shape[3]
            columns = joined[1][:, window[0] * local : window[1] * local]
            product = dot_rows(pick(joined[0]), columns)
            product = product.reshape(len(chunks), own, -1, local).transpose(0, 2, 1, 3)
        results.append(product)
    return results


def owner_products(line, kernel, left, right, pieces, own, send):
    jobs, outs = [], []
    for piece in pieces:
        half = piece.route.held // 2
        part = slice(half, None) if send else slice(half)
        jobs.append((lambda rank, route=piece.route, part=part: route.order(rank)[part], piece.window))
        size = piece.window[1] - piece.window[0]
        if kernel is owned_columns_kernel:
            outs.append(shaped(half, size, own))
        elif kernel is owned_rows_kernel:
            outs.append(shaped(half, own, size))
        else:
            outs.append(shaped(half, size, own, right[0].shape[1] // 3))
    if own % LANES:
        return narrow_products(line, kernel, left, right, jobs, outs, own)
    return line.call(
        functools.partial(kernel, pairs=(len(left), len(right)), jobs=jobs, own=own),
        outs,
        [*left, *right],
        megabytes=20,
    )


def input_back_kernel(rows_ref, qkv_low_ref, send_ref, keep_ref, *, chunks):
    half = send_ref.shape[0] // chunks
    local = qkv_low_ref.shape[2]
    core = core_index()
    for c in range(chunks):
        for target, which in ((send_ref, 1 - core), (keep_ref, core)):
            rows = rows_ref[pl.ds(c * 2 * half + which * half, half), :]
            total = None
            for j in range(3):
                product = dot_wide(rows[:, j * local : (j + 1) * local], qkv_low_ref[j])
                total = product if total is None else total + product
            target[c * half : (c + 1) * half, :] = total


def input_norm_kernel(x_ref, norm_ref, mine_ref, theirs_ref, *refs, chunks):
    grad_hidden = refs[:chunks]
    rows_ref, sums_ref = refs[chunks:]
    half = mine_ref.shape[0] // chunks
    core = core_index()
    gains = offsets = None
    for c in range(chunks):
        rows = slice(c * half, (c + 1) * half)
        inputs = x_ref[pl.ds(c * 2 * half + core * half, half), :].astype(WIDE)
        stat, inverse = normalize(inputs)
        back, gain, offset = norm_back(
            mine_ref[rows, :] + theirs_ref[rows, :], stat, inverse, norm_ref[0:1, :]
        )
        rows_ref[rows, :] = grad_hidden[c][...] + back
        gains = gain if gains is None else gains + gain
        offsets = offset if offsets is None else offsets + offset
    sums_ref[0:1, :] = gains
    sums_ref[1:2, :] = offsets


def place_kernel(mine_ref, theirs_ref, out_ref, *, chunks):
    half = mine_ref.shape[0] // chunks
    core = core_index()
    for c in range(chunks):
        rows = slice(c * half, (c + 1) * half)
        out_ref[pl.ds((2 * c + core) * half, half), :] = mine_ref[rows, :].astype(LOW)
        out_ref[pl.ds((2 * c + 1 - core) * half, half), :] = theirs_ref[rows, :].astype(LOW)


def rows_kernel(source_ref, target_ref):
    target_ref[...] = source_ref[...]


def norm_sums_kernel(*refs, chunks):
    input_ref, norms, losses, out_ref = refs[0], refs[1 : 1 + chunks], refs[1 + chunks : -1], refs[-1]
    out_ref[0:2, :] = input_ref[...]
    out_ref[2:6, :] = sum(ref[...] for ref in norms[1:]) + norms[0][...]
    out_ref[6:8, :] = sum(ref[...] for ref in losses[1:]) + losses[0][...]


def stage_kernel(*refs, counts, crossed):
    terms, outs = refs[3 : 3 + sum(counts)], refs[3 + sum(counts) :]
    for source, target in zip(refs[:3], outs[:3]):
        target[...] = source[...]
    at = 0
    for count, out_ref, cross in zip(counts, outs[3:], crossed):
        out_ref[...] = gathered([term[...] for term in terms[at : at + count]], cross)
        at += count


def finish_kernel(gradient_ref, first_ref, second_ref, first_new_ref, second_new_ref):
    first_new, second_new, _ = moment_step(gradient_ref[...], first_ref[...], second_ref[...])
    first_new_ref[...] = first_new
    second_new_ref[...] = second_new


def moment_step(gradient, first_state, second_state):
    first_new = first_decay * first_state + (1.0 - first_decay) * gradient
    second_new = second_decay * second_state + (1.0 - second_decay) * gradient * gradient
    direction = (
        first_new
        / (1.0 - first_decay**STEP)
        / (jnp.sqrt(second_new / (1.0 - second_decay**STEP)) + adam_epsilon)
    )
    return (first_new, second_new, direction)


def total_of(values):
    rows = values.reshape(-1, values.shape[-1])
    return jnp.sum(jnp.sum(rows, axis=0, keepdims=True), axis=1, keepdims=True)


def moments_kernel(
    master_ref, first_ref, second_ref, squares_ref, *refs, row, regions, counts, crossed, late
):
    table_ref = refs[-1]
    kept_ref, update_ref, *moment_refs = refs[sum(counts) : -1]
    at = 0
    sizes = []
    for region, count, cross in zip(regions, counts, crossed):
        gradient = gathered([term[...] for term in refs[at : at + count]], cross)
        at += count
        first_new, second_new, direction = moment_step(
            gradient, first_ref[region], second_ref[region]
        )
        for target, found in zip(moment_refs, [gradient] if late else [first_new, second_new]):
            target[region] = found
        master = master_ref[region]
        kept_ref[region] = master
        update = direction + decay_rate * master
        update_ref[region] = update
        sizes.append((total_of(master * master), total_of(update * update)))
    table_ref[...] = squares_ref[...]
    for place, size in ((row, 0), (row + 4, 1)):
        amount = sizes[0][size]
        for other in sizes[1:]:
            amount = amount + other[size]
        table_ref[place : place + 1, :] = jnp.broadcast_to(amount, (1, LANES))


def join_kernel(*refs):
    terms, norms_ref, out_ref = refs[:-2], refs[-2], refs[-1]
    terms = [ref[...] for ref in terms]
    while len(terms) > 1:
        terms = [terms[i] + terms[i + 1] for i in range(0, len(terms), 2)]
    out_ref[:, 0:LANES] = terms[0]
    out_ref[:, LANES:] = norms_ref[...]


def masters_kernel(norm_ref, first_ref, second_ref, *refs, terms, own):
    sums, refs = refs[:terms], refs[terms:]
    masters, updates, outs = refs[:4], refs[4:8], refs[8:12]
    norms_ref, norm_new_ref, first_new_ref, second_new_ref = refs[12:]
    total = sums[0][:, 0:LANES]
    for ref in sums[1:]:
        total = total + ref[:, 0:LANES]
    sizes = jnp.sqrt(total[0:4, :])
    steps = jnp.sqrt(total[4:8, :] + trust_epsilon)
    lane = lax.broadcasted_iota(jnp.int32, (1, 4), 1)
    for place, found in ((0, sizes), (1, steps)):
        row = jnp.zeros((1, 4), WIDE)
        for index in range(4):
            row = jnp.where(lane == index, found[index : index + 1, 0:1], row)
        norms_ref[place : place + 1, :] = row
    ratio = learn_rate * (sizes / steps)
    for index in range(4):
        scale = ratio[index : index + 1, 0:1]
        if len(masters[index].shape) == 3:
            scale = scale.reshape(1, 1, 1)
        outs[index][...] = masters[index][...] - scale * updates[index][...]
    if own % LANES:
        gradient = sums[0][:, LANES:]
        for ref in sums[1:]:
            gradient = gradient + ref[:, LANES:]
        norm_new_ref[...] = gradient
        return
    start = pl.multiple_of(lax.axis_index("dp") * own, own)
    gradient = sums[0][:, pl.ds(LANES + start, own)]
    for ref in sums[1:]:
        gradient = gradient + ref[:, pl.ds(LANES + start, own)]
    first_new, second_new, direction = moment_step(gradient, first_ref[...], second_ref[...])
    first_new_ref[...] = first_new
    second_new_ref[...] = second_new
    norm_new_ref[...] = norm_ref[:, pl.ds(start, own)] - learn_rate * direction


def shards(
    block_input,
    lengths,
    norm_params,
    qkv_weight,
    out_weight,
    up_weight,
    down_weight,
    qkv_first,
    qkv_second,
    out_first,
    out_second,
    up_first,
    up_second,
    down_first,
    down_second,
    norm_first,
    norm_second,
    out_grad,
):
    row_count, width = block_input.shape
    local = qkv_weight.shape[2]
    hidden_units = up_weight.shape[1]
    group_count = lax.axis_size("dp")
    own = width // group_count
    own_start = lax.axis_index("dp") * own
    part = row_count // CHUNKS
    half = part // 2
    chunks = range(CHUNKS)
    bits = list(range(log2_of(group_count)))

    line = Line()
    qkv_parts = jnp.transpose(qkv_weight, (1, 0, 2))
    cosine, sine = rotary_tables(row_count)
    live = Raw(lengths, SMEM)
    joined = group_count == 8 and own % LANES == 0

    def relay_of(theirs):
        copied = line.call(rows_kernel, [cut(half, width, CUT_RELAY)], [theirs])[0]
        return theirs, near(copied)

    weight_shapes = [shaped(3, width, local, kind=LOW), shaped(local, width, kind=LOW)]
    chunk_shapes = [
        shaped(part, width, kind=LOW),
        shaped(part, local, kind=LOW),
        shaped(part, local, kind=LOW),
        shaped(part, local, kind=LOW),
        shaped(part, local, kind=LOW),
        shaped(part, LANES),
        cut(half, width, CUT_ATTENTION),
        shaped(half, width),
    ]
    low_weights, parts, branch_terms = [], [], []

    def attention(c):
        if c == 0:
            outs = line.call(
                first_kernel,
                weight_shapes + chunk_shapes,
                [live]
                + [
                    Raw(a, HBM)
                    for a in (block_input, norm_params, cosine, sine, qkv_parts, out_weight)
                ],
                scratch=[
                    pltpu.VMEM((part, width), LOW),
                    pltpu.VMEM(norm_params.shape, WIDE),
                    pltpu.VMEM((part, LANES), WIDE),
                    pltpu.VMEM((part, LANES), WIDE),
                    pltpu.VMEM((3, width, local), WIDE),
                    pltpu.VMEM((local, width), WIDE),
                    pltpu.SemaphoreType.DMA((8,)),
                ],
                megabytes=60,
                first=True,
            )
            low_weights.extend(outs[:2])
            outs = outs[2:]
        else:
            before = [p[2] for p in parts] + [p[3] for p in parts]
            outs = line.call(
                functools.partial(next_kernel, first_row=c * part, part=part),
                chunk_shapes,
                [live, block_input, norm_params, cosine, sine, *low_weights, *before],
            )
        parts.append(outs)
        branch_terms.append((outs[7], near(outs[6])))

    def sum_branch(c):
        branch_terms[c] = sum_rows(line, *branch_terms[c])

    def cast(weight):
        return line.call(cast_kernel, [shaped(*weight.shape, kind=LOW)], [Take(weight)])[0]

    branch, hidden, normed_mid, up, active, mlp_terms = [], [], [], [], [], []
    normed_other, ships, normed_theirs, active_theirs, slope_theirs = [], [], [], [], []

    def middle(c):
        outs = line.call(
            functools.partial(middle_kernel, c * part),
            [shaped(half, width), shaped(half, width), cut(half, width, CUT_MIDDLE)]
            + [shaped(half, width)] * joined,
            [block_input, norm_params, *branch_terms[c]],
        )
        branch.append(outs[0])
        hidden.append(outs[1])
        normed_other.append((outs[2], near(outs[2])))
        ships.append(swap(outs[3], "dp", 2) if joined else None)

    def relay(c):
        if joined:
            ships[c] = relay_of(ships[c])

    def mlp(c):
        outs = line.call(
            mlp_kernel,
            [
                shaped(part, width, kind=LOW),
                shaped(part, hidden_units),
                shaped(part, hidden_units, kind=LOW),
                cut(half, width, CUT_MLP),
                shaped(half, width),
            ],
            [*normed_other[c], up_low, down_low],
        )
        normed_mid.append(outs[0])
        up.append(outs[1])
        active.append(outs[2])
        mlp_terms.append((outs[4], near(outs[3])))

    def sum_mlp(c):
        mlp_terms[c] = sum_rows(line, *mlp_terms[c])

    def again(c):
        if joined:
            outs = line.call(
                again_kernel,
                [
                    shaped(part, width, kind=LOW),
                    shaped(part, hidden_units, kind=LOW),
                    shaped(part, hidden_units),
                ],
                [*ships[c], up_low],
            )
            normed_theirs.append(outs[0])
            active_theirs.append(outs[1])
            slope_theirs.append(outs[2])

    line.own, line.table = own, jnp.zeros((8, LANES), WIDE)
    route_a, route_b, route_j = routes(group_count)
    columns = lambda: (slice(None), pl.ds(pl.multiple_of(lax.axis_index("dp") * own, own), own))
    rows = lambda: (pl.ds(pl.multiple_of(lax.axis_index("dp") * own, own), own),)
    part_rows = lambda: (slice(None), *rows())
    mine = lambda array, axis: lax.dynamic_slice_in_dim(array, own_start, own, axis)
    block_rows, loss_sums, grad_final, grad_up_rows, mid_terms = [], [], [], [], []
    grad_mlp, grad_mlp_theirs, grad_up_theirs, ships_back = [], [], [], []
    grad_hidden, norms_sums, own_back, other_back = [], [], [], []
    flip = lambda array: jnp.transpose(array, (1, 0, 2))
    qkv = Weight(
        line,
        0,
        3,
        owned_parts_kernel,
        lambda: ([p[0] for p in parts], [grad_rows]),
        Take(qkv_parts, (3, own, local), part_rows),
        [flip(qkv_first), flip(qkv_second)],
    )
    out = Weight(
        line,
        1,
        local,
        owned_columns_kernel,
        lambda: ([p[4] for p in parts], [grad_branch]),
        Take(mine(out_weight, 1)) if own % LANES else Take(out_weight, (local, own), columns),
        [out_first, out_second],
    )
    up_matrix = Weight(
        line,
        2,
        hidden_units,
        owned_rows_kernel,
        lambda: (normed_mid + normed_theirs, grad_up_rows + grad_up_theirs),
        Take(up_weight, (own, hidden_units), rows),
        [up_first, up_second],
    )
    down = Weight(
        line,
        3,
        hidden_units,
        owned_columns_kernel,
        lambda: (active + active_theirs, grad_mlp + grad_mlp_theirs),
        Take(mine(down_weight, 1))
        if own % LANES
        else Take(down_weight, (hidden_units, own), columns),
        [down_first, down_second],
    )
    d0 = down.piece(0, 8, 8, route_j)
    u0 = up_matrix.piece(0, 8, 8, route_j)
    q0 = qkv.piece(0, 2, 3, route_b)
    q1 = qkv.piece(2, 3, 3, route_b)
    o0 = out.piece(0, 1, 1, route_b)


    def loss(c):
        outs = line.call(
            functools.partial(loss_kernel, c * part),
            [shaped(half, width), shaped(2, width), cut(half, width, CUT_LOSS)]
            + [shaped(half, width)] * joined,
            [out_grad, norm_params, hidden[c], *mlp_terms[c]],
        )
        block_rows.append(outs[0])
        loss_sums.append(outs[1])
        grad_final.append((outs[2], near(outs[2])))
        ships_back.append(swap(outs[3], "dp", 2) if joined else None)

    def back_relay(c):
        if joined:
            ships_back[c] = relay_of(ships_back[c])

    def mlp_back(c):
        outs = line.call(
            mlp_back_kernel,
            [
                shaped(part, width, kind=LOW),
                shaped(part, hidden_units, kind=LOW),
                cut(half, width, CUT_MLP if c < CHUNKS - 1 else CUT_MID),
                shaped(half, width),
            ],
            [*grad_final[c], up[c], up_low, down_low],
        )
        grad_mlp.append(outs[0])
        grad_up_rows.append(outs[1])
        mid_terms.append((outs[3], near(outs[2])))

    def back_again(c):
        if joined:
            outs = line.call(
                back_again_kernel,
                [shaped(part, width, kind=LOW), shaped(part, hidden_units, kind=LOW)],
                [*ships_back[c], slope_theirs[c], down_low],
            )
            grad_mlp_theirs.append(outs[0])
            grad_up_theirs.append(outs[1])

    def sum_mid(c):
        mid_terms[c] = sum_rows(line, *mid_terms[c])

    def norms(c):
        outs = line.call(
            functools.partial(norms_back_kernel, c * part),
            [shaped(half, width), cut(half, width, CUT_NORMS), shaped(4, width)],
            [out_grad, norm_params, hidden[c], branch[c], *mid_terms[c]],
        )
        grad_hidden.append(outs[0])
        norms_sums.append(outs[2])
        own_back.append(outs[1])
        other_back.append(near(outs[1]))

    def attention_back():
        return line.call(
            functools.partial(attention_back_kernel, chunks=CHUNKS),
            [shaped(row_count, width, kind=LOW), shaped(row_count, 3 * local, kind=LOW)],
            [live, low_weights[1], cosine, sine, *own_back, *other_back]
            + [p[which] for which in (1, 2, 3, 5) for p in parts],
            scratch=[pltpu.VMEM((row_count, local), WIDE), pltpu.VMEM((row_count, local), WIDE)],
        )

    def input_back():
        return line.call(
            functools.partial(input_back_kernel, chunks=CHUNKS),
            [cut(row_count // 2, width, CUT_BACK), shaped(row_count // 2, width)],
            [grad_rows, low_weights[0]],
        )

    def input_norm():
        return line.call(
            functools.partial(input_norm_kernel, chunks=CHUNKS),
            [cut(row_count // 2, width, CUT_INPUT), shaped(2, width)],
            [block_input, norm_params, *in_terms, *grad_hidden],
        )

    def send_output():
        return line.call(
            rows_kernel, [cut(row_count // 2, width, CUT_OUTPUT)], [block_rows]
        )[0]

    def place(blocks, others):
        return line.call(
            functools.partial(place_kernel, chunks=CHUNKS),
            [shaped(row_count, width, kind=LOW)],
            [blocks, others],
        )[0]

    def norm_sums():
        return line.call(
            functools.partial(norm_sums_kernel, chunks=CHUNKS),
            [shaped(8, width)],
            [input_sums, *norms_sums, *loss_sums],
        )[0]

    def sum_norms():
        return line.call(
            sum_kernel, [shaped(8, width)], [grad_norms, norms_other]
        )[0]

    attention(0)
    sum_branch(0)
    attention(1)
    sum_branch(1)
    up_low = cast(up_weight)
    down_low = cast(down_weight)
    middle(0)
    mlp(0)
    sum_mlp(0)
    middle(1)
    mlp(1)
    sum_mlp(1)
    relay(0)
    loss(0)
    mlp_back(0)
    again(0)
    relay(1)
    sum_mid(0)
    loss(1)
    again(1)
    back_relay(0)
    mlp_back(1)
    sent_rows = send_output()
    block_other = near(sent_rows)
    sum_mid(1)
    back_again(0)
    norms(0)
    back_relay(1)
    back_again(1)
    d0.start()
    down.hold()
    norms(1)
    up_matrix.hold()
    grad_branch, grad_rows = attention_back()
    q0.start()
    u0.start()
    qkv.hold()
    out.hold()
    o0.start()
    send, keep = input_back()
    crossing = near(send)
    d0.advance()
    in_terms = sum_rows(line, keep, crossing)
    q0.advance()
    u0.advance()
    block_output = place(sent_rows, block_other)
    o0.advance()
    d0.advance()
    q1.start()
    input_rows, input_sums = input_norm()
    input_other = near(input_rows)
    q0.advance()
    q1.advance()
    o0.advance()
    u0.advance()
    down.moments()
    q0.advance()
    q1.advance()
    up_matrix.moments()
    o0.advance()
    q1.advance()
    out.moments()
    grad_norms = norm_sums()
    norms_other = swap(grad_norms, "tensor", 1)
    grad_norms = sum_norms()
    input_grad = place(input_rows, input_other)
    qkv.stage()
    qkv.moments()

    tensor_bits = log2_of(lax.axis_size("tensor"))
    found = line.table
    for start in range(0, tensor_bits, 2):
        terms = sum_terms(found, "tensor", start, min(2, tensor_bits - start))
        if start == 0:
            qkv.finish()
        if start + 2 >= tensor_bits:
            found = line.call(join_kernel, [shaped(8, LANES + width)], [*terms, grad_norms])[0]
        else:
            found = line.call(pairs_kernel, [shaped(8, LANES)], terms)[0]
    for start in range(0, len(bits), 2):
        terms = sum_terms(found, "dp", start, min(2, len(bits) - start))
        if start + 2 < len(bits) or len(terms) > 2:
            found = line.call(pairs_kernel, [shaped(8, LANES + width)], terms)[0]
            terms = [found]
    weights = (qkv, out, up_matrix, down)
    outs = line.call(
        functools.partial(masters_kernel, terms=len(terms), own=own),
        [shaped(*weight.kept.shape) for weight in weights]
        + [shaped(2, 4), shaped(8, width if own % LANES else own), shaped(8, own), shaped(8, own)],
        [
            norm_params,
            norm_first,
            norm_second,
            *terms,
            *[weight.kept for weight in weights],
            *[weight.update for weight in weights],
        ],
    )
    matrix_norms, norm_new, norm_first_new, norm_second_new = outs[4:]
    if own % LANES:
        norm_first_new, norm_second_new, direction = moment_step(
            mine(norm_new, 1), norm_first, norm_second
        )
        norm_new = mine(norm_params, 1) - learn_rate * direction
    return (
        block_output,
        input_grad,
        flip(outs[0]),
        flip(qkv.first_new),
        flip(qkv.second_new),
        outs[1],
        out.first_new,
        out.second_new,
        outs[2],
        up_matrix.first_new,
        up_matrix.second_new,
        outs[3],
        down.first_new,
        down.second_new,
        norm_new,
        norm_first_new,
        norm_second_new,
        matrix_norms,
    )


def solution(mesh):
    in_specs = (
        P("dp", None),
        P("dp"),
        P(),
        P(None, None, "tensor"),
        P("tensor", None),
        P(None, "tensor"),
        P("tensor", None),
        P("dp", None, "tensor"),
        P("dp", None, "tensor"),
        P("tensor", "dp"),
        P("tensor", "dp"),
        P("dp", "tensor"),
        P("dp", "tensor"),
        P("tensor", "dp"),
        P("tensor", "dp"),
        P(None, "dp"),
        P(None, "dp"),
        P("dp", None),
    )
    out_specs = (
        P("dp", None),
        P("dp", None),
        P("dp", None, "tensor"),
        P("dp", None, "tensor"),
        P("dp", None, "tensor"),
        P("tensor", "dp"),
        P("tensor", "dp"),
        P("tensor", "dp"),
        P("dp", "tensor"),
        P("dp", "tensor"),
        P("dp", "tensor"),
        P("tensor", "dp"),
        P("tensor", "dp"),
        P("tensor", "dp"),
        P(None, "dp"),
        P(None, "dp"),
        P(None, "dp"),
        P(),
    )
    return jax.shard_map(shards, mesh=mesh, in_specs=in_specs, out_specs=out_specs, check_vma=False)
```

```python
import functools

import jax
import jax.numpy as jnp
import numpy as np
from jax import lax
from jax.experimental import pallas as pl
from jax.experimental.pallas import tpu as pltpu
from jax.sharding import PartitionSpec as P

HEAD_DIM = 64
STEP = 10
CHUNKS = 2
LANES = 128

norm_epsilon = 1e-05
rotary_base = 10000.0
mask_fill = -1000000000.0
first_decay = 0.9
second_decay = 0.999
adam_epsilon = 1e-06
trust_epsilon = 1e-06
decay_rate = 0.01
learn_rate = 0.25

CUT_ATTENTION, CUT_MIDDLE, CUT_MLP, CUT_LOSS = 4, 4, 4, 4
CUT_RELAY = 2
CUT_MID, CUT_NORMS, CUT_BACK, CUT_INPUT, CUT_OUTPUT = 2, 4, 4, 2, 4

LOW = jnp.bfloat16
WIDE = jnp.float32
VMEM = pl.BlockSpec(memory_space=pltpu.VMEM)
SMEM = pl.BlockSpec(memory_space=pltpu.SMEM)
HBM = pl.BlockSpec(memory_space=pltpu.HBM)


def log2_of(count):
    bits = 0
    while (1 << bits) < count:
        bits += 1
    return bits


def swap(values, axis, distance):
    count = lax.axis_size(axis)
    return lax.ppermute(values, axis, [(i, i ^ distance) for i in range(count)])


class Route:
    def __init__(self, order, steps, held, joined=False):
        self.order, self.steps, self.held, self.joined = order, steps, held, joined


HALF, CROSS, BACK = range(3)


def apart(count, distance, among=None):
    return [(i, i ^ distance) for i in (range(count) if among is None else among)]


def outside(rank):
    place = lax.div(rank, 2)
    return (place == 0) | (place == 3)


def line_chunks(rank):
    place = lax.div(rank, 2)
    beside, side = lax.bitwise_xor(place, 1), lax.div(place, 2)
    near, far = (place, beside), (2 - side, 3 - 3 * side)
    end = outside(rank)
    keep = [jnp.where(end, a, b) for a, b in zip(near, far)]
    send = [jnp.where(end, a, b) for a, b in zip(far, (beside, place))]
    return keep, send


def routes(count):
    if count == 8:

        def across_first(rank):
            keep, send = line_chunks(rank)
            row = lax.rem(rank, 2)
            return [place * 2 + y for y in (row, 1 - row) for place in keep + send]

        def along_first(rank):
            keep, send = line_chunks(rank)
            row = lax.rem(rank, 2)
            return [place * 2 + y for part in (keep, send) for y in (row, 1 - row) for place in part]

        def joined(rank):
            keep, _ = line_chunks(rank)
            row = lax.rem(rank, 2)
            return [place * 2 + y for y in (row, 1 - row) for place in keep]

        across = (HALF, apart(8, 1))
        along, back = (HALF, apart(8, 2)), (BACK, apart(8, 2))
        cross = (CROSS, apart(8, 6, range(2, 6)))
        return (
            Route(across_first, [across, along, cross, back], 8),
            Route(along_first, [along, across, cross, back], 8),
            Route(joined, [across, cross, back], 4, True),
        )
    order = [0]
    bits = range(log2_of(count))
    for bit in reversed(bits):
        order = order + [distance ^ (1 << bit) for distance in order]
    found = Route(
        lambda rank: [lax.bitwise_xor(rank, distance) for distance in order],
        [(HALF, apart(count, 1 << bit)) for bit in bits],
        count,
    )
    return found, found, found


def normalize(values):
    center = values - jnp.mean(values, axis=-1, keepdims=True)
    inverse = lax.rsqrt(jnp.mean(center * center, axis=-1, keepdims=True) + norm_epsilon)
    return center * inverse, inverse


def norm_back(incoming, normed, inverse, gain):
    scaled = incoming * gain
    inner = (
        scaled
        - jnp.mean(scaled, axis=-1, keepdims=True)
        - normed * jnp.mean(scaled * normed, axis=-1, keepdims=True)
    )
    gain_grad = jnp.sum(incoming * normed, axis=0, keepdims=True)
    return inner * inverse, gain_grad, jnp.sum(incoming, axis=0, keepdims=True)


def rotary_tables(length):
    half = HEAD_DIM // 2
    lane = np.arange(LANES)
    frequency = (rotary_base ** (-((lane % half).astype(np.float32) * 2.0 / HEAD_DIM))).astype(np.float32)
    angles = np.arange(length, dtype=np.float32)[:, None] * frequency[None, :]
    sign = np.where(lane % HEAD_DIM < half, -1.0, 1.0)
    cosine = np.cos(angles.astype(np.float64)).astype(np.float32)
    sine = (np.sin(angles.astype(np.float64)) * sign[None, :]).astype(np.float32)
    return jnp.asarray(cosine), jnp.asarray(sine)


def turn(values, cosine, sine):
    half = HEAD_DIM // 2
    lane = lax.broadcasted_iota(jnp.int32, (1, LANES), 1)
    first = lax.rem(lane, HEAD_DIM) < half
    tiles = []
    for start in range(0, values.shape[1], LANES):
        tile = values[:, start : start + LANES]
        other = jnp.where(
            first, pltpu.roll(tile, LANES - half, 1), pltpu.roll(tile, half, 1)
        )
        tiles.append(tile * cosine + other * sine)
    return tiles[0] if len(tiles) == 1 else jnp.concatenate(tiles, axis=1)


def gelu_mass(up):
    return 0.5 * (1.0 + lax.erf(up * (0.5**0.5)))


def gelu_slope(up, mass):
    return mass + up * jnp.exp(-0.5 * up * up) * float((2.0 * np.pi) ** -0.5)


def dot(left, right):
    return jnp.dot(left, right, preferred_element_type=WIDE)


def dot_rows(left, right):
    return lax.dot_general(left, right, (((0,), (0,)), ((), ())), preferred_element_type=WIDE)


def dot_wide(left, right):
    return lax.dot_general(left, right, (((1,), (1,)), ((), ())), preferred_element_type=WIDE)


def of_head(values, head):
    lane = lax.broadcasted_iota(jnp.int32, (1, values.shape[1]), 1)
    mine = (lane >= head * HEAD_DIM) & (lane < (head + 1) * HEAD_DIM)
    return jnp.where(mine, values, jnp.zeros_like(values))


def core_index():
    return lax.rem(lax.axis_index("tensor"), 2)


def shaped(*shape, kind=WIDE):
    return jax.ShapeDtypeStruct(shape, kind)


def cut(rows, width, count=4):
    return [shaped(rows // count, width)] * count


def near(values):
    return [swap(piece, "tensor", 1) for piece in values]


class Take:
    def __init__(self, array, shape=None, index=None):
        self.array = array
        self.shape = array.shape if shape is None else shape
        self.index = index


class Raw:
    def __init__(self, array, spec):
        self.array = array
        self.spec = spec


class Rows:
    def __init__(self, refs):
        self.refs = refs
        self.step = refs[0].shape[0]
        self.shape = (self.step * len(refs), refs[0].shape[1])

    def spans(self, key):
        first, last = 0, self.shape[0]
        if key is not Ellipsis and key[0] != slice(None):
            first, last = key[0].start, key[0].stop
        for place, ref in enumerate(self.refs):
            start, stop = max(first, place * self.step), min(last, (place + 1) * self.step)
            if start < stop:
                inside = slice(start - place * self.step, stop - place * self.step)
                yield ref, inside, slice(start - first, stop - first)

    def __getitem__(self, key):
        pieces = [ref[inside, :] for ref, inside, _ in self.spans(key)]
        return pieces[0] if len(pieces) == 1 else jnp.concatenate(pieces, axis=0)

    def __setitem__(self, key, value):
        for ref, inside, outside in self.spans(key):
            ref[inside, :] = value[outside]


class Line:
    def __init__(self):
        self.token = jnp.zeros((8, LANES), WIDE)

    def call(self, kernel, outs, args, scratch=(), megabytes=12, first=False):
        arrays, specs, buffers, layout, takes = [], [], [], [], []
        for arg in args:
            if isinstance(arg, Take):
                layout.append(0)
                takes.append((len(arrays), arg))
                arrays.append(arg.array)
                specs.append(HBM)
                buffers.append(pltpu.VMEM(arg.shape, arg.array.dtype))
            elif isinstance(arg, Raw):
                layout.append(0)
                arrays.append(arg.array)
                specs.append(arg.spec)
            elif isinstance(arg, (list, tuple)):
                layout.append(len(arg))
                arrays += arg
                specs += [VMEM] * len(arg)
            else:
                layout.append(0)
                arrays.append(arg)
                specs.append(VMEM)
        if takes:
            buffers.append(pltpu.SemaphoreType.DMA((len(takes),)))
        token = [] if first else [self.token]
        out_layout = [len(out) if isinstance(out, list) else 0 for out in outs]
        out_shapes = [o for out in outs for o in (out if isinstance(out, list) else [out])]

        def joined(refs, layout):
            refs = list(refs)
            return [
                Rows([refs.pop(0) for _ in range(count)]) if count else refs.pop(0)
                for count in layout
            ]

        def body(*refs):
            inputs = list(refs[: len(arrays)])
            rest = refs[len(arrays) + len(token) :]
            results, rest = rest[: len(out_shapes)], rest[len(out_shapes) + len(token) :]
            own, rest = rest[: len(scratch)], rest[len(scratch) :]
            copies = []
            for place, (i, take) in enumerate(takes):
                source = inputs[i]
                if take.index is not None:
                    source = source.at[take.index()]
                copies.append(pltpu.make_async_copy(source, rest[place], rest[-1].at[place]))
                inputs[i] = rest[place]
            for copy in copies:
                copy.start()
            for copy in copies:
                copy.wait()
            kernel(*joined(inputs, layout), *joined(results, out_layout), *own)

        results = pl.pallas_call(
            body,
            out_shape=(*out_shapes, *[shaped(8, LANES) for _ in token]),
            in_specs=[*specs, *[HBM for _ in token]],
            out_specs=tuple([VMEM] * len(out_shapes) + [HBM for _ in token]),
            scratch_shapes=[*scratch, *buffers],
            input_output_aliases={len(arrays): len(out_shapes)} if token else {},
            compiler_params=pltpu.CompilerParams(vmem_limit_bytes=megabytes * 1024 * 1024),
            cost_estimate=pl.CostEstimate(flops=0, bytes_accessed=0, transcendentals=0),
        )(*arrays, *token)
        found = list(results)
        if token:
            self.token = found.pop()
        return [
            [found.pop(0) for _ in range(count)] if count else found.pop(0) for count in out_layout
        ]


def sum_kernel(*refs):
    total = refs[0][...]
    for ref in refs[1:-1]:
        total = total + ref[...]
    refs[-1][...] = total


def pairs_kernel(*refs):
    terms = [ref[...] for ref in refs[:-1]]
    while len(terms) > 1:
        terms = [terms[i] + terms[i + 1] for i in range(0, len(terms), 2)]
    refs[-1][...] = terms[0]


def sum_rows(line, keep, arrived, count=1):
    mine, theirs = keep, arrived
    for bit in range(1, log2_of(lax.axis_size("tensor"))):
        mine = line.call(sum_kernel, [cut(*keep.shape, count)], [mine, theirs])[0]
        theirs = [swap(piece, "tensor", 1 << bit) for piece in mine]
    return mine, theirs


def sum_terms(values, axis, start, taken):
    return [values] + [swap(values, axis, distance << start) for distance in range(1, 1 << taken)]


def gathered(values, crossed):
    if crossed:
        first = jnp.where(outside(lax.axis_index("dp")), values[0], values[1])
        values = [first, *values[2:]]
    total = values[0]
    for value in values[1:]:
        total = total + value
    return total


def gather_kernel(*refs, crossed):
    refs[-1][...] = gathered([ref[...] for ref in refs[:-1]], crossed)


class Piece:
    def __init__(self, weight, window, route):
        self.weight, self.window, self.route = weight, window, route
        self.joined = route.joined
        self.terms, self.stage, self.crossed = [], 0, False

    def exchange(self, values):
        self.terms.append(lax.ppermute(values, "dp", self.route.steps[self.stage][1]))
        self.stage += 1

    def start(self):
        self.size = self.route.held // 2
        self.exchange(self.weight.products([self], True)[0])

    def sum_of(self, first, size):
        shape = (size,) + self.terms[0].shape[1:]
        index = lambda: (pl.ds(first, size),)
        return self.weight.line.call(
            functools.partial(gather_kernel, crossed=self.crossed),
            [shaped(*shape)],
            [Take(term, shape, index) for term in self.terms],
        )[0]

    def advance(self):
        if self.stage == len(self.route.steps):
            return
        if self.route.steps[self.stage][0] == CROSS:
            self.terms = [self.sum_of(0, self.size)]
            self.exchange(self.terms[0])
            self.crossed = True
        else:
            self.size //= 2
            self.exchange(self.sum_of(self.size, self.size))


class Weight:
    tables = {}

    def __init__(self, line, row, size, kernel, factors, mine, master, states):
        self.line, self.row, self.size, self.kernel = line, row, size, kernel
        self.factors, self.mine, self.master, self.states = factors, mine, master, states
        self.pieces = []

    def piece(self, first, last, count, route):
        found = Piece(self, (self.size * first // count, self.size * last // count), route)
        self.pieces.append(found)
        return found

    def products(self, pieces, send):
        line = self.line
        if any(piece.joined for piece in pieces):
            return owner_products(
                line, self.kernel, *self.factors(), pieces, line.own, send, CHUNKS
            )
        return owner_products(line, self.kernel, *self.mine(), pieces, line.own, send)

    def hold(self):
        for piece, keep in zip(self.pieces, self.products(self.pieces, False)):
            piece.terms.insert(0, keep)

    def stage(self):
        before = [self.master, *[Take(state) for state in self.states]]
        terms = [
            Take(term, term.shape[1:], lambda: (0,))
            for piece in self.pieces
            for term in piece.terms[:-1]
        ]
        crossed = [piece.crossed for piece in self.pieces]
        shapes = [shaped(*piece.terms[0].shape[1:]) for piece in self.pieces]
        counts = [len(piece.terms) - 1 for piece in self.pieces]
        self.master, *outs = self.line.call(
            functools.partial(stage_kernel, counts=counts, crossed=crossed),
            [shaped(*self.master.shape)] * 3 + shapes,
            before + terms,
        )
        self.states = outs[:2]
        self.partial = outs[2:]

    def moments(self):
        for piece in self.pieces:
            while piece.stage < len(piece.route.steps):
                piece.advance()
        everything = slice(None)
        if self.kernel is owned_rows_kernel:
            regions = [(everything, slice(*piece.window)) for piece in self.pieces]
        else:
            regions = [(slice(*piece.window),) for piece in self.pieces]
        late = not isinstance(self.master, Take)
        states, terms, counts, crossed = self.states, [], [], []
        if not late:
            states = [Take(state) for state in states]
        for index, piece in enumerate(self.pieces):
            found = [self.partial[index]] if late else []
            for term in piece.terms[-1:] if late else piece.terms:
                found.append(Take(term, term.shape[1:], lambda: (0,)))
            terms += found
            counts.append(len(found))
            crossed.append(piece.crossed and not late)
        shape = shaped(*self.master.shape)
        outs = self.line.call(
            functools.partial(
                moments_kernel,
                row=self.row,
                regions=regions,
                counts=counts,
                crossed=crossed,
                late=late,
            ),
            [shape, shape] + [shape] * (1 if late else 2) + [shaped(8, LANES)],
            [self.master, *states, self.line.table, *terms],
            megabytes=16,
        )
        self.kept, self.update, *self.found, self.line.table = outs
        if not late:
            self.first_new, self.second_new = self.found

    def finish(self):
        self.first_new, self.second_new = self.line.call(
            finish_kernel, [shaped(*self.master.shape)] * 2, [*self.found, *self.states]
        )


def project(normed, weights, cosine, sine):
    query = turn(dot(normed, weights[0]), cosine, sine).astype(LOW)
    keys = turn(dot(normed, weights[1]), cosine, sine).astype(LOW)
    return query, keys, dot(normed, weights[2]).astype(LOW)


def attend(query, keys, values, first_row, live_len):
    rows, reach = query.shape[0], keys.shape[0]
    row = first_row + lax.broadcasted_iota(jnp.int32, (rows, reach), 0)
    column = lax.broadcasted_iota(jnp.int32, (rows, reach), 1)
    visible = (column <= row) & (column < live_len)
    lane = lax.broadcasted_iota(jnp.int32, (1, LANES), 1)
    mixed = jnp.zeros((rows, query.shape[1]), WIDE)
    masses = jnp.zeros((rows, LANES), WIDE)
    for head in range(query.shape[1] // HEAD_DIM):
        scores = dot_wide(of_head(query, head), keys) * HEAD_DIM ** (-0.5)
        scores = jnp.where(visible, scores, mask_fill)
        top = jnp.max(scores, axis=-1, keepdims=True)
        expo = jnp.exp(scores - top)
        total = jnp.sum(expo, axis=-1, keepdims=True)
        probs = (expo * (1.0 / total)).astype(LOW)
        mixed = mixed + dot(probs, of_head(values, head))
        masses = jnp.where(lane == head, top + jnp.log(total), masses)
    live = first_row + lax.broadcasted_iota(jnp.int32, (rows, 1), 0) < live_len
    return jnp.where(live, mixed, 0.0).astype(LOW), masses


def split_rows(left_ref, right, send_ref, keep_ref, how):
    half = send_ref.shape[0]
    core = core_index()
    send_ref[...] = how(left_ref[pl.ds((1 - core) * half, half), :], right)
    keep_ref[...] = how(left_ref[pl.ds(core * half, half), :], right)


def first_kernel(
    live_ref, x_any, norm_any, cos_any, sin_any, qkv_any, out_any,
    qkv_low_ref, out_low_ref, normed_ref, q_ref, k_ref, v_ref, attn_ref, mass_ref, send_ref, keep_ref,
    x_ref, norm_ref, cos_ref, sin_ref, qkv_in, out_in, arrived,
):
    part = x_ref.shape[0]
    sources = [x_any.at[pl.ds(0, part)], norm_any, cos_any.at[pl.ds(0, part)], sin_any.at[pl.ds(0, part)]]
    targets = [x_ref, norm_ref, cos_ref, sin_ref]
    sources += [qkv_any.at[j] for j in range(3)] + [out_any]
    targets += [qkv_in.at[j] for j in range(3)] + [out_in]
    copies = [
        pltpu.make_async_copy(source, target, arrived.at[i])
        for i, (source, target) in enumerate(zip(sources, targets))
    ]
    for copy in copies:
        copy.start()
    copies[0].wait()
    copies[1].wait()
    stat, _ = normalize(x_ref[...].astype(WIDE))
    normed = (stat * norm_ref[0:1, :] + norm_ref[1:2, :]).astype(LOW)
    normed_ref[...] = normed
    copies[2].wait()
    copies[3].wait()
    weights = []
    for j in range(3):
        copies[4 + j].wait()
        weights.append(qkv_in[j].astype(LOW))
        qkv_low_ref[j] = weights[j]
    query, keys, values = project(normed, weights, cos_ref[...], sin_ref[...])
    q_ref[...], k_ref[...], v_ref[...] = query, keys, values
    attn_ref[...], mass_ref[...] = attend(query, keys, values, 0, live_ref[0])
    copies[7].wait()
    out_low = out_in[...].astype(LOW)
    out_low_ref[...] = out_low
    split_rows(attn_ref, out_low, send_ref, keep_ref, dot)


def next_kernel(
    live_ref, x_ref, norm_ref, cos_ref, sin_ref, qkv_low_ref, out_low_ref, *refs, first_row, part
):
    earlier = first_row // part
    rows = slice(first_row, first_row + part)
    k_before, v_before = refs[:earlier], refs[earlier : 2 * earlier]
    normed_ref, q_ref, k_ref, v_ref, attn_ref, mass_ref, send_ref, keep_ref = refs[2 * earlier :]
    stat, _ = normalize(x_ref[rows, :].astype(WIDE))
    normed = (stat * norm_ref[0:1, :] + norm_ref[1:2, :]).astype(LOW)
    normed_ref[...] = normed
    weights = [qkv_low_ref[j] for j in range(3)]
    query, keys, values = project(normed, weights, cos_ref[rows, :], sin_ref[rows, :])
    q_ref[...], k_ref[...], v_ref[...] = query, keys, values
    keys = jnp.concatenate([ref[...] for ref in k_before] + [keys], axis=0)
    values = jnp.concatenate([ref[...] for ref in v_before] + [values], axis=0)
    attn_ref[...], mass_ref[...] = attend(query, keys, values, first_row, live_ref[0])
    split_rows(attn_ref, out_low_ref[...], send_ref, keep_ref, dot)


def cast_kernel(wide_ref, low_ref):
    low_ref[...] = wide_ref[...].astype(LOW)


def middle_kernel(
    first_row, x_ref, norm_ref, mine_ref, theirs_ref, branch_ref, hidden_ref, *normed_refs
):
    half = mine_ref.shape[0]
    branch = mine_ref[...] + theirs_ref[...]
    branch_ref[...] = branch
    stat, _ = normalize(branch)
    inputs = x_ref[pl.ds(first_row + core_index() * half, half), :].astype(WIDE)
    hidden = inputs + stat * norm_ref[2:3, :] + norm_ref[3:4, :]
    hidden_ref[...] = hidden
    stat, _ = normalize(hidden)
    normed = stat * norm_ref[4:5, :] + norm_ref[5:6, :]
    for normed_ref in normed_refs:
        normed_ref[...] = normed


def mlp_kernel(own_ref, other_ref, up_w_ref, down_w_ref, normed_ref, up_ref, active_ref, send_ref, keep_ref):
    half = own_ref.shape[0]
    normed = jnp.concatenate([own_ref[...].astype(LOW), other_ref[...].astype(LOW)], axis=0)
    normed_ref[...] = normed
    step = min(256, up_w_ref.shape[1])
    total = None
    for start in range(0, up_w_ref.shape[1], step):
        block = slice(start, start + step)
        up = dot(normed, up_w_ref[:, block])
        up_ref[:, block] = up
        active = (up * gelu_mass(up)).astype(LOW)
        active_ref[:, block] = active
        product = dot(active, down_w_ref[block, :])
        total = product if total is None else total + product
    keep_ref[...] = total[:half]
    send_ref[...] = total[half:]


def again_kernel(own_ref, other_ref, up_w_ref, normed_ref, active_ref, slope_ref):
    normed = jnp.concatenate([own_ref[...].astype(LOW), other_ref[...].astype(LOW)], axis=0)
    normed_ref[...] = normed
    step = min(256, up_w_ref.shape[1])
    for start in range(0, up_w_ref.shape[1], step):
        block = slice(start, start + step)
        up = dot(normed, up_w_ref[:, block])
        mass = gelu_mass(up)
        active_ref[:, block] = (up * mass).astype(LOW)
        slope_ref[:, block] = gelu_slope(up, mass)


def back_again_kernel(own_ref, other_ref, slope_ref, down_w_ref, grad_mlp_ref, grad_up_ref):
    grad_mlp = jnp.concatenate([own_ref[...].astype(LOW), other_ref[...].astype(LOW)], axis=0)
    grad_mlp_ref[...] = grad_mlp
    step = min(256, slope_ref.shape[1])
    for start in range(0, slope_ref.shape[1], step):
        block = slice(start, start + step)
        grad_up = dot_wide(grad_mlp, down_w_ref[block, :]) * slope_ref[:, block]
        grad_up_ref[:, block] = grad_up.astype(LOW)


def loss_kernel(
    first_row, grad_ref, norm_ref, hidden_ref, mine_ref, theirs_ref, block_ref, sums_ref, *back_refs
):
    half = mine_ref.shape[0]
    stat, inverse = normalize(mine_ref[...] + theirs_ref[...])
    block_ref[...] = hidden_ref[...] + stat * norm_ref[6:7, :] + norm_ref[7:8, :]
    incoming = grad_ref[pl.ds(first_row + core_index() * half, half), :].astype(WIDE)
    back, gain, offset = norm_back(incoming, stat, inverse, norm_ref[6:7, :])
    for back_ref in back_refs:
        back_ref[...] = back
    sums_ref[0:1, :] = gain
    sums_ref[1:2, :] = offset


def mlp_back_kernel(
    own_ref, other_ref, up_ref, up_w_ref, down_w_ref, grad_mlp_ref, grad_up_ref, send_ref, keep_ref
):
    half = own_ref.shape[0]
    grad_mlp = jnp.concatenate([own_ref[...].astype(LOW), other_ref[...].astype(LOW)], axis=0)
    grad_mlp_ref[...] = grad_mlp
    step = min(256, up_w_ref.shape[1])
    total = None
    for start in range(0, up_w_ref.shape[1], step):
        block = slice(start, start + step)
        up = up_ref[:, block]
        slope = gelu_slope(up, gelu_mass(up))
        grad_up = (dot_wide(grad_mlp, down_w_ref[block, :]) * slope).astype(LOW)
        grad_up_ref[:, block] = grad_up
        product = dot_wide(grad_up, up_w_ref[:, block])
        total = product if total is None else total + product
    keep_ref[...] = total[:half]
    send_ref[...] = total[half:]


def norms_back_kernel(
    first_row, grad_ref, norm_ref, hidden_ref, branch_ref, mine_ref, theirs_ref,
    grad_hidden_ref, back_ref, sums_ref,
):
    half = mine_ref.shape[0]
    stat, inverse = normalize(hidden_ref[...])
    back, gain, offset = norm_back(
        mine_ref[...] + theirs_ref[...], stat, inverse, norm_ref[4:5, :]
    )
    incoming = grad_ref[pl.ds(first_row + core_index() * half, half), :].astype(WIDE)
    grad_hidden = incoming + back
    grad_hidden_ref[...] = grad_hidden
    sums_ref[2:3, :] = gain
    sums_ref[3:4, :] = offset
    stat, inverse = normalize(branch_ref[...])
    back, gain, offset = norm_back(grad_hidden, stat, inverse, norm_ref[2:3, :])
    back_ref[...] = back
    sums_ref[0:1, :] = gain
    sums_ref[1:2, :] = offset


def attention_back_kernel(live_ref, out_low_ref, cos_ref, sin_ref, *refs, chunks):
    groups = [refs[i * chunks : (i + 1) * chunks] for i in range(6)]
    own, other, query_refs, key_refs, value_refs, mass_refs = groups
    grad_branch_ref, rows_ref = refs[6 * chunks : 6 * chunks + 2]
    keys_sum, values_sum = refs[6 * chunks + 2 :]
    half = own[0].shape[0]
    part = 2 * half
    core = core_index()
    live_len = live_ref[0]
    local = rows_ref.shape[1] // 3
    heads = local // HEAD_DIM
    for c in range(chunks):
        grad_branch_ref[pl.ds(c * part + core * half, half), :] = own[c][...].astype(LOW)
        grad_branch_ref[pl.ds(c * part + (1 - core) * half, half), :] = other[c][...].astype(LOW)
    keys_all = jnp.concatenate([ref[...] for ref in key_refs], axis=0)
    values_all = jnp.concatenate([ref[...] for ref in value_refs], axis=0)
    for c in range(chunks):
        reach = (c + 1) * part
        first_row = c * part
        row = first_row + lax.broadcasted_iota(jnp.int32, (part, reach), 0)
        column = lax.broadcasted_iota(jnp.int32, (part, reach), 1)
        visible = (column <= row) & (column < live_len)
        live = first_row + lax.broadcasted_iota(jnp.int32, (part, 1), 0) < live_len
        grad_attn = dot_wide(grad_branch_ref[first_row : first_row + part, :], out_low_ref[...])
        grad_mixed = jnp.where(live, grad_attn, 0.0).astype(LOW)
        query, masses = query_refs[c][...], mass_refs[c][...]
        keys, values = keys_all[:reach], values_all[:reach]
        grad_query = jnp.zeros((part, local), WIDE)
        grad_keys = jnp.zeros((reach, local), WIDE)
        grad_values = jnp.zeros((reach, local), WIDE)
        for head in range(heads):
            query_h, grad_h = of_head(query, head), of_head(grad_mixed, head)
            scores = dot_wide(query_h, keys) * HEAD_DIM ** (-0.5)
            scores = jnp.where(visible, scores, mask_fill)
            probs = jnp.exp(scores - masses[:, head : head + 1])
            grad_values = grad_values + dot_rows(probs.astype(LOW), grad_h)
            grad_probs = dot_wide(grad_h, values)
            inner = jnp.sum(grad_probs * probs, axis=-1, keepdims=True)
            grad_scores = (probs * (grad_probs - inner)).astype(LOW)
            grad_query = grad_query + dot(grad_scores, of_head(keys, head))
            grad_keys = grad_keys + dot_rows(grad_scores, query_h)
        cosine = cos_ref[first_row : first_row + part, :]
        sine = sin_ref[first_row : first_row + part, :]
        grad_query = turn(grad_query * HEAD_DIM ** (-0.5), cosine, -sine)
        rows_ref[first_row : first_row + part, 0:local] = grad_query.astype(LOW)
        if c == 0:
            keys_sum[0:reach, :] = grad_keys
            values_sum[0:reach, :] = grad_values
        else:
            keys_sum[0:first_row, :] += grad_keys[:first_row]
            keys_sum[first_row:reach, :] = grad_keys[first_row:]
            values_sum[0:first_row, :] += grad_values[:first_row]
            values_sum[first_row:reach, :] = grad_values[first_row:]
    grad_keys = turn(keys_sum[...] * HEAD_DIM ** (-0.5), cos_ref[...], -sin_ref[...])
    rows_ref[:, local : 2 * local] = grad_keys.astype(LOW)
    rows_ref[:, 2 * local : 3 * local] = values_sum[...].astype(LOW)


def picked_columns(refs, chunks, own):
    blocks = []
    for chunk in chunks:
        start = pl.multiple_of(chunk * own, own)
        pieces = [ref[:, pl.ds(start, own)].astype(LOW) for ref in refs]
        blocks.append(pieces[0] if len(pieces) == 1 else jnp.concatenate(pieces, axis=0))
    return blocks[0] if len(blocks) == 1 else jnp.concatenate(blocks, axis=1)


def whole_rows(refs, window):
    pieces = [ref[:, window[0] : window[1]].astype(LOW) for ref in refs]
    return pieces[0] if len(pieces) == 1 else jnp.concatenate(pieces, axis=0)


def owned_columns_kernel(*refs, pairs, jobs, own):
    (lefts, rights), outs = pairs, refs[sum(pairs) :]
    left, right = refs[:lefts], refs[lefts : lefts + rights]
    for (order, window, blocks), out_ref in zip(jobs, outs):
        chunks = order(lax.axis_index("dp"))
        rows = whole_rows(left[:blocks], window)
        product = dot_rows(rows, picked_columns(right[:blocks], chunks, own))
        for place in range(len(chunks)):
            out_ref[place] = product[:, place * own : (place + 1) * own]


def owned_rows_kernel(*refs, pairs, jobs, own):
    (lefts, rights), outs = pairs, refs[sum(pairs) :]
    left, right = refs[:lefts], refs[lefts : lefts + rights]
    for (order, window, blocks), out_ref in zip(jobs, outs):
        chunks = order(lax.axis_index("dp"))
        product = dot_rows(
            picked_columns(left[:blocks], chunks, own), whole_rows(right[:blocks], window)
        )
        for place in range(len(chunks)):
            out_ref[place] = product[place * own : (place + 1) * own, :]


def owned_parts_kernel(*refs, pairs, jobs, own):
    (lefts, rights), outs = pairs, refs[sum(pairs) :]
    left, right = refs[:lefts], refs[lefts : lefts + rights]
    for (order, window, blocks), out_ref in zip(jobs, outs):
        chunks = order(lax.axis_index("dp"))
        local = out_ref.shape[3]
        columns = (window[0] * local, window[1] * local)
        product = dot_rows(picked_columns(left, chunks, own), whole_rows(right, columns))
        for place in range(len(chunks)):
            for j in range(window[1] - window[0]):
                out_ref[place, j] = product[
                    place * own : (place + 1) * own, j * local : (j + 1) * local
                ]


def rounded_kernel(*refs):
    refs[-1][...] = whole_rows(refs[:-1], (0, refs[0].shape[1]))


def narrow_products(line, kernel, left, right, jobs, outs, own):
    joined = []
    for arrays in (left, right):
        rows = sum(array.shape[0] for array in arrays)
        low = shaped(rows, arrays[0].shape[1], kind=LOW)
        joined.append(line.call(rounded_kernel, [low], arrays)[0])
    results = []
    for (order, window, _), out in zip(jobs, outs):
        chunks = order(lax.axis_index("dp"))
        pick = lambda array: jnp.concatenate(
            [lax.dynamic_slice_in_dim(array, chunk * own, own, 1) for chunk in chunks], axis=1
        )
        if kernel is owned_columns_kernel:
            product = dot_rows(joined[0][:, window[0] : window[1]], pick(joined[1]))
            product = product.reshape(-1, len(chunks), own).transpose(1, 0, 2)
        elif kernel is owned_rows_kernel:
            product = dot_rows(pick(joined[0]), joined[1][:, window[0] : window[1]])
            product = product.reshape(out.shape)
        else:
            local = out.shape[3]
            columns = joined[1][:, window[0] * local : window[1] * local]
            product = dot_rows(pick(joined[0]), columns)
            product = product.reshape(len(chunks), own, -1, local).transpose(0, 2, 1, 3)
        results.append(product)
    return results


def owner_products(line, kernel, left, right, pieces, own, send, blocks=None):
    jobs, outs = [], []
    for piece in pieces:
        half = piece.route.held // 2
        part = slice(half, None) if send else slice(half)
        order = lambda rank, route=piece.route, part=part: route.order(rank)[part]
        jobs.append((order, piece.window, None if piece.joined else blocks))
        size = piece.window[1] - piece.window[0]
        if kernel is owned_columns_kernel:
            outs.append(shaped(half, size, own))
        elif kernel is owned_rows_kernel:
            outs.append(shaped(half, own, size))
        else:
            outs.append(shaped(half, size, own, right[0].shape[1] // 3))
    if own % LANES:
        return narrow_products(line, kernel, left, right, jobs, outs, own)
    return line.call(
        functools.partial(kernel, pairs=(len(left), len(right)), jobs=jobs, own=own),
        outs,
        [*left, *right],
        megabytes=20,
    )


def input_back_kernel(rows_ref, qkv_low_ref, send_ref, keep_ref, *, chunks):
    half = send_ref.shape[0] // chunks
    local = qkv_low_ref.shape[2]
    core = core_index()
    for c in range(chunks):
        for target, which in ((send_ref, 1 - core), (keep_ref, core)):
            rows = rows_ref[pl.ds(c * 2 * half + which * half, half), :]
            total = None
            for j in range(3):
                product = dot_wide(rows[:, j * local : (j + 1) * local], qkv_low_ref[j])
                total = product if total is None else total + product
            target[c * half : (c + 1) * half, :] = total


def input_norm_kernel(x_ref, norm_ref, mine_ref, theirs_ref, *refs, chunks):
    grad_hidden = refs[:chunks]
    rows_ref, sums_ref = refs[chunks:]
    half = mine_ref.shape[0] // chunks
    core = core_index()
    gains = offsets = None
    for c in range(chunks):
        rows = slice(c * half, (c + 1) * half)
        inputs = x_ref[pl.ds(c * 2 * half + core * half, half), :].astype(WIDE)
        stat, inverse = normalize(inputs)
        back, gain, offset = norm_back(
            mine_ref[rows, :] + theirs_ref[rows, :], stat, inverse, norm_ref[0:1, :]
        )
        rows_ref[rows, :] = grad_hidden[c][...] + back
        gains = gain if gains is None else gains + gain
        offsets = offset if offsets is None else offsets + offset
    sums_ref[0:1, :] = gains
    sums_ref[1:2, :] = offsets


def place_kernel(mine_ref, theirs_ref, out_ref, *, chunks):
    half = mine_ref.shape[0] // chunks
    core = core_index()
    for c in range(chunks):
        rows = slice(c * half, (c + 1) * half)
        out_ref[pl.ds((2 * c + core) * half, half), :] = mine_ref[rows, :].astype(LOW)
        out_ref[pl.ds((2 * c + 1 - core) * half, half), :] = theirs_ref[rows, :].astype(LOW)


def rows_kernel(source_ref, target_ref):
    target_ref[...] = source_ref[...]


def norm_sums_kernel(*refs, chunks):
    input_ref, norms, losses, out_ref = refs[0], refs[1 : 1 + chunks], refs[1 + chunks : -1], refs[-1]
    out_ref[0:2, :] = input_ref[...]
    out_ref[2:6, :] = sum(ref[...] for ref in norms[1:]) + norms[0][...]
    out_ref[6:8, :] = sum(ref[...] for ref in losses[1:]) + losses[0][...]


def stage_kernel(*refs, counts, crossed):
    terms, outs = refs[3 : 3 + sum(counts)], refs[3 + sum(counts) :]
    for source, target in zip(refs[:3], outs[:3]):
        target[...] = source[...]
    at = 0
    for count, out_ref, cross in zip(counts, outs[3:], crossed):
        out_ref[...] = gathered([term[...] for term in terms[at : at + count]], cross)
        at += count


def finish_kernel(gradient_ref, first_ref, second_ref, first_new_ref, second_new_ref):
    first_new, second_new, _ = moment_step(gradient_ref[...], first_ref[...], second_ref[...])
    first_new_ref[...] = first_new
    second_new_ref[...] = second_new


def moment_step(gradient, first_state, second_state):
    first_new = first_decay * first_state + (1.0 - first_decay) * gradient
    second_new = second_decay * second_state + (1.0 - second_decay) * gradient * gradient
    direction = (
        first_new
        / (1.0 - first_decay**STEP)
        / (jnp.sqrt(second_new / (1.0 - second_decay**STEP)) + adam_epsilon)
    )
    return (first_new, second_new, direction)


def total_of(values):
    rows = values.reshape(-1, values.shape[-1])
    return jnp.sum(jnp.sum(rows, axis=0, keepdims=True), axis=1, keepdims=True)


def moments_kernel(
    master_ref, first_ref, second_ref, squares_ref, *refs, row, regions, counts, crossed, late
):
    table_ref = refs[-1]
    kept_ref, update_ref, *moment_refs = refs[sum(counts) : -1]
    at = 0
    sizes = []
    for region, count, cross in zip(regions, counts, crossed):
        gradient = gathered([term[...] for term in refs[at : at + count]], cross)
        at += count
        first_new, second_new, direction = moment_step(
            gradient, first_ref[region], second_ref[region]
        )
        for target, found in zip(moment_refs, [gradient] if late else [first_new, second_new]):
            target[region] = found
        master = master_ref[region]
        kept_ref[region] = master
        update = direction + decay_rate * master
        update_ref[region] = update
        sizes.append((total_of(master * master), total_of(update * update)))
    table_ref[...] = squares_ref[...]
    for place, size in ((row, 0), (row + 4, 1)):
        amount = sizes[0][size]
        for other in sizes[1:]:
            amount = amount + other[size]
        table_ref[place : place + 1, :] = jnp.broadcast_to(amount, (1, LANES))


def join_kernel(*refs):
    terms, norms_ref, out_ref = refs[:-2], refs[-2], refs[-1]
    terms = [ref[...] for ref in terms]
    while len(terms) > 1:
        terms = [terms[i] + terms[i + 1] for i in range(0, len(terms), 2)]
    out_ref[:, 0:LANES] = terms[0]
    out_ref[:, LANES:] = norms_ref[...]


def masters_kernel(norm_ref, first_ref, second_ref, *refs, terms, own):
    sums, refs = refs[:terms], refs[terms:]
    masters, updates, outs = refs[:4], refs[4:8], refs[8:12]
    norms_ref, norm_new_ref, first_new_ref, second_new_ref = refs[12:]
    total = sums[0][:, 0:LANES]
    for ref in sums[1:]:
        total = total + ref[:, 0:LANES]
    sizes = jnp.sqrt(total[0:4, :])
    steps = jnp.sqrt(total[4:8, :] + trust_epsilon)
    lane = lax.broadcasted_iota(jnp.int32, (1, 4), 1)
    for place, found in ((0, sizes), (1, steps)):
        row = jnp.zeros((1, 4), WIDE)
        for index in range(4):
            row = jnp.where(lane == index, found[index : index + 1, 0:1], row)
        norms_ref[place : place + 1, :] = row
    ratio = learn_rate * (sizes / steps)
    for index in range(4):
        scale = ratio[index : index + 1, 0:1]
        if len(masters[index].shape) == 3:
            scale = scale.reshape(1, 1, 1)
        outs[index][...] = masters[index][...] - scale * updates[index][...]
    if own % LANES:
        gradient = sums[0][:, LANES:]
        for ref in sums[1:]:
            gradient = gradient + ref[:, LANES:]
        norm_new_ref[...] = gradient
        return
    start = pl.multiple_of(lax.axis_index("dp") * own, own)
    gradient = sums[0][:, pl.ds(LANES + start, own)]
    for ref in sums[1:]:
        gradient = gradient + ref[:, pl.ds(LANES + start, own)]
    first_new, second_new, direction = moment_step(gradient, first_ref[...], second_ref[...])
    first_new_ref[...] = first_new
    second_new_ref[...] = second_new
    norm_new_ref[...] = norm_ref[:, pl.ds(start, own)] - learn_rate * direction


def shards(
    block_input,
    lengths,
    norm_params,
    qkv_weight,
    out_weight,
    up_weight,
    down_weight,
    qkv_first,
    qkv_second,
    out_first,
    out_second,
    up_first,
    up_second,
    down_first,
    down_second,
    norm_first,
    norm_second,
    out_grad,
):
    row_count, width = block_input.shape
    local = qkv_weight.shape[2]
    hidden_units = up_weight.shape[1]
    group_count = lax.axis_size("dp")
    own = width // group_count
    own_start = lax.axis_index("dp") * own
    part = row_count // CHUNKS
    half = part // 2
    chunks = range(CHUNKS)
    bits = list(range(log2_of(group_count)))

    line = Line()
    qkv_parts = jnp.transpose(qkv_weight, (1, 0, 2))
    cosine, sine = rotary_tables(row_count)
    live = Raw(lengths, SMEM)
    joined = group_count == 8 and own % LANES == 0

    def relay_of(theirs):
        copied = line.call(rows_kernel, [cut(half, width, CUT_RELAY)], [theirs])[0]
        return theirs, near(copied)

    weight_shapes = [shaped(3, width, local, kind=LOW), shaped(local, width, kind=LOW)]
    chunk_shapes = [
        shaped(part, width, kind=LOW),
        shaped(part, local, kind=LOW),
        shaped(part, local, kind=LOW),
        shaped(part, local, kind=LOW),
        shaped(part, local, kind=LOW),
        shaped(part, LANES),
        cut(half, width, CUT_ATTENTION),
        shaped(half, width),
    ]
    low_weights, parts, branch_terms = [], [], []

    def attention(c):
        if c == 0:
            outs = line.call(
                first_kernel,
                weight_shapes + chunk_shapes,
                [live]
                + [
                    Raw(a, HBM)
                    for a in (block_input, norm_params, cosine, sine, qkv_parts, out_weight)
                ],
                scratch=[
                    pltpu.VMEM((part, width), LOW),
                    pltpu.VMEM(norm_params.shape, WIDE),
                    pltpu.VMEM((part, LANES), WIDE),
                    pltpu.VMEM((part, LANES), WIDE),
                    pltpu.VMEM((3, width, local), WIDE),
                    pltpu.VMEM((local, width), WIDE),
                    pltpu.SemaphoreType.DMA((8,)),
                ],
                megabytes=60,
                first=True,
            )
            low_weights.extend(outs[:2])
            outs = outs[2:]
        else:
            before = [p[2] for p in parts] + [p[3] for p in parts]
            outs = line.call(
                functools.partial(next_kernel, first_row=c * part, part=part),
                chunk_shapes,
                [live, block_input, norm_params, cosine, sine, *low_weights, *before],
            )
        parts.append(outs)
        branch_terms.append((outs[7], near(outs[6])))

    def sum_branch(c):
        branch_terms[c] = sum_rows(line, *branch_terms[c])

    def cast(weight):
        return line.call(cast_kernel, [shaped(*weight.shape, kind=LOW)], [Take(weight)])[0]

    branch, hidden, normed_mid, up, active, mlp_terms = [], [], [], [], [], []
    normed_other, ships, normed_theirs, active_theirs, slope_theirs = [], [], [], [], []

    def middle(c):
        outs = line.call(
            functools.partial(middle_kernel, c * part),
            [shaped(half, width), shaped(half, width), cut(half, width, CUT_MIDDLE)]
            + [shaped(half, width)] * joined,
            [block_input, norm_params, *branch_terms[c]],
        )
        branch.append(outs[0])
        hidden.append(outs[1])
        normed_other.append((outs[2], near(outs[2])))
        ships.append(swap(outs[3], "dp", 2) if joined else None)

    def relay(c):
        if joined:
            ships[c] = relay_of(ships[c])

    def mlp(c):
        outs = line.call(
            mlp_kernel,
            [
                shaped(part, width, kind=LOW),
                shaped(part, hidden_units),
                shaped(part, hidden_units, kind=LOW),
                cut(half, width, CUT_MLP),
                shaped(half, width),
            ],
            [*normed_other[c], up_low, down_low],
        )
        normed_mid.append(outs[0])
        up.append(outs[1])
        active.append(outs[2])
        mlp_terms.append((outs[4], near(outs[3])))

    def sum_mlp(c):
        mlp_terms[c] = sum_rows(line, *mlp_terms[c])

    def again(c):
        if joined:
            outs = line.call(
                again_kernel,
                [
                    shaped(part, width, kind=LOW),
                    shaped(part, hidden_units, kind=LOW),
                    shaped(part, hidden_units),
                ],
                [*ships[c], up_low],
            )
            normed_theirs.append(outs[0])
            active_theirs.append(outs[1])
            slope_theirs.append(outs[2])

    line.own, line.table = own, jnp.zeros((8, LANES), WIDE)
    route_a, route_b, route_j = routes(group_count)
    columns = lambda: (slice(None), pl.ds(pl.multiple_of(lax.axis_index("dp") * own, own), own))
    rows = lambda: (pl.ds(pl.multiple_of(lax.axis_index("dp") * own, own), own),)
    part_rows = lambda: (slice(None), *rows())
    mine = lambda array, axis: lax.dynamic_slice_in_dim(array, own_start, own, axis)
    block_rows, loss_sums, grad_final, grad_up_rows, mid_terms = [], [], [], [], []
    grad_mlp, grad_mlp_theirs, grad_up_theirs, ships_back = [], [], [], []
    grad_hidden, norms_sums, own_back, other_back = [], [], [], []
    flip = lambda array: jnp.transpose(array, (1, 0, 2))
    qkv = Weight(
        line,
        0,
        3,
        owned_parts_kernel,
        lambda: ([p[0] for p in parts], [grad_rows]),
        lambda: ([p[0] for p in parts], [grad_rows]),
        Take(qkv_parts, (3, own, local), part_rows),
        [flip(qkv_first), flip(qkv_second)],
    )
    out = Weight(
        line,
        1,
        local,
        owned_columns_kernel,
        lambda: ([p[4] for p in parts], [grad_branch]),
        lambda: ([p[4] for p in parts], [grad_branch]),
        Take(mine(out_weight, 1)) if own % LANES else Take(out_weight, (local, own), columns),
        [out_first, out_second],
    )
    up_matrix = Weight(
        line,
        2,
        hidden_units,
        owned_rows_kernel,
        lambda: (normed_mid + normed_theirs, grad_up_rows + grad_up_theirs),
        lambda: (normed_mid, grad_up_rows),
        Take(up_weight, (own, hidden_units), rows),
        [up_first, up_second],
    )
    down = Weight(
        line,
        3,
        hidden_units,
        owned_columns_kernel,
        lambda: (active + active_theirs, grad_mlp + grad_mlp_theirs),
        lambda: (active, [block for pair in grad_final for rows in pair for block in rows]),
        Take(mine(down_weight, 1))
        if own % LANES
        else Take(down_weight, (hidden_units, own), columns),
        [down_first, down_second],
    )
    d0 = down.piece(0, 8, 8, route_j)
    u0 = up_matrix.piece(0, 8, 8, route_j)
    q0 = qkv.piece(0, 2, 3, route_b)
    q1 = qkv.piece(2, 3, 3, route_b)
    o0 = out.piece(0, 1, 1, route_b)


    def loss(c):
        outs = line.call(
            functools.partial(loss_kernel, c * part),
            [shaped(half, width), shaped(2, width), cut(half, width, CUT_LOSS)]
            + [shaped(half, width)] * joined,
            [out_grad, norm_params, hidden[c], *mlp_terms[c]],
        )
        block_rows.append(outs[0])
        loss_sums.append(outs[1])
        grad_final.append((outs[2], near(outs[2])))
        ships_back.append(swap(outs[3], "dp", 2) if joined else None)

    def back_relay(c):
        if joined:
            ships_back[c] = relay_of(ships_back[c])

    def mlp_back(c):
        outs = line.call(
            mlp_back_kernel,
            [
                shaped(part, width, kind=LOW),
                shaped(part, hidden_units, kind=LOW),
                cut(half, width, CUT_MLP if c < CHUNKS - 1 else CUT_MID),
                shaped(half, width),
            ],
            [*grad_final[c], up[c], up_low, down_low],
        )
        grad_mlp.append(outs[0])
        grad_up_rows.append(outs[1])
        mid_terms.append((outs[3], near(outs[2])))

    def back_again(c):
        if joined:
            outs = line.call(
                back_again_kernel,
                [shaped(part, width, kind=LOW), shaped(part, hidden_units, kind=LOW)],
                [*ships_back[c], slope_theirs[c], down_low],
            )
            grad_mlp_theirs.append(outs[0])
            grad_up_theirs.append(outs[1])

    def sum_mid(c):
        mid_terms[c] = sum_rows(line, *mid_terms[c])

    def norms(c):
        outs = line.call(
            functools.partial(norms_back_kernel, c * part),
            [shaped(half, width), cut(half, width, CUT_NORMS), shaped(4, width)],
            [out_grad, norm_params, hidden[c], branch[c], *mid_terms[c]],
        )
        grad_hidden.append(outs[0])
        norms_sums.append(outs[2])
        own_back.append(outs[1])
        other_back.append(near(outs[1]))

    def attention_back():
        return line.call(
            functools.partial(attention_back_kernel, chunks=CHUNKS),
            [shaped(row_count, width, kind=LOW), shaped(row_count, 3 * local, kind=LOW)],
            [live, low_weights[1], cosine, sine, *own_back, *other_back]
            + [p[which] for which in (1, 2, 3, 5) for p in parts],
            scratch=[pltpu.VMEM((row_count, local), WIDE), pltpu.VMEM((row_count, local), WIDE)],
        )

    def input_back():
        return line.call(
            functools.partial(input_back_kernel, chunks=CHUNKS),
            [cut(row_count // 2, width, CUT_BACK), shaped(row_count // 2, width)],
            [grad_rows, low_weights[0]],
        )

    def input_norm():
        return line.call(
            functools.partial(input_norm_kernel, chunks=CHUNKS),
            [cut(row_count // 2, width, CUT_INPUT), shaped(2, width)],
            [block_input, norm_params, *in_terms, *grad_hidden],
        )

    def send_output():
        return line.call(
            rows_kernel, [cut(row_count // 2, width, CUT_OUTPUT)], [block_rows]
        )[0]

    def place(blocks, others):
        return line.call(
            functools.partial(place_kernel, chunks=CHUNKS),
            [shaped(row_count, width, kind=LOW)],
            [blocks, others],
        )[0]

    def norm_sums():
        return line.call(
            functools.partial(norm_sums_kernel, chunks=CHUNKS),
            [shaped(8, width)],
            [input_sums, *norms_sums, *loss_sums],
        )[0]

    def sum_norms():
        return line.call(
            sum_kernel, [shaped(8, width)], [grad_norms, norms_other]
        )[0]

    attention(0)
    sum_branch(0)
    attention(1)
    sum_branch(1)
    up_low = cast(up_weight)
    down_low = cast(down_weight)
    middle(0)
    mlp(0)
    sum_mlp(0)
    middle(1)
    mlp(1)
    relay(0)
    sum_mlp(1)
    loss(0)
    mlp_back(0)
    again(0)
    relay(1)
    sum_mid(0)
    loss(1)
    back_relay(0)
    again(1)
    mlp_back(1)
    norms(0)
    sum_mid(1)
    back_again(0)
    back_relay(1)
    back_again(1)
    d0.start()
    down.hold()
    u0.start()
    norms(1)
    grad_branch, grad_rows = attention_back()
    send, keep = input_back()
    crossing = near(send)
    q0.start()
    in_terms = sum_rows(line, keep, crossing)
    qkv.hold()
    sent_rows = send_output()
    block_other = near(sent_rows)
    o0.start()
    d0.advance()
    q1.start()
    block_output = place(sent_rows, block_other)
    up_matrix.hold()
    q0.advance()
    u0.advance()
    d0.advance()
    q1.advance()
    out.hold()
    input_rows, input_sums = input_norm()
    input_other = near(input_rows)
    q0.advance()
    o0.advance()
    input_grad = place(input_rows, input_other)
    u0.advance()
    o0.advance()
    down.moments()
    q1.advance()
    q0.advance()
    o0.advance()
    q1.advance()
    up_matrix.moments()
    out.moments()
    grad_norms = norm_sums()
    norms_other = swap(grad_norms, "tensor", 1)
    grad_norms = sum_norms()
    qkv.stage()
    qkv.moments()

    tensor_bits = log2_of(lax.axis_size("tensor"))
    found = line.table
    for start in range(0, tensor_bits, 2):
        terms = sum_terms(found, "tensor", start, min(2, tensor_bits - start))
        if start == 0:
            qkv.finish()
        if start + 2 >= tensor_bits:
            found = line.call(join_kernel, [shaped(8, LANES + width)], [*terms, grad_norms])[0]
        else:
            found = line.call(pairs_kernel, [shaped(8, LANES)], terms)[0]
    for start in range(0, len(bits), 2):
        terms = sum_terms(found, "dp", start, min(2, len(bits) - start))
        if start + 2 < len(bits) or len(terms) > 2:
            found = line.call(pairs_kernel, [shaped(8, LANES + width)], terms)[0]
            terms = [found]
    weights = (qkv, out, up_matrix, down)
    outs = line.call(
        functools.partial(masters_kernel, terms=len(terms), own=own),
        [shaped(*weight.kept.shape) for weight in weights]
        + [shaped(2, 4), shaped(8, width if own % LANES else own), shaped(8, own), shaped(8, own)],
        [
            norm_params,
            norm_first,
            norm_second,
            *terms,
            *[weight.kept for weight in weights],
            *[weight.update for weight in weights],
        ],
    )
    matrix_norms, norm_new, norm_first_new, norm_second_new = outs[4:]
    if own % LANES:
        norm_first_new, norm_second_new, direction = moment_step(
            mine(norm_new, 1), norm_first, norm_second
        )
        norm_new = mine(norm_params, 1) - learn_rate * direction
    return (
        block_output,
        input_grad,
        flip(outs[0]),
        flip(qkv.first_new),
        flip(qkv.second_new),
        outs[1],
        out.first_new,
        out.second_new,
        outs[2],
        up_matrix.first_new,
        up_matrix.second_new,
        outs[3],
        down.first_new,
        down.second_new,
        norm_new,
        norm_first_new,
        norm_second_new,
        matrix_norms,
    )


def solution(mesh):
    in_specs = (
        P("dp", None),
        P("dp"),
        P(),
        P(None, None, "tensor"),
        P("tensor", None),
        P(None, "tensor"),
        P("tensor", None),
        P("dp", None, "tensor"),
        P("dp", None, "tensor"),
        P("tensor", "dp"),
        P("tensor", "dp"),
        P("dp", "tensor"),
        P("dp", "tensor"),
        P("tensor", "dp"),
        P("tensor", "dp"),
        P(None, "dp"),
        P(None, "dp"),
        P("dp", None),
    )
    out_specs = (
        P("dp", None),
        P("dp", None),
        P("dp", None, "tensor"),
        P("dp", None, "tensor"),
        P("dp", None, "tensor"),
        P("tensor", "dp"),
        P("tensor", "dp"),
        P("tensor", "dp"),
        P("dp", "tensor"),
        P("dp", "tensor"),
        P("dp", "tensor"),
        P("tensor", "dp"),
        P("tensor", "dp"),
        P("tensor", "dp"),
        P(None, "dp"),
        P(None, "dp"),
        P(None, "dp"),
        P(),
    )
    return jax.shard_map(shards, mesh=mesh, in_specs=in_specs, out_specs=out_specs, check_vma=False)
```

```python
import functools

import jax
import jax.numpy as jnp
import numpy as np
from jax import lax
from jax.experimental import pallas as pl
from jax.experimental.pallas import tpu as pltpu
from jax.sharding import PartitionSpec as P

HEAD_DIM = 64
STEP = 10
CHUNKS = 2
LANES = 128

norm_epsilon = 1e-05
rotary_base = 10000.0
mask_fill = -1000000000.0
first_decay = 0.9
second_decay = 0.999
adam_epsilon = 1e-06
trust_epsilon = 1e-06
decay_rate = 0.01
learn_rate = 0.25

CUT_ATTENTION, CUT_MIDDLE, CUT_MLP, CUT_LOSS = 4, 4, 4, 4
CUT_RELAY = 2
CUT_MID, CUT_NORMS, CUT_BACK, CUT_INPUT, CUT_OUTPUT = 2, 2, 4, 2, 4

LOW = jnp.bfloat16
WIDE = jnp.float32
VMEM = pl.BlockSpec(memory_space=pltpu.VMEM)
SMEM = pl.BlockSpec(memory_space=pltpu.SMEM)
HBM = pl.BlockSpec(memory_space=pltpu.HBM)


def log2_of(count):
    bits = 0
    while (1 << bits) < count:
        bits += 1
    return bits


def swap(values, axis, distance):
    count = lax.axis_size(axis)
    return lax.ppermute(values, axis, [(i, i ^ distance) for i in range(count)])


class Route:
    def __init__(self, order, steps, held, joined=False):
        self.order, self.steps, self.held, self.joined = order, steps, held, joined


HALF, CROSS, BACK = range(3)


def apart(count, distance, among=None):
    return [(i, i ^ distance) for i in (range(count) if among is None else among)]


def outside(rank):
    place = lax.div(rank, 2)
    return (place == 0) | (place == 3)


def line_chunks(rank):
    place = lax.div(rank, 2)
    beside, side = lax.bitwise_xor(place, 1), lax.div(place, 2)
    near, far = (place, beside), (2 - side, 3 - 3 * side)
    end = outside(rank)
    keep = [jnp.where(end, a, b) for a, b in zip(near, far)]
    send = [jnp.where(end, a, b) for a, b in zip(far, (beside, place))]
    return keep, send


def routes(count):
    if count == 8:

        def across_first(rank):
            keep, send = line_chunks(rank)
            row = lax.rem(rank, 2)
            return [place * 2 + y for y in (row, 1 - row) for place in keep + send]

        def along_first(rank):
            keep, send = line_chunks(rank)
            row = lax.rem(rank, 2)
            return [place * 2 + y for part in (keep, send) for y in (row, 1 - row) for place in part]

        def joined(rank):
            keep, _ = line_chunks(rank)
            row = lax.rem(rank, 2)
            return [place * 2 + y for y in (row, 1 - row) for place in keep]

        across = (HALF, apart(8, 1))
        along, back = (HALF, apart(8, 2)), (BACK, apart(8, 2))
        cross = (CROSS, apart(8, 6, range(2, 6)))
        return (
            Route(across_first, [across, along, cross, back], 8),
            Route(along_first, [along, across, cross, back], 8),
            Route(joined, [across, cross, back], 4, True),
        )
    order = [0]
    bits = range(log2_of(count))
    for bit in reversed(bits):
        order = order + [distance ^ (1 << bit) for distance in order]
    found = Route(
        lambda rank: [lax.bitwise_xor(rank, distance) for distance in order],
        [(HALF, apart(count, 1 << bit)) for bit in bits],
        count,
    )
    return found, found, found


def normalize(values):
    center = values - jnp.mean(values, axis=-1, keepdims=True)
    inverse = lax.rsqrt(jnp.mean(center * center, axis=-1, keepdims=True) + norm_epsilon)
    return center * inverse, inverse


def norm_back(incoming, normed, inverse, gain):
    scaled = incoming * gain
    inner = (
        scaled
        - jnp.mean(scaled, axis=-1, keepdims=True)
        - normed * jnp.mean(scaled * normed, axis=-1, keepdims=True)
    )
    gain_grad = jnp.sum(incoming * normed, axis=0, keepdims=True)
    return inner * inverse, gain_grad, jnp.sum(incoming, axis=0, keepdims=True)


def rotary_tables(length):
    half = HEAD_DIM // 2
    lane = np.arange(LANES)
    frequency = (rotary_base ** (-((lane % half).astype(np.float32) * 2.0 / HEAD_DIM))).astype(np.float32)
    angles = np.arange(length, dtype=np.float32)[:, None] * frequency[None, :]
    sign = np.where(lane % HEAD_DIM < half, -1.0, 1.0)
    cosine = np.cos(angles.astype(np.float64)).astype(np.float32)
    sine = (np.sin(angles.astype(np.float64)) * sign[None, :]).astype(np.float32)
    return jnp.asarray(cosine), jnp.asarray(sine)


def turn(values, cosine, sine):
    half = HEAD_DIM // 2
    lane = lax.broadcasted_iota(jnp.int32, (1, LANES), 1)
    first = lax.rem(lane, HEAD_DIM) < half
    tiles = []
    for start in range(0, values.shape[1], LANES):
        tile = values[:, start : start + LANES]
        other = jnp.where(
            first, pltpu.roll(tile, LANES - half, 1), pltpu.roll(tile, half, 1)
        )
        tiles.append(tile * cosine + other * sine)
    return tiles[0] if len(tiles) == 1 else jnp.concatenate(tiles, axis=1)


def gelu_mass(up):
    return 0.5 * (1.0 + lax.erf(up * (0.5**0.5)))


def gelu_slope(up, mass):
    return mass + up * jnp.exp(-0.5 * up * up) * float((2.0 * np.pi) ** -0.5)


def dot(left, right):
    return jnp.dot(left, right, preferred_element_type=WIDE)


def dot_rows(left, right):
    return lax.dot_general(left, right, (((0,), (0,)), ((), ())), preferred_element_type=WIDE)


def dot_wide(left, right):
    return lax.dot_general(left, right, (((1,), (1,)), ((), ())), preferred_element_type=WIDE)


def of_head(values, head):
    lane = lax.broadcasted_iota(jnp.int32, (1, values.shape[1]), 1)
    mine = (lane >= head * HEAD_DIM) & (lane < (head + 1) * HEAD_DIM)
    return jnp.where(mine, values, jnp.zeros_like(values))


def core_index():
    return lax.rem(lax.axis_index("tensor"), 2)


def shaped(*shape, kind=WIDE):
    return jax.ShapeDtypeStruct(shape, kind)


def cut(rows, width, count=4):
    return [shaped(rows // count, width)] * count


def near(values):
    return [swap(piece, "tensor", 1) for piece in values]


class Take:
    def __init__(self, array, shape=None, index=None):
        self.array = array
        self.shape = array.shape if shape is None else shape
        self.index = index


class Raw:
    def __init__(self, array, spec):
        self.array = array
        self.spec = spec


class Rows:
    def __init__(self, refs):
        self.refs = refs
        self.step = refs[0].shape[0]
        self.shape = (self.step * len(refs), refs[0].shape[1])

    def spans(self, key):
        first, last = 0, self.shape[0]
        if key is not Ellipsis and key[0] != slice(None):
            first, last = key[0].start, key[0].stop
        for place, ref in enumerate(self.refs):
            start, stop = max(first, place * self.step), min(last, (place + 1) * self.step)
            if start < stop:
                inside = slice(start - place * self.step, stop - place * self.step)
                yield ref, inside, slice(start - first, stop - first)

    def __getitem__(self, key):
        pieces = [ref[inside, :] for ref, inside, _ in self.spans(key)]
        return pieces[0] if len(pieces) == 1 else jnp.concatenate(pieces, axis=0)

    def __setitem__(self, key, value):
        for ref, inside, outside in self.spans(key):
            ref[inside, :] = value[outside]


class Line:
    def __init__(self):
        self.token = jnp.zeros((8, LANES), WIDE)

    def call(self, kernel, outs, args, scratch=(), megabytes=12, first=False):
        arrays, specs, buffers, layout, takes = [], [], [], [], []
        for arg in args:
            if isinstance(arg, Take):
                layout.append(0)
                takes.append((len(arrays), arg))
                arrays.append(arg.array)
                specs.append(HBM)
                buffers.append(pltpu.VMEM(arg.shape, arg.array.dtype))
            elif isinstance(arg, Raw):
                layout.append(0)
                arrays.append(arg.array)
                specs.append(arg.spec)
            elif isinstance(arg, (list, tuple)):
                layout.append(len(arg))
                arrays += arg
                specs += [VMEM] * len(arg)
            else:
                layout.append(0)
                arrays.append(arg)
                specs.append(VMEM)
        if takes:
            buffers.append(pltpu.SemaphoreType.DMA((len(takes),)))
        token = [] if first else [self.token]
        out_layout = [len(out) if isinstance(out, list) else 0 for out in outs]
        out_shapes = [o for out in outs for o in (out if isinstance(out, list) else [out])]

        def joined(refs, layout):
            refs = list(refs)
            return [
                Rows([refs.pop(0) for _ in range(count)]) if count else refs.pop(0)
                for count in layout
            ]

        def body(*refs):
            inputs = list(refs[: len(arrays)])
            rest = refs[len(arrays) + len(token) :]
            results, rest = rest[: len(out_shapes)], rest[len(out_shapes) + len(token) :]
            own, rest = rest[: len(scratch)], rest[len(scratch) :]
            copies = []
            for place, (i, take) in enumerate(takes):
                source = inputs[i]
                if take.index is not None:
                    source = source.at[take.index()]
                copies.append(pltpu.make_async_copy(source, rest[place], rest[-1].at[place]))
                inputs[i] = rest[place]
            for copy in copies:
                copy.start()
            for copy in copies:
                copy.wait()
            kernel(*joined(inputs, layout), *joined(results, out_layout), *own)

        results = pl.pallas_call(
            body,
            out_shape=(*out_shapes, *[shaped(8, LANES) for _ in token]),
            in_specs=[*specs, *[HBM for _ in token]],
            out_specs=tuple([VMEM] * len(out_shapes) + [HBM for _ in token]),
            scratch_shapes=[*scratch, *buffers],
            input_output_aliases={len(arrays): len(out_shapes)} if token else {},
            compiler_params=pltpu.CompilerParams(vmem_limit_bytes=megabytes * 1024 * 1024),
            cost_estimate=pl.CostEstimate(flops=0, bytes_accessed=0, transcendentals=0),
        )(*arrays, *token)
        found = list(results)
        if token:
            self.token = found.pop()
        return [
            [found.pop(0) for _ in range(count)] if count else found.pop(0) for count in out_layout
        ]


def sum_kernel(*refs):
    total = refs[0][...]
    for ref in refs[1:-1]:
        total = total + ref[...]
    refs[-1][...] = total


def pairs_kernel(*refs):
    terms = [ref[...] for ref in refs[:-1]]
    while len(terms) > 1:
        terms = [terms[i] + terms[i + 1] for i in range(0, len(terms), 2)]
    refs[-1][...] = terms[0]


def sum_rows(line, keep, arrived, count=1):
    mine, theirs = keep, arrived
    for bit in range(1, log2_of(lax.axis_size("tensor"))):
        mine = line.call(sum_kernel, [cut(*keep.shape, count)], [mine, theirs])[0]
        theirs = [swap(piece, "tensor", 1 << bit) for piece in mine]
    return mine, theirs


def sum_terms(values, axis, start, taken):
    return [values] + [swap(values, axis, distance << start) for distance in range(1, 1 << taken)]


def gathered(values, crossed):
    if crossed:
        first = jnp.where(outside(lax.axis_index("dp")), values[0], values[1])
        values = [first, *values[2:]]
    total = values[0]
    for value in values[1:]:
        total = total + value
    return total


def gather_kernel(*refs, crossed):
    refs[-1][...] = gathered([ref[...] for ref in refs[:-1]], crossed)


class Piece:
    def __init__(self, weight, window, route):
        self.weight, self.window, self.route = weight, window, route
        self.joined = route.joined
        self.terms, self.stage, self.crossed = [], 0, False

    def exchange(self, values):
        self.terms.append(lax.ppermute(values, "dp", self.route.steps[self.stage][1]))
        self.stage += 1

    def start(self):
        self.size = self.route.held // 2
        self.exchange(self.weight.products([self], True)[0])

    def sum_of(self, first, size):
        shape = (size,) + self.terms[0].shape[1:]
        index = lambda: (pl.ds(first, size),)
        return self.weight.line.call(
            functools.partial(gather_kernel, crossed=self.crossed),
            [shaped(*shape)],
            [Take(term, shape, index) for term in self.terms],
        )[0]

    def advance(self):
        if self.stage == len(self.route.steps):
            return
        if self.route.steps[self.stage][0] == CROSS:
            self.terms = [self.sum_of(0, self.size)]
            self.exchange(self.terms[0])
            self.crossed = True
        else:
            self.size //= 2
            self.exchange(self.sum_of(self.size, self.size))


class Weight:
    tables = {}

    def __init__(self, line, row, size, kernel, factors, mine, master, states):
        self.line, self.row, self.size, self.kernel = line, row, size, kernel
        self.factors, self.mine, self.master, self.states = factors, mine, master, states
        self.pieces = []

    def piece(self, first, last, count, route):
        found = Piece(self, (self.size * first // count, self.size * last // count), route)
        self.pieces.append(found)
        return found

    def products(self, pieces, send):
        line = self.line
        if any(piece.joined for piece in pieces):
            return owner_products(
                line, self.kernel, *self.factors(), pieces, line.own, send, CHUNKS
            )
        return owner_products(line, self.kernel, *self.mine(), pieces, line.own, send)

    def hold(self):
        for piece, keep in zip(self.pieces, self.products(self.pieces, False)):
            piece.terms.insert(0, keep)

    def stage(self):
        before = [self.master, *[Take(state) for state in self.states]]
        terms = [
            Take(term, term.shape[1:], lambda: (0,))
            for piece in self.pieces
            for term in piece.terms[:-1]
        ]
        crossed = [piece.crossed for piece in self.pieces]
        shapes = [shaped(*piece.terms[0].shape[1:]) for piece in self.pieces]
        counts = [len(piece.terms) - 1 for piece in self.pieces]
        self.master, *outs = self.line.call(
            functools.partial(stage_kernel, counts=counts, crossed=crossed),
            [shaped(*self.master.shape)] * 3 + shapes,
            before + terms,
        )
        self.states = outs[:2]
        self.partial = outs[2:]

    def moments(self):
        for piece in self.pieces:
            while piece.stage < len(piece.route.steps):
                piece.advance()
        everything = slice(None)
        if self.kernel is owned_rows_kernel:
            regions = [(everything, slice(*piece.window)) for piece in self.pieces]
        else:
            regions = [(slice(*piece.window),) for piece in self.pieces]
        late = not isinstance(self.master, Take)
        states, terms, counts, crossed = self.states, [], [], []
        if not late:
            states = [Take(state) for state in states]
        for index, piece in enumerate(self.pieces):
            found = [self.partial[index]] if late else []
            for term in piece.terms[-1:] if late else piece.terms:
                found.append(Take(term, term.shape[1:], lambda: (0,)))
            terms += found
            counts.append(len(found))
            crossed.append(piece.crossed and not late)
        shape = shaped(*self.master.shape)
        outs = self.line.call(
            functools.partial(
                moments_kernel,
                row=self.row,
                regions=regions,
                counts=counts,
                crossed=crossed,
                late=late,
            ),
            [shape, shape] + [shape] * (1 if late else 2) + [shaped(8, LANES)],
            [self.master, *states, self.line.table, *terms],
            megabytes=16,
        )
        self.kept, self.update, *self.found, self.line.table = outs
        if not late:
            self.first_new, self.second_new = self.found

    def finish(self):
        self.first_new, self.second_new = self.line.call(
            finish_kernel, [shaped(*self.master.shape)] * 2, [*self.found, *self.states]
        )


def project(normed, weights, cosine, sine):
    query = turn(dot(normed, weights[0]), cosine, sine).astype(LOW)
    keys = turn(dot(normed, weights[1]), cosine, sine).astype(LOW)
    return query, keys, dot(normed, weights[2]).astype(LOW)


def attend(query, keys, values, first_row, live_len):
    rows, reach = query.shape[0], keys.shape[0]
    row = first_row + lax.broadcasted_iota(jnp.int32, (rows, reach), 0)
    column = lax.broadcasted_iota(jnp.int32, (rows, reach), 1)
    visible = (column <= row) & (column < live_len)
    lane = lax.broadcasted_iota(jnp.int32, (1, LANES), 1)
    mixed = jnp.zeros((rows, query.shape[1]), WIDE)
    masses = jnp.zeros((rows, LANES), WIDE)
    for head in range(query.shape[1] // HEAD_DIM):
        scores = dot_wide(of_head(query, head), keys) * HEAD_DIM ** (-0.5)
        scores = jnp.where(visible, scores, mask_fill)
        top = jnp.max(scores, axis=-1, keepdims=True)
        expo = jnp.exp(scores - top)
        total = jnp.sum(expo, axis=-1, keepdims=True)
        probs = (expo * (1.0 / total)).astype(LOW)
        mixed = mixed + dot(probs, of_head(values, head))
        masses = jnp.where(lane == head, top + jnp.log(total), masses)
    live = first_row + lax.broadcasted_iota(jnp.int32, (rows, 1), 0) < live_len
    return jnp.where(live, mixed, 0.0).astype(LOW), masses


def split_rows(left_ref, right, send_ref, keep_ref, how):
    half = send_ref.shape[0]
    core = core_index()
    send_ref[...] = how(left_ref[pl.ds((1 - core) * half, half), :], right)
    keep_ref[...] = how(left_ref[pl.ds(core * half, half), :], right)


def first_kernel(
    live_ref, x_any, norm_any, cos_any, sin_any, qkv_any, out_any,
    normed_ref, q_ref, k_ref, v_ref, attn_ref, mass_ref, send_ref, keep_ref,
    x_ref, norm_ref, cos_ref, sin_ref, qkv_in, out_in, arrived,
):
    part = x_ref.shape[0]
    sources = [x_any.at[pl.ds(0, part)], norm_any, cos_any.at[pl.ds(0, part)], sin_any.at[pl.ds(0, part)]]
    targets = [x_ref, norm_ref, cos_ref, sin_ref]
    sources += [qkv_any.at[j] for j in range(3)] + [out_any]
    targets += [qkv_in.at[j] for j in range(3)] + [out_in]
    copies = [
        pltpu.make_async_copy(source, target, arrived.at[i])
        for i, (source, target) in enumerate(zip(sources, targets))
    ]
    for copy in copies:
        copy.start()
    copies[0].wait()
    copies[1].wait()
    stat, _ = normalize(x_ref[...].astype(WIDE))
    normed = (stat * norm_ref[0:1, :] + norm_ref[1:2, :]).astype(LOW)
    normed_ref[...] = normed
    copies[2].wait()
    copies[3].wait()
    weights = []
    for j in range(3):
        copies[4 + j].wait()
        weights.append(qkv_in[j].astype(LOW))
    query, keys, values = project(normed, weights, cos_ref[...], sin_ref[...])
    q_ref[...], k_ref[...], v_ref[...] = query, keys, values
    attn_ref[...], mass_ref[...] = attend(query, keys, values, 0, live_ref[0])
    copies[7].wait()
    split_rows(attn_ref, out_in[...].astype(LOW), send_ref, keep_ref, dot)


def next_kernel(
    live_ref, x_ref, norm_ref, cos_ref, sin_ref, qkv_ref, out_ref, *refs, first_row, part
):
    earlier = first_row // part
    rows = slice(first_row, first_row + part)
    k_before, v_before = refs[:earlier], refs[earlier : 2 * earlier]
    normed_ref, q_ref, k_ref, v_ref, attn_ref, mass_ref, send_ref, keep_ref = refs[
        2 * earlier : 2 * earlier + 8
    ]
    stat, _ = normalize(x_ref[rows, :].astype(WIDE))
    normed = (stat * norm_ref[0:1, :] + norm_ref[1:2, :]).astype(LOW)
    normed_ref[...] = normed
    weights = [qkv_ref[j].astype(LOW) for j in range(3)]
    out_low = out_ref[...].astype(LOW)
    for low_ref, low in zip(refs[2 * earlier + 8 :], (jnp.stack(weights), out_low)):
        low_ref[...] = low
    query, keys, values = project(normed, weights, cos_ref[rows, :], sin_ref[rows, :])
    q_ref[...], k_ref[...], v_ref[...] = query, keys, values
    keys = jnp.concatenate([ref[...] for ref in k_before] + [keys], axis=0)
    values = jnp.concatenate([ref[...] for ref in v_before] + [values], axis=0)
    attn_ref[...], mass_ref[...] = attend(query, keys, values, first_row, live_ref[0])
    split_rows(attn_ref, out_low, send_ref, keep_ref, dot)


def cast_kernel(wide_ref, low_ref):
    low_ref[...] = wide_ref[...].astype(LOW)


def middle_kernel(
    first_row, x_ref, norm_ref, mine_ref, theirs_ref, branch_ref, hidden_ref, *normed_refs
):
    half = mine_ref.shape[0]
    branch = mine_ref[...] + theirs_ref[...]
    branch_ref[...] = branch
    stat, _ = normalize(branch)
    inputs = x_ref[pl.ds(first_row + core_index() * half, half), :].astype(WIDE)
    hidden = inputs + stat * norm_ref[2:3, :] + norm_ref[3:4, :]
    hidden_ref[...] = hidden
    stat, _ = normalize(hidden)
    normed = stat * norm_ref[4:5, :] + norm_ref[5:6, :]
    for normed_ref in normed_refs:
        normed_ref[...] = normed


def mlp_kernel(own_ref, other_ref, up_w_ref, down_w_ref, normed_ref, up_ref, active_ref, send_ref, keep_ref):
    half = own_ref.shape[0]
    normed = jnp.concatenate([own_ref[...].astype(LOW), other_ref[...].astype(LOW)], axis=0)
    normed_ref[...] = normed
    step = min(256, up_w_ref.shape[1])
    total = None
    for start in range(0, up_w_ref.shape[1], step):
        block = slice(start, start + step)
        up = dot(normed, up_w_ref[:, block])
        up_ref[:, block] = up
        active = (up * gelu_mass(up)).astype(LOW)
        active_ref[:, block] = active
        product = dot(active, down_w_ref[block, :])
        total = product if total is None else total + product
    keep_ref[...] = total[:half]
    send_ref[...] = total[half:]


def again_kernel(own_ref, other_ref, up_w_ref, normed_ref, active_ref, slope_ref):
    normed = jnp.concatenate([own_ref[...].astype(LOW), other_ref[...].astype(LOW)], axis=0)
    normed_ref[...] = normed
    step = min(256, up_w_ref.shape[1])
    for start in range(0, up_w_ref.shape[1], step):
        block = slice(start, start + step)
        up = dot(normed, up_w_ref[:, block])
        mass = gelu_mass(up)
        active_ref[:, block] = (up * mass).astype(LOW)
        slope_ref[:, block] = gelu_slope(up, mass)


def back_again_kernel(own_ref, other_ref, slope_ref, down_w_ref, grad_mlp_ref, grad_up_ref):
    grad_mlp = jnp.concatenate([own_ref[...].astype(LOW), other_ref[...].astype(LOW)], axis=0)
    grad_mlp_ref[...] = grad_mlp
    step = min(256, slope_ref.shape[1])
    for start in range(0, slope_ref.shape[1], step):
        block = slice(start, start + step)
        grad_up = dot_wide(grad_mlp, down_w_ref[block, :]) * slope_ref[:, block]
        grad_up_ref[:, block] = grad_up.astype(LOW)


def loss_kernel(
    first_row, grad_ref, norm_ref, hidden_ref, mine_ref, theirs_ref, block_ref, sums_ref, *back_refs
):
    half = mine_ref.shape[0]
    stat, inverse = normalize(mine_ref[...] + theirs_ref[...])
    block_ref[...] = hidden_ref[...] + stat * norm_ref[6:7, :] + norm_ref[7:8, :]
    incoming = grad_ref[pl.ds(first_row + core_index() * half, half), :].astype(WIDE)
    back, gain, offset = norm_back(incoming, stat, inverse, norm_ref[6:7, :])
    for back_ref in back_refs:
        back_ref[...] = back
    sums_ref[0:1, :] = gain
    sums_ref[1:2, :] = offset


def mlp_back_kernel(
    own_ref, other_ref, up_ref, up_w_ref, down_w_ref, grad_mlp_ref, grad_up_ref, send_ref, keep_ref
):
    half = own_ref.shape[0]
    grad_mlp = jnp.concatenate([own_ref[...].astype(LOW), other_ref[...].astype(LOW)], axis=0)
    grad_mlp_ref[...] = grad_mlp
    step = min(256, up_w_ref.shape[1])
    total = None
    for start in range(0, up_w_ref.shape[1], step):
        block = slice(start, start + step)
        up = up_ref[:, block]
        slope = gelu_slope(up, gelu_mass(up))
        grad_up = (dot_wide(grad_mlp, down_w_ref[block, :]) * slope).astype(LOW)
        grad_up_ref[:, block] = grad_up
        product = dot_wide(grad_up, up_w_ref[:, block])
        total = product if total is None else total + product
    keep_ref[...] = total[:half]
    send_ref[...] = total[half:]


def norms_back_kernel(
    first_row, grad_ref, norm_ref, hidden_ref, branch_ref, mine_ref, theirs_ref,
    grad_hidden_ref, back_ref, sums_ref,
):
    half = mine_ref.shape[0]
    stat, inverse = normalize(hidden_ref[...])
    back, gain, offset = norm_back(
        mine_ref[...] + theirs_ref[...], stat, inverse, norm_ref[4:5, :]
    )
    incoming = grad_ref[pl.ds(first_row + core_index() * half, half), :].astype(WIDE)
    grad_hidden = incoming + back
    grad_hidden_ref[...] = grad_hidden
    sums_ref[2:3, :] = gain
    sums_ref[3:4, :] = offset
    stat, inverse = normalize(branch_ref[...])
    back, gain, offset = norm_back(grad_hidden, stat, inverse, norm_ref[2:3, :])
    back_ref[...] = back
    sums_ref[0:1, :] = gain
    sums_ref[1:2, :] = offset


def attention_back_kernel(live_ref, out_low_ref, cos_ref, sin_ref, *refs, chunks):
    groups = [refs[i * chunks : (i + 1) * chunks] for i in range(6)]
    own, other, query_refs, key_refs, value_refs, mass_refs = groups
    grad_branch_ref, rows_ref = refs[6 * chunks : 6 * chunks + 2]
    keys_sum, values_sum = refs[6 * chunks + 2 :]
    half = own[0].shape[0]
    part = 2 * half
    core = core_index()
    live_len = live_ref[0]
    local = rows_ref.shape[1] // 3
    heads = local // HEAD_DIM
    for c in range(chunks):
        grad_branch_ref[pl.ds(c * part + core * half, half), :] = own[c][...].astype(LOW)
        grad_branch_ref[pl.ds(c * part + (1 - core) * half, half), :] = other[c][...].astype(LOW)
    keys_all = jnp.concatenate([ref[...] for ref in key_refs], axis=0)
    values_all = jnp.concatenate([ref[...] for ref in value_refs], axis=0)
    for c in range(chunks):
        reach = (c + 1) * part
        first_row = c * part
        row = first_row + lax.broadcasted_iota(jnp.int32, (part, reach), 0)
        column = lax.broadcasted_iota(jnp.int32, (part, reach), 1)
        visible = (column <= row) & (column < live_len)
        live = first_row + lax.broadcasted_iota(jnp.int32, (part, 1), 0) < live_len
        grad_attn = dot_wide(grad_branch_ref[first_row : first_row + part, :], out_low_ref[...])
        grad_mixed = jnp.where(live, grad_attn, 0.0).astype(LOW)
        query, masses = query_refs[c][...], mass_refs[c][...]
        keys, values = keys_all[:reach], values_all[:reach]
        grad_query = jnp.zeros((part, local), WIDE)
        grad_keys = jnp.zeros((reach, local), WIDE)
        grad_values = jnp.zeros((reach, local), WIDE)
        for head in range(heads):
            query_h, grad_h = of_head(query, head), of_head(grad_mixed, head)
            scores = dot_wide(query_h, keys) * HEAD_DIM ** (-0.5)
            scores = jnp.where(visible, scores, mask_fill)
            probs = jnp.exp(scores - masses[:, head : head + 1])
            grad_values = grad_values + dot_rows(probs.astype(LOW), grad_h)
            grad_probs = dot_wide(grad_h, values)
            inner = jnp.sum(grad_probs * probs, axis=-1, keepdims=True)
            grad_scores = (probs * (grad_probs - inner)).astype(LOW)
            grad_query = grad_query + dot(grad_scores, of_head(keys, head))
            grad_keys = grad_keys + dot_rows(grad_scores, query_h)
        cosine = cos_ref[first_row : first_row + part, :]
        sine = sin_ref[first_row : first_row + part, :]
        grad_query = turn(grad_query * HEAD_DIM ** (-0.5), cosine, -sine)
        rows_ref[first_row : first_row + part, 0:local] = grad_query.astype(LOW)
        if c == 0:
            keys_sum[0:reach, :] = grad_keys
            values_sum[0:reach, :] = grad_values
        else:
            keys_sum[0:first_row, :] += grad_keys[:first_row]
            keys_sum[first_row:reach, :] = grad_keys[first_row:]
            values_sum[0:first_row, :] += grad_values[:first_row]
            values_sum[first_row:reach, :] = grad_values[first_row:]
    grad_keys = turn(keys_sum[...] * HEAD_DIM ** (-0.5), cos_ref[...], -sin_ref[...])
    rows_ref[:, local : 2 * local] = grad_keys.astype(LOW)
    rows_ref[:, 2 * local : 3 * local] = values_sum[...].astype(LOW)


def picked_columns(refs, chunks, own):
    blocks = []
    for chunk in chunks:
        start = pl.multiple_of(chunk * own, own)
        pieces = [ref[:, pl.ds(start, own)].astype(LOW) for ref in refs]
        blocks.append(pieces[0] if len(pieces) == 1 else jnp.concatenate(pieces, axis=0))
    return blocks[0] if len(blocks) == 1 else jnp.concatenate(blocks, axis=1)


def whole_rows(refs, window):
    pieces = [ref[:, window[0] : window[1]].astype(LOW) for ref in refs]
    return pieces[0] if len(pieces) == 1 else jnp.concatenate(pieces, axis=0)


def owned_columns_kernel(*refs, pairs, jobs, own):
    (lefts, rights), outs = pairs, refs[sum(pairs) :]
    left, right = refs[:lefts], refs[lefts : lefts + rights]
    for (order, window, blocks), out_ref in zip(jobs, outs):
        chunks = order(lax.axis_index("dp"))
        rows = whole_rows(left[:blocks], window)
        product = dot_rows(rows, picked_columns(right[:blocks], chunks, own))
        for place in range(len(chunks)):
            out_ref[place] = product[:, place * own : (place + 1) * own]


def owned_rows_kernel(*refs, pairs, jobs, own):
    (lefts, rights), outs = pairs, refs[sum(pairs) :]
    left, right = refs[:lefts], refs[lefts : lefts + rights]
    for (order, window, blocks), out_ref in zip(jobs, outs):
        chunks = order(lax.axis_index("dp"))
        product = dot_rows(
            picked_columns(left[:blocks], chunks, own), whole_rows(right[:blocks], window)
        )
        for place in range(len(chunks)):
            out_ref[place] = product[place * own : (place + 1) * own, :]


def owned_parts_kernel(*refs, pairs, jobs, own):
    (lefts, rights), outs = pairs, refs[sum(pairs) :]
    left, right = refs[:lefts], refs[lefts : lefts + rights]
    for (order, window, blocks), out_ref in zip(jobs, outs):
        chunks = order(lax.axis_index("dp"))
        local = out_ref.shape[3]
        columns = (window[0] * local, window[1] * local)
        product = dot_rows(picked_columns(left, chunks, own), whole_rows(right, columns))
        for place in range(len(chunks)):
            for j in range(window[1] - window[0]):
                out_ref[place, j] = product[
                    place * own : (place + 1) * own, j * local : (j + 1) * local
                ]


def rounded_kernel(*refs):
    refs[-1][...] = whole_rows(refs[:-1], (0, refs[0].shape[1]))


def narrow_products(line, kernel, left, right, jobs, outs, own):
    joined = []
    for arrays in (left, right):
        rows = sum(array.shape[0] for array in arrays)
        low = shaped(rows, arrays[0].shape[1], kind=LOW)
        joined.append(line.call(rounded_kernel, [low], arrays)[0])
    results = []
    for (order, window, _), out in zip(jobs, outs):
        chunks = order(lax.axis_index("dp"))
        pick = lambda array: jnp.concatenate(
            [lax.dynamic_slice_in_dim(array, chunk * own, own, 1) for chunk in chunks], axis=1
        )
        if kernel is owned_columns_kernel:
            product = dot_rows(joined[0][:, window[0] : window[1]], pick(joined[1]))
            product = product.reshape(-1, len(chunks), own).transpose(1, 0, 2)
        elif kernel is owned_rows_kernel:
            product = dot_rows(pick(joined[0]), joined[1][:, window[0] : window[1]])
            product = product.reshape(out.shape)
        else:
            local = out.shape[3]
            columns = joined[1][:, window[0] * local : window[1] * local]
            product = dot_rows(pick(joined[0]), columns)
            product = product.reshape(len(chunks), own, -1, local).transpose(0, 2, 1, 3)
        results.append(product)
    return results


def owner_products(line, kernel, left, right, pieces, own, send, blocks=None):
    jobs, outs = [], []
    for piece in pieces:
        half = piece.route.held // 2
        part = slice(half, None) if send else slice(half)
        order = lambda rank, route=piece.route, part=part: route.order(rank)[part]
        jobs.append((order, piece.window, None if piece.joined else blocks))
        size = piece.window[1] - piece.window[0]
        if kernel is owned_columns_kernel:
            outs.append(shaped(half, size, own))
        elif kernel is owned_rows_kernel:
            outs.append(shaped(half, own, size))
        else:
            outs.append(shaped(half, size, own, right[0].shape[1] // 3))
    if own % LANES:
        return narrow_products(line, kernel, left, right, jobs, outs, own)
    return line.call(
        functools.partial(kernel, pairs=(len(left), len(right)), jobs=jobs, own=own),
        outs,
        [*left, *right],
        megabytes=20,
    )


def input_back_kernel(rows_ref, qkv_low_ref, send_ref, keep_ref, *, chunks):
    half = send_ref.shape[0] // chunks
    local = qkv_low_ref.shape[2]
    core = core_index()
    for c in range(chunks):
        for target, which in ((send_ref, 1 - core), (keep_ref, core)):
            rows = rows_ref[pl.ds(c * 2 * half + which * half, half), :]
            total = None
            for j in range(3):
                product = dot_wide(rows[:, j * local : (j + 1) * local], qkv_low_ref[j])
                total = product if total is None else total + product
            target[c * half : (c + 1) * half, :] = total


def input_norm_kernel(x_ref, norm_ref, mine_ref, theirs_ref, *refs, chunks):
    grad_hidden = refs[:chunks]
    rows_ref, sums_ref = refs[chunks:]
    half = mine_ref.shape[0] // chunks
    core = core_index()
    gains = offsets = None
    for c in range(chunks):
        rows = slice(c * half, (c + 1) * half)
        inputs = x_ref[pl.ds(c * 2 * half + core * half, half), :].astype(WIDE)
        stat, inverse = normalize(inputs)
        back, gain, offset = norm_back(
            mine_ref[rows, :] + theirs_ref[rows, :], stat, inverse, norm_ref[0:1, :]
        )
        rows_ref[rows, :] = grad_hidden[c][...] + back
        gains = gain if gains is None else gains + gain
        offsets = offset if offsets is None else offsets + offset
    sums_ref[0:1, :] = gains
    sums_ref[1:2, :] = offsets


def place_kernel(mine_ref, theirs_ref, out_ref, *, chunks):
    half = mine_ref.shape[0] // chunks
    core = core_index()
    for c in range(chunks):
        rows = slice(c * half, (c + 1) * half)
        out_ref[pl.ds((2 * c + core) * half, half), :] = mine_ref[rows, :].astype(LOW)
        out_ref[pl.ds((2 * c + 1 - core) * half, half), :] = theirs_ref[rows, :].astype(LOW)


def rows_kernel(source_ref, target_ref):
    target_ref[...] = source_ref[...]


def norm_sums_kernel(*refs, chunks):
    input_ref, norms, losses, out_ref = refs[0], refs[1 : 1 + chunks], refs[1 + chunks : -1], refs[-1]
    out_ref[0:2, :] = input_ref[...]
    out_ref[2:6, :] = sum(ref[...] for ref in norms[1:]) + norms[0][...]
    out_ref[6:8, :] = sum(ref[...] for ref in losses[1:]) + losses[0][...]


def stage_kernel(*refs, counts, crossed):
    terms, outs = refs[3 : 3 + sum(counts)], refs[3 + sum(counts) :]
    for source, target in zip(refs[:3], outs[:3]):
        target[...] = source[...]
    at = 0
    for count, out_ref, cross in zip(counts, outs[3:], crossed):
        out_ref[...] = gathered([term[...] for term in terms[at : at + count]], cross)
        at += count


def finish_kernel(gradient_ref, first_ref, second_ref, first_new_ref, second_new_ref):
    first_new, second_new, _ = moment_step(gradient_ref[...], first_ref[...], second_ref[...])
    first_new_ref[...] = first_new
    second_new_ref[...] = second_new


def moment_step(gradient, first_state, second_state):
    first_new = first_decay * first_state + (1.0 - first_decay) * gradient
    second_new = second_decay * second_state + (1.0 - second_decay) * gradient * gradient
    direction = (
        first_new
        / (1.0 - first_decay**STEP)
        / (jnp.sqrt(second_new / (1.0 - second_decay**STEP)) + adam_epsilon)
    )
    return (first_new, second_new, direction)


def total_of(values):
    rows = values.reshape(-1, values.shape[-1])
    return jnp.sum(jnp.sum(rows, axis=0, keepdims=True), axis=1, keepdims=True)


def moments_kernel(
    master_ref, first_ref, second_ref, squares_ref, *refs, row, regions, counts, crossed, late
):
    table_ref = refs[-1]
    kept_ref, update_ref, *moment_refs = refs[sum(counts) : -1]
    at = 0
    sizes = []
    for region, count, cross in zip(regions, counts, crossed):
        gradient = gathered([term[...] for term in refs[at : at + count]], cross)
        at += count
        first_new, second_new, direction = moment_step(
            gradient, first_ref[region], second_ref[region]
        )
        for target, found in zip(moment_refs, [gradient] if late else [first_new, second_new]):
            target[region] = found
        master = master_ref[region]
        kept_ref[region] = master
        update = direction + decay_rate * master
        update_ref[region] = update
        sizes.append((total_of(master * master), total_of(update * update)))
    table_ref[...] = squares_ref[...]
    for place, size in ((row, 0), (row + 4, 1)):
        amount = sizes[0][size]
        for other in sizes[1:]:
            amount = amount + other[size]
        table_ref[place : place + 1, :] = jnp.broadcast_to(amount, (1, LANES))


def join_kernel(*refs):
    terms, norms_ref, out_ref = refs[:-2], refs[-2], refs[-1]
    terms = [ref[...] for ref in terms]
    while len(terms) > 1:
        terms = [terms[i] + terms[i + 1] for i in range(0, len(terms), 2)]
    out_ref[:, 0:LANES] = terms[0]
    out_ref[:, LANES:] = norms_ref[...]


def masters_kernel(norm_ref, first_ref, second_ref, *refs, terms, own):
    sums, refs = refs[:terms], refs[terms:]
    masters, updates, outs = refs[:4], refs[4:8], refs[8:12]
    norms_ref, norm_new_ref, first_new_ref, second_new_ref = refs[12:]
    total = sums[0][:, 0:LANES]
    for ref in sums[1:]:
        total = total + ref[:, 0:LANES]
    sizes = jnp.sqrt(total[0:4, :])
    steps = jnp.sqrt(total[4:8, :] + trust_epsilon)
    lane = lax.broadcasted_iota(jnp.int32, (1, 4), 1)
    for place, found in ((0, sizes), (1, steps)):
        row = jnp.zeros((1, 4), WIDE)
        for index in range(4):
            row = jnp.where(lane == index, found[index : index + 1, 0:1], row)
        norms_ref[place : place + 1, :] = row
    ratio = learn_rate * (sizes / steps)
    for index in range(4):
        scale = ratio[index : index + 1, 0:1]
        if len(masters[index].shape) == 3:
            scale = scale.reshape(1, 1, 1)
        outs[index][...] = masters[index][...] - scale * updates[index][...]
    if own % LANES:
        gradient = sums[0][:, LANES:]
        for ref in sums[1:]:
            gradient = gradient + ref[:, LANES:]
        norm_new_ref[...] = gradient
        return
    start = pl.multiple_of(lax.axis_index("dp") * own, own)
    gradient = sums[0][:, pl.ds(LANES + start, own)]
    for ref in sums[1:]:
        gradient = gradient + ref[:, pl.ds(LANES + start, own)]
    first_new, second_new, direction = moment_step(gradient, first_ref[...], second_ref[...])
    first_new_ref[...] = first_new
    second_new_ref[...] = second_new
    norm_new_ref[...] = norm_ref[:, pl.ds(start, own)] - learn_rate * direction


def shards(
    block_input,
    lengths,
    norm_params,
    qkv_weight,
    out_weight,
    up_weight,
    down_weight,
    qkv_first,
    qkv_second,
    out_first,
    out_second,
    up_first,
    up_second,
    down_first,
    down_second,
    norm_first,
    norm_second,
    out_grad,
):
    row_count, width = block_input.shape
    local = qkv_weight.shape[2]
    hidden_units = up_weight.shape[1]
    group_count = lax.axis_size("dp")
    own = width // group_count
    own_start = lax.axis_index("dp") * own
    part = row_count // CHUNKS
    half = part // 2
    chunks = range(CHUNKS)
    bits = list(range(log2_of(group_count)))

    line = Line()
    qkv_parts = jnp.transpose(qkv_weight, (1, 0, 2))
    cosine, sine = rotary_tables(row_count)
    live = Raw(lengths, SMEM)
    joined = group_count == 8 and own % LANES == 0

    def relay_of(theirs):
        copied = line.call(rows_kernel, [cut(half, width, CUT_RELAY)], [theirs])[0]
        return theirs, near(copied)

    weight_shapes = [shaped(3, width, local, kind=LOW), shaped(local, width, kind=LOW)]
    chunk_shapes = [
        shaped(part, width, kind=LOW),
        shaped(part, local, kind=LOW),
        shaped(part, local, kind=LOW),
        shaped(part, local, kind=LOW),
        shaped(part, local, kind=LOW),
        shaped(part, LANES),
        cut(half, width, CUT_ATTENTION),
        shaped(half, width),
    ]
    low_weights, parts, branch_terms = [], [], []

    def attention(c):
        if c == 0:
            outs = line.call(
                first_kernel,
                chunk_shapes,
                [live]
                + [
                    Raw(a, HBM)
                    for a in (block_input, norm_params, cosine, sine, qkv_parts, out_weight)
                ],
                scratch=[
                    pltpu.VMEM((part, width), LOW),
                    pltpu.VMEM(norm_params.shape, WIDE),
                    pltpu.VMEM((part, LANES), WIDE),
                    pltpu.VMEM((part, LANES), WIDE),
                    pltpu.VMEM((3, width, local), WIDE),
                    pltpu.VMEM((local, width), WIDE),
                    pltpu.SemaphoreType.DMA((8,)),
                ],
                megabytes=60,
                first=True,
            )
            keep = Take(outs[7])
        else:
            before = [p[2] for p in parts] + [p[3] for p in parts]
            outs = line.call(
                functools.partial(next_kernel, first_row=c * part, part=part),
                chunk_shapes + weight_shapes * (c == 1),
                [live, block_input, norm_params, cosine, sine]
                + (low_weights or [qkv_parts, out_weight])
                + before,
            )
            keep = outs[7]
            low_weights.extend(outs[8:])
        parts.append(outs)
        branch_terms.append((keep, near(outs[6])))

    def sum_branch(c):
        branch_terms[c] = sum_rows(line, *branch_terms[c])

    def cast(weight):
        return line.call(cast_kernel, [shaped(*weight.shape, kind=LOW)], [Take(weight)])[0]

    branch, hidden, normed_mid, up, active, mlp_terms = [], [], [], [], [], []
    normed_other, ships, normed_theirs, active_theirs, slope_theirs = [], [], [], [], []

    def middle(c):
        outs = line.call(
            functools.partial(middle_kernel, c * part),
            [shaped(half, width), shaped(half, width), cut(half, width, CUT_MIDDLE)]
            + [shaped(half, width)] * joined,
            [block_input, norm_params, *branch_terms[c]],
        )
        branch.append(outs[0])
        hidden.append(outs[1])
        normed_other.append((outs[2], near(outs[2])))
        ships.append(swap(outs[3], "dp", 2) if joined else None)

    def relay(c):
        if joined:
            ships[c] = relay_of(ships[c])

    def mlp(c):
        outs = line.call(
            mlp_kernel,
            [
                shaped(part, width, kind=LOW),
                shaped(part, hidden_units),
                shaped(part, hidden_units, kind=LOW),
                cut(half, width, CUT_MLP),
                shaped(half, width),
            ],
            [*normed_other[c], up_low, down_low],
        )
        normed_mid.append(outs[0])
        up.append(outs[1])
        active.append(outs[2])
        mlp_terms.append((outs[4], near(outs[3])))

    def sum_mlp(c):
        mlp_terms[c] = sum_rows(line, *mlp_terms[c])

    def again(c):
        if joined:
            outs = line.call(
                again_kernel,
                [
                    shaped(part, width, kind=LOW),
                    shaped(part, hidden_units, kind=LOW),
                    shaped(part, hidden_units),
                ],
                [*ships[c], up_low],
            )
            normed_theirs.append(outs[0])
            active_theirs.append(outs[1])
            slope_theirs.append(outs[2])

    line.own, line.table = own, jnp.zeros((8, LANES), WIDE)
    route_a, route_b, route_j = routes(group_count)
    columns = lambda: (slice(None), pl.ds(pl.multiple_of(lax.axis_index("dp") * own, own), own))
    rows = lambda: (pl.ds(pl.multiple_of(lax.axis_index("dp") * own, own), own),)
    part_rows = lambda: (slice(None), *rows())
    mine = lambda array, axis: lax.dynamic_slice_in_dim(array, own_start, own, axis)
    block_rows, loss_sums, grad_final, grad_up_rows, mid_terms = [], [], [], [], []
    grad_mlp, grad_mlp_theirs, grad_up_theirs, ships_back = [], [], [], []
    grad_hidden, norms_sums, own_back, other_back = [], [], [], []
    flip = lambda array: jnp.transpose(array, (1, 0, 2))
    qkv = Weight(
        line,
        0,
        3,
        owned_parts_kernel,
        lambda: ([p[0] for p in parts], [grad_rows]),
        lambda: ([p[0] for p in parts], [grad_rows]),
        Take(qkv_parts, (3, own, local), part_rows),
        [flip(qkv_first), flip(qkv_second)],
    )
    out = Weight(
        line,
        1,
        local,
        owned_columns_kernel,
        lambda: ([p[4] for p in parts], [grad_branch]),
        lambda: ([p[4] for p in parts], [grad_branch]),
        Take(mine(out_weight, 1)) if own % LANES else Take(out_weight, (local, own), columns),
        [out_first, out_second],
    )
    up_matrix = Weight(
        line,
        2,
        hidden_units,
        owned_rows_kernel,
        lambda: (normed_mid + normed_theirs, grad_up_rows + grad_up_theirs),
        lambda: (normed_mid, grad_up_rows),
        Take(up_weight, (own, hidden_units), rows),
        [up_first, up_second],
    )
    down = Weight(
        line,
        3,
        hidden_units,
        owned_columns_kernel,
        lambda: (active + active_theirs, grad_mlp + grad_mlp_theirs),
        lambda: (active, [block for pair in grad_final for rows in pair for block in rows]),
        Take(mine(down_weight, 1))
        if own % LANES
        else Take(down_weight, (hidden_units, own), columns),
        [down_first, down_second],
    )
    d0 = down.piece(0, 8, 8, route_j)
    u0 = up_matrix.piece(0, 8, 8, route_j)
    q0 = qkv.piece(0, 2, 3, route_b)
    q1 = qkv.piece(2, 3, 3, route_b)
    o0 = out.piece(0, 1, 1, route_b)


    def loss(c):
        outs = line.call(
            functools.partial(loss_kernel, c * part),
            [shaped(half, width), shaped(2, width), cut(half, width, CUT_LOSS)]
            + [shaped(half, width)] * joined,
            [out_grad, norm_params, hidden[c], *mlp_terms[c]],
        )
        block_rows.append(outs[0])
        loss_sums.append(outs[1])
        grad_final.append((outs[2], near(outs[2])))
        ships_back.append(swap(outs[3], "dp", 2) if joined else None)

    def back_relay(c):
        if joined:
            ships_back[c] = relay_of(ships_back[c])

    def mlp_back(c):
        outs = line.call(
            mlp_back_kernel,
            [
                shaped(part, width, kind=LOW),
                shaped(part, hidden_units, kind=LOW),
                cut(half, width, CUT_MLP if c < CHUNKS - 1 else CUT_MID),
                shaped(half, width),
            ],
            [*grad_final[c], up[c], up_low, down_low],
        )
        grad_mlp.append(outs[0])
        grad_up_rows.append(outs[1])
        mid_terms.append((outs[3], near(outs[2])))

    def back_again(c):
        if joined:
            outs = line.call(
                back_again_kernel,
                [shaped(part, width, kind=LOW), shaped(part, hidden_units, kind=LOW)],
                [*ships_back[c], slope_theirs[c], down_low],
            )
            grad_mlp_theirs.append(outs[0])
            grad_up_theirs.append(outs[1])

    def sum_mid(c):
        mid_terms[c] = sum_rows(line, *mid_terms[c])

    def norms(c):
        outs = line.call(
            functools.partial(norms_back_kernel, c * part),
            [shaped(half, width), cut(half, width, CUT_NORMS), shaped(4, width)],
            [out_grad, norm_params, hidden[c], branch[c], *mid_terms[c]],
        )
        grad_hidden.append(outs[0])
        norms_sums.append(outs[2])
        own_back.append(outs[1])
        other_back.append(near(outs[1]))

    def attention_back():
        return line.call(
            functools.partial(attention_back_kernel, chunks=CHUNKS),
            [shaped(row_count, width, kind=LOW), shaped(row_count, 3 * local, kind=LOW)],
            [live, low_weights[1], cosine, sine, *own_back, *other_back]
            + [p[which] for which in (1, 2, 3, 5) for p in parts],
            scratch=[pltpu.VMEM((row_count, local), WIDE), pltpu.VMEM((row_count, local), WIDE)],
        )

    def input_back():
        return line.call(
            functools.partial(input_back_kernel, chunks=CHUNKS),
            [cut(row_count // 2, width, CUT_BACK), shaped(row_count // 2, width)],
            [grad_rows, low_weights[0]],
        )

    def input_norm():
        return line.call(
            functools.partial(input_norm_kernel, chunks=CHUNKS),
            [cut(row_count // 2, width, CUT_INPUT), shaped(2, width)],
            [block_input, norm_params, *in_terms, *grad_hidden],
        )

    def send_output():
        return line.call(
            rows_kernel, [cut(row_count // 2, width, CUT_OUTPUT)], [block_rows]
        )[0]

    def place(blocks, others):
        return line.call(
            functools.partial(place_kernel, chunks=CHUNKS),
            [shaped(row_count, width, kind=LOW)],
            [blocks, others],
        )[0]

    def norm_sums():
        return line.call(
            functools.partial(norm_sums_kernel, chunks=CHUNKS),
            [shaped(8, width)],
            [input_sums, *norms_sums, *loss_sums],
        )[0]

    def sum_norms():
        return line.call(
            sum_kernel, [shaped(8, width)], [grad_norms, norms_other]
        )[0]

    attention(0)
    sum_branch(0)
    attention(1)
    sum_branch(1)
    up_low = cast(up_weight)
    down_low = cast(down_weight)
    middle(0)
    mlp(0)
    sum_mlp(0)
    middle(1)
    mlp(1)
    relay(0)
    sum_mlp(1)
    loss(0)
    mlp_back(0)
    again(0)
    relay(1)
    sum_mid(0)
    loss(1)
    back_relay(0)
    again(1)
    mlp_back(1)
    norms(0)
    sum_mid(1)
    back_again(0)
    back_relay(1)
    back_again(1)
    d0.start()
    down.hold()
    u0.start()
    norms(1)
    grad_branch, grad_rows = attention_back()
    send, keep = input_back()
    crossing = near(send)
    q0.start()
    in_terms = sum_rows(line, keep, crossing)
    qkv.hold()
    sent_rows = send_output()
    block_other = near(sent_rows)
    o0.start()
    d0.advance()
    q1.start()
    block_output = place(sent_rows, block_other)
    up_matrix.hold()
    q0.advance()
    u0.advance()
    d0.advance()
    q1.advance()
    out.hold()
    input_rows, input_sums = input_norm()
    input_other = near(input_rows)
    q0.advance()
    o0.advance()
    input_grad = place(input_rows, input_other)
    u0.advance()
    o0.advance()
    down.moments()
    q1.advance()
    q0.advance()
    o0.advance()
    q1.advance()
    up_matrix.moments()
    out.moments()
    grad_norms = norm_sums()
    norms_other = swap(grad_norms, "tensor", 1)
    grad_norms = sum_norms()
    qkv.stage()
    qkv.moments()

    tensor_bits = log2_of(lax.axis_size("tensor"))
    found = line.table
    for start in range(0, tensor_bits, 2):
        terms = sum_terms(found, "tensor", start, min(2, tensor_bits - start))
        if start == 0:
            qkv.finish()
        if start + 2 >= tensor_bits:
            found = line.call(join_kernel, [shaped(8, LANES + width)], [*terms, grad_norms])[0]
        else:
            found = line.call(pairs_kernel, [shaped(8, LANES)], terms)[0]
    for start in range(0, len(bits), 2):
        terms = sum_terms(found, "dp", start, min(2, len(bits) - start))
        if start + 2 < len(bits) or len(terms) > 2:
            found = line.call(pairs_kernel, [shaped(8, LANES + width)], terms)[0]
            terms = [found]
    weights = (qkv, out, up_matrix, down)
    outs = line.call(
        functools.partial(masters_kernel, terms=len(terms), own=own),
        [shaped(*weight.kept.shape) for weight in weights]
        + [shaped(2, 4), shaped(8, width if own % LANES else own), shaped(8, own), shaped(8, own)],
        [
            norm_params,
            norm_first,
            norm_second,
            *terms,
            *[weight.kept for weight in weights],
            *[weight.update for weight in weights],
        ],
    )
    matrix_norms, norm_new, norm_first_new, norm_second_new = outs[4:]
    if own % LANES:
        norm_first_new, norm_second_new, direction = moment_step(
            mine(norm_new, 1), norm_first, norm_second
        )
        norm_new = mine(norm_params, 1) - learn_rate * direction
    return (
        block_output,
        input_grad,
        flip(outs[0]),
        flip(qkv.first_new),
        flip(qkv.second_new),
        outs[1],
        out.first_new,
        out.second_new,
        outs[2],
        up_matrix.first_new,
        up_matrix.second_new,
        outs[3],
        down.first_new,
        down.second_new,
        norm_new,
        norm_first_new,
        norm_second_new,
        matrix_norms,
    )


def solution(mesh):
    in_specs = (
        P("dp", None),
        P("dp"),
        P(),
        P(None, None, "tensor"),
        P("tensor", None),
        P(None, "tensor"),
        P("tensor", None),
        P("dp", None, "tensor"),
        P("dp", None, "tensor"),
        P("tensor", "dp"),
        P("tensor", "dp"),
        P("dp", "tensor"),
        P("dp", "tensor"),
        P("tensor", "dp"),
        P("tensor", "dp"),
        P(None, "dp"),
        P(None, "dp"),
        P("dp", None),
    )
    out_specs = (
        P("dp", None),
        P("dp", None),
        P("dp", None, "tensor"),
        P("dp", None, "tensor"),
        P("dp", None, "tensor"),
        P("tensor", "dp"),
        P("tensor", "dp"),
        P("tensor", "dp"),
        P("dp", "tensor"),
        P("dp", "tensor"),
        P("dp", "tensor"),
        P("tensor", "dp"),
        P("tensor", "dp"),
        P("tensor", "dp"),
        P(None, "dp"),
        P(None, "dp"),
        P(None, "dp"),
        P(),
    )
    return jax.shard_map(shards, mesh=mesh, in_specs=in_specs, out_specs=out_specs, check_vma=False)
```

```python
import functools

import jax
import jax.numpy as jnp
import numpy as np
from jax import lax
from jax.experimental import pallas as pl
from jax.experimental.pallas import tpu as pltpu
from jax.sharding import PartitionSpec as P

HEAD_DIM = 64
STEP = 10
CHUNKS = 2
LANES = 128

norm_epsilon = 1e-05
rotary_base = 10000.0
mask_fill = -1000000000.0
first_decay = 0.9
second_decay = 0.999
adam_epsilon = 1e-06
trust_epsilon = 1e-06
decay_rate = 0.01
learn_rate = 0.25

CUT_ATTENTION, CUT_MIDDLE, CUT_MLP, CUT_LOSS = 4, 4, 4, 4
CUT_RELAY = 2
CUT_MID, CUT_NORMS, CUT_BACK, CUT_INPUT, CUT_OUTPUT = 2, 2, 4, 2, 4

LOW = jnp.bfloat16
WIDE = jnp.float32
VMEM = pl.BlockSpec(memory_space=pltpu.VMEM)
SMEM = pl.BlockSpec(memory_space=pltpu.SMEM)
HBM = pl.BlockSpec(memory_space=pltpu.HBM)


def log2_of(count):
    bits = 0
    while (1 << bits) < count:
        bits += 1
    return bits


def swap(values, axis, distance):
    count = lax.axis_size(axis)
    return lax.ppermute(values, axis, [(i, i ^ distance) for i in range(count)])


class Route:
    def __init__(self, order, steps, held, joined=False):
        self.order, self.steps, self.held, self.joined = order, steps, held, joined


HALF, CROSS, BACK = range(3)


def apart(count, distance, among=None):
    return [(i, i ^ distance) for i in (range(count) if among is None else among)]


def outside(rank):
    place = lax.div(rank, 2)
    return (place == 0) | (place == 3)


def line_chunks(rank):
    place = lax.div(rank, 2)
    beside, side = lax.bitwise_xor(place, 1), lax.div(place, 2)
    near, far = (place, beside), (2 - side, 3 - 3 * side)
    end = outside(rank)
    keep = [jnp.where(end, a, b) for a, b in zip(near, far)]
    send = [jnp.where(end, a, b) for a, b in zip(far, (beside, place))]
    return keep, send


def routes(count):
    if count == 8:

        def across_first(rank):
            keep, send = line_chunks(rank)
            row = lax.rem(rank, 2)
            return [place * 2 + y for y in (row, 1 - row) for place in keep + send]

        def along_first(rank):
            keep, send = line_chunks(rank)
            row = lax.rem(rank, 2)
            return [place * 2 + y for part in (keep, send) for y in (row, 1 - row) for place in part]

        def joined(rank):
            keep, _ = line_chunks(rank)
            row = lax.rem(rank, 2)
            return [place * 2 + y for y in (row, 1 - row) for place in keep]

        across = (HALF, apart(8, 1))
        along, back = (HALF, apart(8, 2)), (BACK, apart(8, 2))
        cross = (CROSS, apart(8, 6, range(2, 6)))
        return (
            Route(across_first, [across, along, cross, back], 8),
            Route(along_first, [along, across, cross, back], 8),
            Route(joined, [across, cross, back], 4, True),
        )
    order = [0]
    bits = range(log2_of(count))
    for bit in reversed(bits):
        order = order + [distance ^ (1 << bit) for distance in order]
    found = Route(
        lambda rank: [lax.bitwise_xor(rank, distance) for distance in order],
        [(HALF, apart(count, 1 << bit)) for bit in bits],
        count,
    )
    return found, found, found


def normalize(values):
    center = values - jnp.mean(values, axis=-1, keepdims=True)
    inverse = lax.rsqrt(jnp.mean(center * center, axis=-1, keepdims=True) + norm_epsilon)
    return center * inverse, inverse


def norm_back(incoming, normed, inverse, gain):
    scaled = incoming * gain
    inner = (
        scaled
        - jnp.mean(scaled, axis=-1, keepdims=True)
        - normed * jnp.mean(scaled * normed, axis=-1, keepdims=True)
    )
    gain_grad = jnp.sum(incoming * normed, axis=0, keepdims=True)
    return inner * inverse, gain_grad, jnp.sum(incoming, axis=0, keepdims=True)


def rotary_tables(length):
    half = HEAD_DIM // 2
    lane = np.arange(LANES)
    frequency = (rotary_base ** (-((lane % half).astype(np.float32) * 2.0 / HEAD_DIM))).astype(np.float32)
    angles = np.arange(length, dtype=np.float32)[:, None] * frequency[None, :]
    sign = np.where(lane % HEAD_DIM < half, -1.0, 1.0)
    cosine = np.cos(angles.astype(np.float64)).astype(np.float32)
    sine = (np.sin(angles.astype(np.float64)) * sign[None, :]).astype(np.float32)
    return jnp.asarray(cosine), jnp.asarray(sine)


def turn(values, cosine, sine):
    half = HEAD_DIM // 2
    lane = lax.broadcasted_iota(jnp.int32, (1, LANES), 1)
    first = lax.rem(lane, HEAD_DIM) < half
    tiles = []
    for start in range(0, values.shape[1], LANES):
        tile = values[:, start : start + LANES]
        other = jnp.where(
            first, pltpu.roll(tile, LANES - half, 1), pltpu.roll(tile, half, 1)
        )
        tiles.append(tile * cosine + other * sine)
    return tiles[0] if len(tiles) == 1 else jnp.concatenate(tiles, axis=1)


def gelu_mass(up):
    return 0.5 * (1.0 + lax.erf(up * (0.5**0.5)))


def gelu_slope(up, mass):
    return mass + up * jnp.exp(-0.5 * up * up) * float((2.0 * np.pi) ** -0.5)


def dot(left, right):
    return jnp.dot(left, right, preferred_element_type=WIDE)


def dot_rows(left, right):
    return lax.dot_general(left, right, (((0,), (0,)), ((), ())), preferred_element_type=WIDE)


def dot_wide(left, right):
    return lax.dot_general(left, right, (((1,), (1,)), ((), ())), preferred_element_type=WIDE)


def of_head(values, head):
    lane = lax.broadcasted_iota(jnp.int32, (1, values.shape[1]), 1)
    mine = (lane >= head * HEAD_DIM) & (lane < (head + 1) * HEAD_DIM)
    return jnp.where(mine, values, jnp.zeros_like(values))


def core_index():
    return lax.rem(lax.axis_index("tensor"), 2)


def shaped(*shape, kind=WIDE):
    return jax.ShapeDtypeStruct(shape, kind)


def cut(rows, width, count=4):
    return [shaped(rows // count, width)] * count


def near(values):
    return [swap(piece, "tensor", 1) for piece in values]


class Take:
    def __init__(self, array, shape=None, index=None):
        self.array = array
        self.shape = array.shape if shape is None else shape
        self.index = index


class Raw:
    def __init__(self, array, spec):
        self.array = array
        self.spec = spec


class Rows:
    def __init__(self, refs):
        self.refs = refs
        self.step = refs[0].shape[0]
        self.shape = (self.step * len(refs), refs[0].shape[1])

    def spans(self, key):
        first, last = 0, self.shape[0]
        if key is not Ellipsis and key[0] != slice(None):
            first, last = key[0].start, key[0].stop
        for place, ref in enumerate(self.refs):
            start, stop = max(first, place * self.step), min(last, (place + 1) * self.step)
            if start < stop:
                inside = slice(start - place * self.step, stop - place * self.step)
                yield ref, inside, slice(start - first, stop - first)

    def __getitem__(self, key):
        pieces = [ref[inside, :] for ref, inside, _ in self.spans(key)]
        return pieces[0] if len(pieces) == 1 else jnp.concatenate(pieces, axis=0)

    def __setitem__(self, key, value):
        for ref, inside, outside in self.spans(key):
            ref[inside, :] = value[outside]


class Line:
    def __init__(self):
        self.token = jnp.zeros((8, LANES), WIDE)

    def call(self, kernel, outs, args, scratch=(), megabytes=12, first=False):
        arrays, specs, buffers, layout, takes = [], [], [], [], []
        for arg in args:
            if isinstance(arg, Take):
                layout.append(0)
                takes.append((len(arrays), arg))
                arrays.append(arg.array)
                specs.append(HBM)
                buffers.append(pltpu.VMEM(arg.shape, arg.array.dtype))
            elif isinstance(arg, Raw):
                layout.append(0)
                arrays.append(arg.array)
                specs.append(arg.spec)
            elif isinstance(arg, (list, tuple)):
                layout.append(len(arg))
                arrays += arg
                specs += [VMEM] * len(arg)
            else:
                layout.append(0)
                arrays.append(arg)
                specs.append(VMEM)
        if takes:
            buffers.append(pltpu.SemaphoreType.DMA((len(takes),)))
        token = [] if first else [self.token]
        out_layout = [len(out) if isinstance(out, list) else 0 for out in outs]
        out_shapes = [o for out in outs for o in (out if isinstance(out, list) else [out])]

        def joined(refs, layout):
            refs = list(refs)
            return [
                Rows([refs.pop(0) for _ in range(count)]) if count else refs.pop(0)
                for count in layout
            ]

        def body(*refs):
            inputs = list(refs[: len(arrays)])
            rest = refs[len(arrays) + len(token) :]
            results, rest = rest[: len(out_shapes)], rest[len(out_shapes) + len(token) :]
            own, rest = rest[: len(scratch)], rest[len(scratch) :]
            copies = []
            for place, (i, take) in enumerate(takes):
                source = inputs[i]
                if take.index is not None:
                    source = source.at[take.index()]
                copies.append(pltpu.make_async_copy(source, rest[place], rest[-1].at[place]))
                inputs[i] = rest[place]
            for copy in copies:
                copy.start()
            for copy in copies:
                copy.wait()
            kernel(*joined(inputs, layout), *joined(results, out_layout), *own)

        results = pl.pallas_call(
            body,
            out_shape=(*out_shapes, *[shaped(8, LANES) for _ in token]),
            in_specs=[*specs, *[HBM for _ in token]],
            out_specs=tuple([VMEM] * len(out_shapes) + [HBM for _ in token]),
            scratch_shapes=[*scratch, *buffers],
            input_output_aliases={len(arrays): len(out_shapes)} if token else {},
            compiler_params=pltpu.CompilerParams(vmem_limit_bytes=megabytes * 1024 * 1024),
            cost_estimate=pl.CostEstimate(flops=0, bytes_accessed=0, transcendentals=0),
        )(*arrays, *token)
        found = list(results)
        if token:
            self.token = found.pop()
        return [
            [found.pop(0) for _ in range(count)] if count else found.pop(0) for count in out_layout
        ]


def sum_kernel(*refs):
    total = refs[0][...]
    for ref in refs[1:-1]:
        total = total + ref[...]
    refs[-1][...] = total


def pairs_kernel(*refs):
    terms = [ref[...] for ref in refs[:-1]]
    while len(terms) > 1:
        terms = [terms[i] + terms[i + 1] for i in range(0, len(terms), 2)]
    refs[-1][...] = terms[0]


def sum_rows(line, keep, arrived, count=1):
    mine, theirs = keep, arrived
    for bit in range(1, log2_of(lax.axis_size("tensor"))):
        mine = line.call(sum_kernel, [cut(*keep.shape, count)], [mine, theirs])[0]
        theirs = [swap(piece, "tensor", 1 << bit) for piece in mine]
    return mine, theirs


def sum_terms(values, axis, start, taken):
    return [values] + [swap(values, axis, distance << start) for distance in range(1, 1 << taken)]


def gathered(values, crossed):
    if crossed:
        first = jnp.where(outside(lax.axis_index("dp")), values[0], values[1])
        values = [first, *values[2:]]
    total = values[0]
    for value in values[1:]:
        total = total + value
    return total


def gather_kernel(*refs, crossed):
    refs[-1][...] = gathered([ref[...] for ref in refs[:-1]], crossed)


class Piece:
    def __init__(self, weight, window, route):
        self.weight, self.window, self.route = weight, window, route
        self.joined = route.joined
        self.terms, self.stage, self.crossed = [], 0, False

    def exchange(self, values):
        self.terms.append(lax.ppermute(values, "dp", self.route.steps[self.stage][1]))
        self.stage += 1

    def start(self):
        self.size = self.route.held // 2
        self.exchange(self.weight.products([self], True)[0])

    def sum_of(self, first, size):
        shape = (size,) + self.terms[0].shape[1:]
        index = lambda: (pl.ds(first, size),)
        return self.weight.line.call(
            functools.partial(gather_kernel, crossed=self.crossed),
            [shaped(*shape)],
            [Take(term, shape, index) for term in self.terms],
        )[0]

    def advance(self):
        if self.stage == len(self.route.steps):
            return
        if self.route.steps[self.stage][0] == CROSS:
            self.terms = [self.sum_of(0, self.size)]
            self.exchange(self.terms[0])
            self.crossed = True
        else:
            self.size //= 2
            self.exchange(self.sum_of(self.size, self.size))


class Weight:
    tables = {}

    def __init__(self, line, row, size, kernel, factors, mine, master, states):
        self.line, self.row, self.size, self.kernel = line, row, size, kernel
        self.factors, self.mine, self.master, self.states = factors, mine, master, states
        self.pieces = []

    def piece(self, first, last, count, route):
        found = Piece(self, (self.size * first // count, self.size * last // count), route)
        self.pieces.append(found)
        return found

    def products(self, pieces, send):
        line = self.line
        if any(piece.joined for piece in pieces):
            return owner_products(
                line, self.kernel, *self.factors(), pieces, line.own, send, CHUNKS
            )
        return owner_products(line, self.kernel, *self.mine(), pieces, line.own, send)

    def hold(self):
        for piece, keep in zip(self.pieces, self.products(self.pieces, False)):
            piece.terms.insert(0, keep)

    def stage(self):
        before = [self.master, *[Take(state) for state in self.states]]
        terms = [
            Take(term, term.shape[1:], lambda: (0,))
            for piece in self.pieces
            for term in piece.terms[:-1]
        ]
        crossed = [piece.crossed for piece in self.pieces]
        shapes = [shaped(*piece.terms[0].shape[1:]) for piece in self.pieces]
        counts = [len(piece.terms) - 1 for piece in self.pieces]
        self.master, *outs = self.line.call(
            functools.partial(stage_kernel, counts=counts, crossed=crossed),
            [shaped(*self.master.shape)] * 3 + shapes,
            before + terms,
        )
        self.states = outs[:2]
        self.partial = outs[2:]

    def moments(self):
        for piece in self.pieces:
            while piece.stage < len(piece.route.steps):
                piece.advance()
        everything = slice(None)
        if self.kernel is owned_rows_kernel:
            regions = [(everything, slice(*piece.window)) for piece in self.pieces]
        else:
            regions = [(slice(*piece.window),) for piece in self.pieces]
        late = not isinstance(self.master, Take)
        states, terms, counts, crossed = self.states, [], [], []
        if not late:
            states = [Take(state) for state in states]
        for index, piece in enumerate(self.pieces):
            found = [self.partial[index]] if late else []
            for term in piece.terms[-1:] if late else piece.terms:
                found.append(Take(term, term.shape[1:], lambda: (0,)))
            terms += found
            counts.append(len(found))
            crossed.append(piece.crossed and not late)
        shape = shaped(*self.master.shape)
        outs = self.line.call(
            functools.partial(
                moments_kernel,
                row=self.row,
                regions=regions,
                counts=counts,
                crossed=crossed,
                late=late,
            ),
            [shape, shape] + [shape] * (1 if late else 2) + [shaped(8, LANES)],
            [self.master, *states, self.line.table, *terms],
            megabytes=16,
        )
        self.kept, self.update, *self.found, self.line.table = outs
        if not late:
            self.first_new, self.second_new = self.found

    def finish(self):
        self.first_new, self.second_new = self.line.call(
            finish_kernel, [shaped(*self.master.shape)] * 2, [*self.found, *self.states]
        )


def project(normed, weights, cosine, sine):
    query = turn(dot(normed, weights[0]), cosine, sine).astype(LOW)
    keys = turn(dot(normed, weights[1]), cosine, sine).astype(LOW)
    return query, keys, dot(normed, weights[2]).astype(LOW)


def attend(query, keys, values, first_row, live_len):
    rows, reach = query.shape[0], keys.shape[0]
    row = first_row + lax.broadcasted_iota(jnp.int32, (rows, reach), 0)
    column = lax.broadcasted_iota(jnp.int32, (rows, reach), 1)
    visible = (column <= row) & (column < live_len)
    lane = lax.broadcasted_iota(jnp.int32, (1, LANES), 1)
    mixed = jnp.zeros((rows, query.shape[1]), WIDE)
    masses = jnp.zeros((rows, LANES), WIDE)
    for head in range(query.shape[1] // HEAD_DIM):
        scores = dot_wide(of_head(query, head), keys) * HEAD_DIM ** (-0.5)
        scores = jnp.where(visible, scores, mask_fill)
        top = jnp.max(scores, axis=-1, keepdims=True)
        expo = jnp.exp(scores - top)
        total = jnp.sum(expo, axis=-1, keepdims=True)
        probs = (expo * (1.0 / total)).astype(LOW)
        mixed = mixed + dot(probs, of_head(values, head))
        masses = jnp.where(lane == head, top + jnp.log(total), masses)
    live = first_row + lax.broadcasted_iota(jnp.int32, (rows, 1), 0) < live_len
    return jnp.where(live, mixed, 0.0).astype(LOW), masses


def split_rows(left_ref, right, send_ref, keep_ref, how):
    half = send_ref.shape[0]
    core = core_index()
    send_ref[...] = how(left_ref[pl.ds((1 - core) * half, half), :], right)
    keep_ref[...] = how(left_ref[pl.ds(core * half, half), :], right)


def first_kernel(
    live_ref, x_any, norm_any, cos_any, sin_any, qkv_any, out_any,
    normed_ref, q_ref, k_ref, v_ref, attn_ref, mass_ref, send_ref, keep_ref,
    x_ref, norm_ref, cos_ref, sin_ref, qkv_in, out_in, arrived,
):
    part = x_ref.shape[0]
    sources = [x_any.at[pl.ds(0, part)], norm_any, cos_any.at[pl.ds(0, part)], sin_any.at[pl.ds(0, part)]]
    targets = [x_ref, norm_ref, cos_ref, sin_ref]
    sources += [qkv_any.at[j] for j in range(3)] + [out_any]
    targets += [qkv_in.at[j] for j in range(3)] + [out_in]
    copies = [
        pltpu.make_async_copy(source, target, arrived.at[i])
        for i, (source, target) in enumerate(zip(sources, targets))
    ]
    for copy in copies:
        copy.start()
    copies[0].wait()
    copies[1].wait()
    stat, _ = normalize(x_ref[...].astype(WIDE))
    normed = (stat * norm_ref[0:1, :] + norm_ref[1:2, :]).astype(LOW)
    normed_ref[...] = normed
    copies[2].wait()
    copies[3].wait()
    weights = []
    for j in range(3):
        copies[4 + j].wait()
        weights.append(qkv_in[j].astype(LOW))
    query, keys, values = project(normed, weights, cos_ref[...], sin_ref[...])
    q_ref[...], k_ref[...], v_ref[...] = query, keys, values
    attn_ref[...], mass_ref[...] = attend(query, keys, values, 0, live_ref[0])
    copies[7].wait()
    split_rows(attn_ref, out_in[...].astype(LOW), send_ref, keep_ref, dot)


def next_kernel(
    live_ref, x_ref, norm_ref, cos_ref, sin_ref, qkv_ref, out_ref, *refs, first_row, part
):
    earlier = first_row // part
    rows = slice(first_row, first_row + part)
    k_before, v_before = refs[:earlier], refs[earlier : 2 * earlier]
    normed_ref, q_ref, k_ref, v_ref, attn_ref, mass_ref, send_ref, keep_ref = refs[
        2 * earlier : 2 * earlier + 8
    ]
    stat, _ = normalize(x_ref[rows, :].astype(WIDE))
    normed = (stat * norm_ref[0:1, :] + norm_ref[1:2, :]).astype(LOW)
    normed_ref[...] = normed
    weights = [qkv_ref[j].astype(LOW) for j in range(3)]
    out_low = out_ref[...].astype(LOW)
    for low_ref, low in zip(refs[2 * earlier + 8 :], (jnp.stack(weights), out_low)):
        low_ref[...] = low
    query, keys, values = project(normed, weights, cos_ref[rows, :], sin_ref[rows, :])
    q_ref[...], k_ref[...], v_ref[...] = query, keys, values
    keys = jnp.concatenate([ref[...] for ref in k_before] + [keys], axis=0)
    values = jnp.concatenate([ref[...] for ref in v_before] + [values], axis=0)
    attn_ref[...], mass_ref[...] = attend(query, keys, values, first_row, live_ref[0])
    split_rows(attn_ref, out_low, send_ref, keep_ref, dot)


def cast_kernel(wide_ref, low_ref):
    low_ref[...] = wide_ref[...].astype(LOW)


def middle_kernel(
    first_row, x_ref, norm_ref, mine_ref, theirs_ref, branch_ref, hidden_ref, *normed_refs
):
    half = mine_ref.shape[0]
    branch = mine_ref[...] + theirs_ref[...]
    branch_ref[...] = branch
    stat, _ = normalize(branch)
    inputs = x_ref[pl.ds(first_row + core_index() * half, half), :].astype(WIDE)
    hidden = inputs + stat * norm_ref[2:3, :] + norm_ref[3:4, :]
    hidden_ref[...] = hidden
    stat, _ = normalize(hidden)
    normed = stat * norm_ref[4:5, :] + norm_ref[5:6, :]
    for normed_ref in normed_refs:
        normed_ref[...] = normed


def mlp_kernel(own_ref, other_ref, up_w_ref, down_w_ref, normed_ref, up_ref, active_ref, send_ref, keep_ref):
    half = own_ref.shape[0]
    normed = jnp.concatenate([own_ref[...].astype(LOW), other_ref[...].astype(LOW)], axis=0)
    normed_ref[...] = normed
    step = min(256, up_w_ref.shape[1])
    total = None
    for start in range(0, up_w_ref.shape[1], step):
        block = slice(start, start + step)
        up = dot(normed, up_w_ref[:, block])
        up_ref[:, block] = up
        active = (up * gelu_mass(up)).astype(LOW)
        active_ref[:, block] = active
        product = dot(active, down_w_ref[block, :])
        total = product if total is None else total + product
    keep_ref[...] = total[:half]
    send_ref[...] = total[half:]


def again_kernel(own_ref, other_ref, up_w_ref, normed_ref, active_ref, slope_ref):
    normed = jnp.concatenate([own_ref[...].astype(LOW), other_ref[...].astype(LOW)], axis=0)
    normed_ref[...] = normed
    step = min(256, up_w_ref.shape[1])
    for start in range(0, up_w_ref.shape[1], step):
        block = slice(start, start + step)
        up = dot(normed, up_w_ref[:, block])
        mass = gelu_mass(up)
        active_ref[:, block] = (up * mass).astype(LOW)
        slope_ref[:, block] = gelu_slope(up, mass)


def back_again_kernel(own_ref, other_ref, slope_ref, down_w_ref, grad_mlp_ref, grad_up_ref):
    grad_mlp = jnp.concatenate([own_ref[...].astype(LOW), other_ref[...].astype(LOW)], axis=0)
    grad_mlp_ref[...] = grad_mlp
    step = min(256, slope_ref.shape[1])
    for start in range(0, slope_ref.shape[1], step):
        block = slice(start, start + step)
        grad_up = dot_wide(grad_mlp, down_w_ref[block, :]) * slope_ref[:, block]
        grad_up_ref[:, block] = grad_up.astype(LOW)


def loss_kernel(
    first_row, grad_ref, norm_ref, hidden_ref, mine_ref, theirs_ref, block_ref, sums_ref, *back_refs
):
    half = mine_ref.shape[0]
    stat, inverse = normalize(mine_ref[...] + theirs_ref[...])
    block_ref[...] = hidden_ref[...] + stat * norm_ref[6:7, :] + norm_ref[7:8, :]
    incoming = grad_ref[pl.ds(first_row + core_index() * half, half), :].astype(WIDE)
    back, gain, offset = norm_back(incoming, stat, inverse, norm_ref[6:7, :])
    for back_ref in back_refs:
        back_ref[...] = back
    sums_ref[0:1, :] = gain
    sums_ref[1:2, :] = offset


def mlp_back_kernel(
    own_ref, other_ref, up_ref, up_w_ref, down_w_ref, grad_mlp_ref, grad_up_ref, send_ref, keep_ref
):
    half = own_ref.shape[0]
    grad_mlp = jnp.concatenate([own_ref[...].astype(LOW), other_ref[...].astype(LOW)], axis=0)
    grad_mlp_ref[...] = grad_mlp
    step = min(256, up_w_ref.shape[1])
    total = None
    for start in range(0, up_w_ref.shape[1], step):
        block = slice(start, start + step)
        up = up_ref[:, block]
        slope = gelu_slope(up, gelu_mass(up))
        grad_up = (dot_wide(grad_mlp, down_w_ref[block, :]) * slope).astype(LOW)
        grad_up_ref[:, block] = grad_up
        product = dot_wide(grad_up, up_w_ref[:, block])
        total = product if total is None else total + product
    keep_ref[...] = total[:half]
    send_ref[...] = total[half:]


def norms_back_kernel(
    first_row, grad_ref, norm_ref, hidden_ref, branch_ref, mine_ref, theirs_ref,
    grad_hidden_ref, back_ref, sums_ref,
):
    half = mine_ref.shape[0]
    stat, inverse = normalize(hidden_ref[...])
    back, gain, offset = norm_back(
        mine_ref[...] + theirs_ref[...], stat, inverse, norm_ref[4:5, :]
    )
    incoming = grad_ref[pl.ds(first_row + core_index() * half, half), :].astype(WIDE)
    grad_hidden = incoming + back
    grad_hidden_ref[...] = grad_hidden
    sums_ref[2:3, :] = gain
    sums_ref[3:4, :] = offset
    stat, inverse = normalize(branch_ref[...])
    back, gain, offset = norm_back(grad_hidden, stat, inverse, norm_ref[2:3, :])
    back_ref[...] = back
    sums_ref[0:1, :] = gain
    sums_ref[1:2, :] = offset


def attention_back_kernel(live_ref, out_low_ref, cos_ref, sin_ref, *refs, chunks):
    groups = [refs[i * chunks : (i + 1) * chunks] for i in range(6)]
    own, other, query_refs, key_refs, value_refs, mass_refs = groups
    grad_branch_ref, rows_ref = refs[6 * chunks : 6 * chunks + 2]
    keys_sum, values_sum = refs[6 * chunks + 2 :]
    half = own[0].shape[0]
    part = 2 * half
    core = core_index()
    live_len = live_ref[0]
    local = rows_ref.shape[1] // 3
    heads = local // HEAD_DIM
    for c in range(chunks):
        grad_branch_ref[pl.ds(c * part + core * half, half), :] = own[c][...].astype(LOW)
        grad_branch_ref[pl.ds(c * part + (1 - core) * half, half), :] = other[c][...].astype(LOW)
    keys_all = jnp.concatenate([ref[...] for ref in key_refs], axis=0)
    values_all = jnp.concatenate([ref[...] for ref in value_refs], axis=0)
    for c in range(chunks):
        reach = (c + 1) * part
        first_row = c * part
        row = first_row + lax.broadcasted_iota(jnp.int32, (part, reach), 0)
        column = lax.broadcasted_iota(jnp.int32, (part, reach), 1)
        visible = (column <= row) & (column < live_len)
        live = first_row + lax.broadcasted_iota(jnp.int32, (part, 1), 0) < live_len
        grad_attn = dot_wide(grad_branch_ref[first_row : first_row + part, :], out_low_ref[...])
        grad_mixed = jnp.where(live, grad_attn, 0.0).astype(LOW)
        query, masses = query_refs[c][...], mass_refs[c][...]
        keys, values = keys_all[:reach], values_all[:reach]
        grad_query = jnp.zeros((part, local), WIDE)
        grad_keys = jnp.zeros((reach, local), WIDE)
        grad_values = jnp.zeros((reach, local), WIDE)
        for head in range(heads):
            query_h, grad_h = of_head(query, head), of_head(grad_mixed, head)
            scores = dot_wide(query_h, keys) * HEAD_DIM ** (-0.5)
            scores = jnp.where(visible, scores, mask_fill)
            probs = jnp.exp(scores - masses[:, head : head + 1])
            grad_values = grad_values + dot_rows(probs.astype(LOW), grad_h)
            grad_probs = dot_wide(grad_h, values)
            inner = jnp.sum(grad_probs * probs, axis=-1, keepdims=True)
            grad_scores = (probs * (grad_probs - inner)).astype(LOW)
            grad_query = grad_query + dot(grad_scores, of_head(keys, head))
            grad_keys = grad_keys + dot_rows(grad_scores, query_h)
        cosine = cos_ref[first_row : first_row + part, :]
        sine = sin_ref[first_row : first_row + part, :]
        grad_query = turn(grad_query * HEAD_DIM ** (-0.5), cosine, -sine)
        rows_ref[first_row : first_row + part, 0:local] = grad_query.astype(LOW)
        if c == 0:
            keys_sum[0:reach, :] = grad_keys
            values_sum[0:reach, :] = grad_values
        else:
            keys_sum[0:first_row, :] += grad_keys[:first_row]
            keys_sum[first_row:reach, :] = grad_keys[first_row:]
            values_sum[0:first_row, :] += grad_values[:first_row]
            values_sum[first_row:reach, :] = grad_values[first_row:]
    grad_keys = turn(keys_sum[...] * HEAD_DIM ** (-0.5), cos_ref[...], -sin_ref[...])
    rows_ref[:, local : 2 * local] = grad_keys.astype(LOW)
    rows_ref[:, 2 * local : 3 * local] = values_sum[...].astype(LOW)


def picked_columns(refs, chunks, own):
    blocks = []
    for chunk in chunks:
        start = pl.multiple_of(chunk * own, own)
        pieces = [ref[:, pl.ds(start, own)].astype(LOW) for ref in refs]
        blocks.append(pieces[0] if len(pieces) == 1 else jnp.concatenate(pieces, axis=0))
    return blocks[0] if len(blocks) == 1 else jnp.concatenate(blocks, axis=1)


def whole_rows(refs, window):
    pieces = [ref[:, window[0] : window[1]].astype(LOW) for ref in refs]
    return pieces[0] if len(pieces) == 1 else jnp.concatenate(pieces, axis=0)


def owned_columns_kernel(*refs, pairs, jobs, own):
    (lefts, rights), outs = pairs, refs[sum(pairs) :]
    left, right = refs[:lefts], refs[lefts : lefts + rights]
    for (order, window, blocks), out_ref in zip(jobs, outs):
        chunks = order(lax.axis_index("dp"))
        rows = whole_rows(left[:blocks], window)
        product = dot_rows(rows, picked_columns(right[:blocks], chunks, own))
        for place in range(len(chunks)):
            out_ref[place] = product[:, place * own : (place + 1) * own]


def owned_rows_kernel(*refs, pairs, jobs, own):
    (lefts, rights), outs = pairs, refs[sum(pairs) :]
    left, right = refs[:lefts], refs[lefts : lefts + rights]
    for (order, window, blocks), out_ref in zip(jobs, outs):
        chunks = order(lax.axis_index("dp"))
        product = dot_rows(
            picked_columns(left[:blocks], chunks, own), whole_rows(right[:blocks], window)
        )
        for place in range(len(chunks)):
            out_ref[place] = product[place * own : (place + 1) * own, :]


def owned_parts_kernel(*refs, pairs, jobs, own):
    (lefts, rights), outs = pairs, refs[sum(pairs) :]
    left, right = refs[:lefts], refs[lefts : lefts + rights]
    for (order, window, blocks), out_ref in zip(jobs, outs):
        chunks = order(lax.axis_index("dp"))
        local = out_ref.shape[3]
        columns = (window[0] * local, window[1] * local)
        product = dot_rows(picked_columns(left, chunks, own), whole_rows(right, columns))
        for place in range(len(chunks)):
            for j in range(window[1] - window[0]):
                out_ref[place, j] = product[
                    place * own : (place + 1) * own, j * local : (j + 1) * local
                ]


def rounded_kernel(*refs):
    refs[-1][...] = whole_rows(refs[:-1], (0, refs[0].shape[1]))


def narrow_products(line, kernel, left, right, jobs, outs, own):
    joined = []
    for arrays in (left, right):
        rows = sum(array.shape[0] for array in arrays)
        low = shaped(rows, arrays[0].shape[1], kind=LOW)
        joined.append(line.call(rounded_kernel, [low], arrays)[0])
    results = []
    for (order, window, _), out in zip(jobs, outs):
        chunks = order(lax.axis_index("dp"))
        pick = lambda array: jnp.concatenate(
            [lax.dynamic_slice_in_dim(array, chunk * own, own, 1) for chunk in chunks], axis=1
        )
        if kernel is owned_columns_kernel:
            product = dot_rows(joined[0][:, window[0] : window[1]], pick(joined[1]))
            product = product.reshape(-1, len(chunks), own).transpose(1, 0, 2)
        elif kernel is owned_rows_kernel:
            product = dot_rows(pick(joined[0]), joined[1][:, window[0] : window[1]])
            product = product.reshape(out.shape)
        else:
            local = out.shape[3]
            columns = joined[1][:, window[0] * local : window[1] * local]
            product = dot_rows(pick(joined[0]), columns)
            product = product.reshape(len(chunks), own, -1, local).transpose(0, 2, 1, 3)
        results.append(product)
    return results


def owner_products(line, kernel, left, right, pieces, own, send, blocks=None):
    jobs, outs = [], []
    for piece in pieces:
        half = piece.route.held // 2
        part = slice(half, None) if send else slice(half)
        order = lambda rank, route=piece.route, part=part: route.order(rank)[part]
        jobs.append((order, piece.window, None if piece.joined else blocks))
        size = piece.window[1] - piece.window[0]
        if kernel is owned_columns_kernel:
            outs.append(shaped(half, size, own))
        elif kernel is owned_rows_kernel:
            outs.append(shaped(half, own, size))
        else:
            outs.append(shaped(half, size, own, right[0].shape[1] // 3))
    if own % LANES:
        return narrow_products(line, kernel, left, right, jobs, outs, own)
    return line.call(
        functools.partial(kernel, pairs=(len(left), len(right)), jobs=jobs, own=own),
        outs,
        [*left, *right],
        megabytes=20,
    )


def input_back_kernel(rows_ref, qkv_low_ref, send_ref, keep_ref, *, chunks):
    half = send_ref.shape[0] // chunks
    local = qkv_low_ref.shape[2]
    core = core_index()
    for c in range(chunks):
        for target, which in ((send_ref, 1 - core), (keep_ref, core)):
            rows = rows_ref[pl.ds(c * 2 * half + which * half, half), :]
            total = None
            for j in range(3):
                product = dot_wide(rows[:, j * local : (j + 1) * local], qkv_low_ref[j])
                total = product if total is None else total + product
            target[c * half : (c + 1) * half, :] = total


def input_norm_kernel(x_ref, norm_ref, mine_ref, theirs_ref, *refs, chunks):
    grad_hidden = refs[:chunks]
    rows_ref, sums_ref = refs[chunks:]
    half = mine_ref.shape[0] // chunks
    core = core_index()
    gains = offsets = None
    for c in range(chunks):
        rows = slice(c * half, (c + 1) * half)
        inputs = x_ref[pl.ds(c * 2 * half + core * half, half), :].astype(WIDE)
        stat, inverse = normalize(inputs)
        back, gain, offset = norm_back(
            mine_ref[rows, :] + theirs_ref[rows, :], stat, inverse, norm_ref[0:1, :]
        )
        rows_ref[rows, :] = grad_hidden[c][...] + back
        gains = gain if gains is None else gains + gain
        offsets = offset if offsets is None else offsets + offset
    sums_ref[0:1, :] = gains
    sums_ref[1:2, :] = offsets


def place_kernel(mine_ref, theirs_ref, out_ref, *, chunks):
    half = mine_ref.shape[0] // chunks
    core = core_index()
    for c in range(chunks):
        rows = slice(c * half, (c + 1) * half)
        out_ref[pl.ds((2 * c + core) * half, half), :] = mine_ref[rows, :].astype(LOW)
        out_ref[pl.ds((2 * c + 1 - core) * half, half), :] = theirs_ref[rows, :].astype(LOW)


def rows_kernel(source_ref, target_ref):
    target_ref[...] = source_ref[...]


def norm_sums_kernel(*refs, chunks):
    input_ref, norms, losses, out_ref = refs[0], refs[1 : 1 + chunks], refs[1 + chunks : -1], refs[-1]
    out_ref[0:2, :] = input_ref[...]
    out_ref[2:6, :] = sum(ref[...] for ref in norms[1:]) + norms[0][...]
    out_ref[6:8, :] = sum(ref[...] for ref in losses[1:]) + losses[0][...]


def stage_kernel(*refs, counts, crossed):
    terms, outs = refs[3 : 3 + sum(counts)], refs[3 + sum(counts) :]
    for source, target in zip(refs[:3], outs[:3]):
        target[...] = source[...]
    at = 0
    for count, out_ref, cross in zip(counts, outs[3:], crossed):
        out_ref[...] = gathered([term[...] for term in terms[at : at + count]], cross)
        at += count


def finish_kernel(gradient_ref, first_ref, second_ref, first_new_ref, second_new_ref):
    first_new, second_new, _ = moment_step(gradient_ref[...], first_ref[...], second_ref[...])
    first_new_ref[...] = first_new
    second_new_ref[...] = second_new


def moment_step(gradient, first_state, second_state):
    first_new = first_decay * first_state + (1.0 - first_decay) * gradient
    second_new = second_decay * second_state + (1.0 - second_decay) * gradient * gradient
    direction = (
        first_new
        / (1.0 - first_decay**STEP)
        / (jnp.sqrt(second_new / (1.0 - second_decay**STEP)) + adam_epsilon)
    )
    return (first_new, second_new, direction)


def total_of(values):
    rows = values.reshape(-1, values.shape[-1])
    return jnp.sum(jnp.sum(rows, axis=0, keepdims=True), axis=1, keepdims=True)


def moments_kernel(
    master_ref, first_ref, second_ref, squares_ref, *refs, row, regions, counts, crossed, late
):
    table_ref = refs[-1]
    kept_ref, update_ref, *moment_refs = refs[sum(counts) : -1]
    at = 0
    sizes = []
    for region, count, cross in zip(regions, counts, crossed):
        gradient = gathered([term[...] for term in refs[at : at + count]], cross)
        at += count
        first_new, second_new, direction = moment_step(
            gradient, first_ref[region], second_ref[region]
        )
        for target, found in zip(moment_refs, [gradient] if late else [first_new, second_new]):
            target[region] = found
        master = master_ref[region]
        kept_ref[region] = master
        update = direction + decay_rate * master
        update_ref[region] = update
        sizes.append((total_of(master * master), total_of(update * update)))
    table_ref[...] = squares_ref[...]
    for place, size in ((row, 0), (row + 4, 1)):
        amount = sizes[0][size]
        for other in sizes[1:]:
            amount = amount + other[size]
        table_ref[place : place + 1, :] = jnp.broadcast_to(amount, (1, LANES))


def join_kernel(*refs):
    terms, norms_ref, out_ref = refs[:-2], refs[-2], refs[-1]
    terms = [ref[...] for ref in terms]
    while len(terms) > 1:
        terms = [terms[i] + terms[i + 1] for i in range(0, len(terms), 2)]
    out_ref[:, 0:LANES] = terms[0]
    out_ref[:, LANES:] = norms_ref[...]


def masters_kernel(norm_ref, first_ref, second_ref, *refs, terms, own):
    sums, refs = refs[:terms], refs[terms:]
    masters, updates, outs = refs[:4], refs[4:8], refs[8:12]
    norms_ref, norm_new_ref, first_new_ref, second_new_ref = refs[12:]
    total = sums[0][:, 0:LANES]
    for ref in sums[1:]:
        total = total + ref[:, 0:LANES]
    sizes = jnp.sqrt(total[0:4, :])
    steps = jnp.sqrt(total[4:8, :] + trust_epsilon)
    lane = lax.broadcasted_iota(jnp.int32, (1, 4), 1)
    for place, found in ((0, sizes), (1, steps)):
        row = jnp.zeros((1, 4), WIDE)
        for index in range(4):
            row = jnp.where(lane == index, found[index : index + 1, 0:1], row)
        norms_ref[place : place + 1, :] = row
    ratio = learn_rate * (sizes / steps)
    for index in range(4):
        scale = ratio[index : index + 1, 0:1]
        if len(masters[index].shape) == 3:
            scale = scale.reshape(1, 1, 1)
        outs[index][...] = masters[index][...] - scale * updates[index][...]
    if own % LANES:
        gradient = sums[0][:, LANES:]
        for ref in sums[1:]:
            gradient = gradient + ref[:, LANES:]
        norm_new_ref[...] = gradient
        return
    start = pl.multiple_of(lax.axis_index("dp") * own, own)
    gradient = sums[0][:, pl.ds(LANES + start, own)]
    for ref in sums[1:]:
        gradient = gradient + ref[:, pl.ds(LANES + start, own)]
    first_new, second_new, direction = moment_step(gradient, first_ref[...], second_ref[...])
    first_new_ref[...] = first_new
    second_new_ref[...] = second_new
    norm_new_ref[...] = norm_ref[:, pl.ds(start, own)] - learn_rate * direction


def shards(
    block_input,
    lengths,
    norm_params,
    qkv_weight,
    out_weight,
    up_weight,
    down_weight,
    qkv_first,
    qkv_second,
    out_first,
    out_second,
    up_first,
    up_second,
    down_first,
    down_second,
    norm_first,
    norm_second,
    out_grad,
):
    row_count, width = block_input.shape
    local = qkv_weight.shape[2]
    hidden_units = up_weight.shape[1]
    group_count = lax.axis_size("dp")
    own = width // group_count
    own_start = lax.axis_index("dp") * own
    part = row_count // CHUNKS
    half = part // 2
    chunks = range(CHUNKS)
    bits = list(range(log2_of(group_count)))

    line = Line()
    qkv_parts = jnp.transpose(qkv_weight, (1, 0, 2))
    cosine, sine = rotary_tables(row_count)
    live = Raw(lengths, SMEM)
    joined = group_count == 8 and own % LANES == 0

    def relay_of(theirs):
        copied = line.call(rows_kernel, [cut(half, width, CUT_RELAY)], [theirs])[0]
        return theirs, near(copied)

    weight_shapes = [shaped(3, width, local, kind=LOW), shaped(local, width, kind=LOW)]
    chunk_shapes = [
        shaped(part, width, kind=LOW),
        shaped(part, local, kind=LOW),
        shaped(part, local, kind=LOW),
        shaped(part, local, kind=LOW),
        shaped(part, local, kind=LOW),
        shaped(part, LANES),
        cut(half, width, CUT_ATTENTION),
        shaped(half, width),
    ]
    low_weights, parts, branch_terms = [], [], []

    def attention(c):
        if c == 0:
            outs = line.call(
                first_kernel,
                chunk_shapes,
                [live]
                + [
                    Raw(a, HBM)
                    for a in (block_input, norm_params, cosine, sine, qkv_parts, out_weight)
                ],
                scratch=[
                    pltpu.VMEM((part, width), LOW),
                    pltpu.VMEM(norm_params.shape, WIDE),
                    pltpu.VMEM((part, LANES), WIDE),
                    pltpu.VMEM((part, LANES), WIDE),
                    pltpu.VMEM((3, width, local), WIDE),
                    pltpu.VMEM((local, width), WIDE),
                    pltpu.SemaphoreType.DMA((8,)),
                ],
                megabytes=62,
                first=True,
            )
            keep = Take(outs[7])
        else:
            before = [p[2] for p in parts] + [p[3] for p in parts]
            outs = line.call(
                functools.partial(next_kernel, first_row=c * part, part=part),
                chunk_shapes + weight_shapes * (c == 1),
                [live, block_input, norm_params, cosine, sine]
                + (low_weights or [qkv_parts, out_weight])
                + before,
            )
            keep = outs[7]
            low_weights.extend(outs[8:])
        parts.append(outs)
        branch_terms.append((keep, near(outs[6])))

    def sum_branch(c):
        branch_terms[c] = sum_rows(line, *branch_terms[c])

    def cast(weight):
        return line.call(cast_kernel, [shaped(*weight.shape, kind=LOW)], [Take(weight)])[0]

    branch, hidden, normed_mid, up, active, mlp_terms = [], [], [], [], [], []
    normed_other, ships, normed_theirs, active_theirs, slope_theirs = [], [], [], [], []

    def middle(c):
        outs = line.call(
            functools.partial(middle_kernel, c * part),
            [shaped(half, width), shaped(half, width), cut(half, width, CUT_MIDDLE)]
            + [shaped(half, width)] * joined,
            [block_input, norm_params, *branch_terms[c]],
        )
        branch.append(outs[0])
        hidden.append(outs[1])
        normed_other.append((outs[2], near(outs[2])))
        ships.append(swap(outs[3], "dp", 2) if joined else None)

    def relay(c):
        if joined:
            ships[c] = relay_of(ships[c])

    def mlp(c):
        outs = line.call(
            mlp_kernel,
            [
                shaped(part, width, kind=LOW),
                shaped(part, hidden_units),
                shaped(part, hidden_units, kind=LOW),
                cut(half, width, CUT_MLP),
                shaped(half, width),
            ],
            [*normed_other[c], up_low, down_low],
        )
        normed_mid.append(outs[0])
        up.append(outs[1])
        active.append(outs[2])
        mlp_terms.append((outs[4], near(outs[3])))

    def sum_mlp(c):
        mlp_terms[c] = sum_rows(line, *mlp_terms[c])

    def again(c):
        if joined:
            outs = line.call(
                again_kernel,
                [
                    shaped(part, width, kind=LOW),
                    shaped(part, hidden_units, kind=LOW),
                    shaped(part, hidden_units),
                ],
                [*ships[c], up_low],
            )
            normed_theirs.append(outs[0])
            active_theirs.append(outs[1])
            slope_theirs.append(outs[2])

    line.own, line.table = own, jnp.zeros((8, LANES), WIDE)
    route_a, route_b, route_j = routes(group_count)
    columns = lambda: (slice(None), pl.ds(pl.multiple_of(lax.axis_index("dp") * own, own), own))
    rows = lambda: (pl.ds(pl.multiple_of(lax.axis_index("dp") * own, own), own),)
    part_rows = lambda: (slice(None), *rows())
    mine = lambda array, axis: lax.dynamic_slice_in_dim(array, own_start, own, axis)
    block_rows, loss_sums, grad_final, grad_up_rows, mid_terms = [], [], [], [], []
    grad_mlp, grad_mlp_theirs, grad_up_theirs, ships_back = [], [], [], []
    grad_hidden, norms_sums, own_back, other_back = [], [], [], []
    flip = lambda array: jnp.transpose(array, (1, 0, 2))
    qkv = Weight(
        line,
        0,
        3,
        owned_parts_kernel,
        lambda: ([p[0] for p in parts], [grad_rows]),
        lambda: ([p[0] for p in parts], [grad_rows]),
        Take(qkv_parts, (3, own, local), part_rows),
        [flip(qkv_first), flip(qkv_second)],
    )
    out = Weight(
        line,
        1,
        local,
        owned_columns_kernel,
        lambda: ([p[4] for p in parts], [grad_branch]),
        lambda: ([p[4] for p in parts], [grad_branch]),
        Take(mine(out_weight, 1)) if own % LANES else Take(out_weight, (local, own), columns),
        [out_first, out_second],
    )
    up_matrix = Weight(
        line,
        2,
        hidden_units,
        owned_rows_kernel,
        lambda: (normed_mid + normed_theirs, grad_up_rows + grad_up_theirs),
        lambda: (normed_mid, grad_up_rows),
        Take(up_weight, (own, hidden_units), rows),
        [up_first, up_second],
    )
    down = Weight(
        line,
        3,
        hidden_units,
        owned_columns_kernel,
        lambda: (active + active_theirs, grad_mlp + grad_mlp_theirs),
        lambda: (active, [block for pair in grad_final for rows in pair for block in rows]),
        Take(mine(down_weight, 1))
        if own % LANES
        else Take(down_weight, (hidden_units, own), columns),
        [down_first, down_second],
    )
    d0 = down.piece(0, 8, 8, route_j)
    u0 = up_matrix.piece(0, 8, 8, route_j)
    q0 = qkv.piece(0, 2, 3, route_b)
    q1 = qkv.piece(2, 3, 3, route_b)
    o0 = out.piece(0, 1, 1, route_b)


    def loss(c):
        outs = line.call(
            functools.partial(loss_kernel, c * part),
            [shaped(half, width), shaped(2, width), cut(half, width, CUT_LOSS)]
            + [shaped(half, width)] * joined,
            [out_grad, norm_params, hidden[c], *mlp_terms[c]],
        )
        block_rows.append(outs[0])
        loss_sums.append(outs[1])
        grad_final.append((outs[2], near(outs[2])))
        ships_back.append(swap(outs[3], "dp", 2) if joined else None)

    def back_relay(c):
        if joined:
            ships_back[c] = relay_of(ships_back[c])

    def mlp_back(c):
        outs = line.call(
            mlp_back_kernel,
            [
                shaped(part, width, kind=LOW),
                shaped(part, hidden_units, kind=LOW),
                cut(half, width, CUT_MLP if c < CHUNKS - 1 else CUT_MID),
                shaped(half, width),
            ],
            [*grad_final[c], up[c], up_low, down_low],
        )
        grad_mlp.append(outs[0])
        grad_up_rows.append(outs[1])
        mid_terms.append((outs[3], near(outs[2])))

    def back_again(c):
        if joined:
            outs = line.call(
                back_again_kernel,
                [shaped(part, width, kind=LOW), shaped(part, hidden_units, kind=LOW)],
                [*ships_back[c], slope_theirs[c], down_low],
            )
            grad_mlp_theirs.append(outs[0])
            grad_up_theirs.append(outs[1])

    def sum_mid(c):
        mid_terms[c] = sum_rows(line, *mid_terms[c])

    def norms(c):
        outs = line.call(
            functools.partial(norms_back_kernel, c * part),
            [shaped(half, width), cut(half, width, CUT_NORMS), shaped(4, width)],
            [out_grad, norm_params, hidden[c], branch[c], *mid_terms[c]],
        )
        grad_hidden.append(outs[0])
        norms_sums.append(outs[2])
        own_back.append(outs[1])
        other_back.append(near(outs[1]))

    def attention_back():
        return line.call(
            functools.partial(attention_back_kernel, chunks=CHUNKS),
            [shaped(row_count, width, kind=LOW), shaped(row_count, 3 * local, kind=LOW)],
            [live, low_weights[1], cosine, sine, *own_back, *other_back]
            + [p[which] for which in (1, 2, 3, 5) for p in parts],
            scratch=[pltpu.VMEM((row_count, local), WIDE), pltpu.VMEM((row_count, local), WIDE)],
        )

    def input_back():
        return line.call(
            functools.partial(input_back_kernel, chunks=CHUNKS),
            [cut(row_count // 2, width, CUT_BACK), shaped(row_count // 2, width)],
            [grad_rows, low_weights[0]],
        )

    def input_norm():
        return line.call(
            functools.partial(input_norm_kernel, chunks=CHUNKS),
            [cut(row_count // 2, width, CUT_INPUT), shaped(2, width)],
            [block_input, norm_params, *in_terms, *grad_hidden],
        )

    def send_output():
        return line.call(
            rows_kernel, [cut(row_count // 2, width, CUT_OUTPUT)], [block_rows]
        )[0]

    def place(blocks, others):
        return line.call(
            functools.partial(place_kernel, chunks=CHUNKS),
            [shaped(row_count, width, kind=LOW)],
            [blocks, others],
        )[0]

    def norm_sums():
        return line.call(
            functools.partial(norm_sums_kernel, chunks=CHUNKS),
            [shaped(8, width)],
            [input_sums, *norms_sums, *loss_sums],
        )[0]

    def sum_norms():
        return line.call(
            sum_kernel, [shaped(8, width)], [grad_norms, norms_other]
        )[0]

    attention(0)
    sum_branch(0)
    attention(1)
    sum_branch(1)
    up_low = cast(up_weight)
    down_low = cast(down_weight)
    middle(0)
    mlp(0)
    sum_mlp(0)
    middle(1)
    mlp(1)
    relay(0)
    sum_mlp(1)
    loss(0)
    mlp_back(0)
    again(0)
    relay(1)
    sum_mid(0)
    loss(1)
    back_relay(0)
    again(1)
    mlp_back(1)
    norms(0)
    sum_mid(1)
    back_again(0)
    back_relay(1)
    back_again(1)
    d0.start()
    down.hold()
    u0.start()
    norms(1)
    grad_branch, grad_rows = attention_back()
    send, keep = input_back()
    crossing = near(send)
    q0.start()
    in_terms = sum_rows(line, keep, crossing)
    qkv.hold()
    sent_rows = send_output()
    block_other = near(sent_rows)
    o0.start()
    d0.advance()
    q1.start()
    block_output = place(sent_rows, block_other)
    up_matrix.hold()
    q0.advance()
    u0.advance()
    d0.advance()
    q1.advance()
    out.hold()
    input_rows, input_sums = input_norm()
    input_other = near(input_rows)
    q0.advance()
    o0.advance()
    input_grad = place(input_rows, input_other)
    u0.advance()
    o0.advance()
    down.moments()
    q1.advance()
    q0.advance()
    o0.advance()
    q1.advance()
    up_matrix.moments()
    out.moments()
    grad_norms = norm_sums()
    norms_other = swap(grad_norms, "tensor", 1)
    grad_norms = sum_norms()
    qkv.stage()
    qkv.moments()

    tensor_bits = log2_of(lax.axis_size("tensor"))
    found = line.table
    for start in range(0, tensor_bits, 2):
        terms = sum_terms(found, "tensor", start, min(2, tensor_bits - start))
        if start == 0:
            qkv.finish()
        if start + 2 >= tensor_bits:
            found = line.call(join_kernel, [shaped(8, LANES + width)], [*terms, grad_norms])[0]
        else:
            found = line.call(pairs_kernel, [shaped(8, LANES)], terms)[0]
    for start in range(0, len(bits), 2):
        terms = sum_terms(found, "dp", start, min(2, len(bits) - start))
        if start + 2 < len(bits) or len(terms) > 2:
            found = line.call(pairs_kernel, [shaped(8, LANES + width)], terms)[0]
            terms = [found]
    weights = (qkv, out, up_matrix, down)
    outs = line.call(
        functools.partial(masters_kernel, terms=len(terms), own=own),
        [shaped(*weight.kept.shape) for weight in weights]
        + [shaped(2, 4), shaped(8, width if own % LANES else own), shaped(8, own), shaped(8, own)],
        [
            norm_params,
            norm_first,
            norm_second,
            *terms,
            *[weight.kept for weight in weights],
            *[weight.update for weight in weights],
        ],
    )
    matrix_norms, norm_new, norm_first_new, norm_second_new = outs[4:]
    if own % LANES:
        norm_first_new, norm_second_new, direction = moment_step(
            mine(norm_new, 1), norm_first, norm_second
        )
        norm_new = mine(norm_params, 1) - learn_rate * direction
    return (
        block_output,
        input_grad,
        flip(outs[0]),
        flip(qkv.first_new),
        flip(qkv.second_new),
        outs[1],
        out.first_new,
        out.second_new,
        outs[2],
        up_matrix.first_new,
        up_matrix.second_new,
        outs[3],
        down.first_new,
        down.second_new,
        norm_new,
        norm_first_new,
        norm_second_new,
        matrix_norms,
    )


def solution(mesh):
    in_specs = (
        P("dp", None),
        P("dp"),
        P(),
        P(None, None, "tensor"),
        P("tensor", None),
        P(None, "tensor"),
        P("tensor", None),
        P("dp", None, "tensor"),
        P("dp", None, "tensor"),
        P("tensor", "dp"),
        P("tensor", "dp"),
        P("dp", "tensor"),
        P("dp", "tensor"),
        P("tensor", "dp"),
        P("tensor", "dp"),
        P(None, "dp"),
        P(None, "dp"),
        P("dp", None),
    )
    out_specs = (
        P("dp", None),
        P("dp", None),
        P("dp", None, "tensor"),
        P("dp", None, "tensor"),
        P("dp", None, "tensor"),
        P("tensor", "dp"),
        P("tensor", "dp"),
        P("tensor", "dp"),
        P("dp", "tensor"),
        P("dp", "tensor"),
        P("dp", "tensor"),
        P("tensor", "dp"),
        P("tensor", "dp"),
        P("tensor", "dp"),
        P(None, "dp"),
        P(None, "dp"),
        P(None, "dp"),
        P(),
    )
    return jax.shard_map(shards, mesh=mesh, in_specs=in_specs, out_specs=out_specs, check_vma=False)
```
